32 devices in a mesh: body: 2 (over core), sub: 16 (over z, y, x).
Axes of the slice: x: 2, y: 2, z: 4, core: 2. Of those that a mesh axis runs over, the one named last changes fastest.
Arguments:
- rhs: float32 [8, 1024, 256], P(None, 'sub'), may hold values from -50 to 50
- compliance: float32 [1024, 256], P('sub'), may hold values from 0.5 to 2
- plate_owner: int32 [1024, 1], P('sub'), may hold values from 0 to 15; in each aligned block of 64 rows (0 to 63, 64 to 127, ...) at most 8 rows name the same one
- found_owner: int32 [1024, 1], P('sub'), may hold values from 0 to 15; in each aligned block of 64 rows (0 to 63, 64 to 127, ...) at most 8 rows name the same one
- slot_pairs: int32 [1024, 2], P('sub'), may hold values from 0 to 7
- active: int32 [1024], P('sub'), may hold values 0 or 1
- inverse: bfloat16 [2, 16, 2048, 2048], P('body', 'sub'), may hold values from -0.06 to 4, as said below
Outputs:
- multipliers: float32 [8, 1024, 256], P(None, 'sub')
The draws below stay inside these ranges and needn't reach their ends.
Inputs may be any that keep to these rules, and one draw needn't show every extreme that they name: `plate_owner`: at most 8 patches among the list of one index of sub name the same plate substructure; some list names one exactly 8 times. `found_owner`: at most 8 patches among the list of one index of sub name the same foundation substructure; some list names one exactly 8 times. Each block inverse[b, t] is symmetric positive definite.
All inputs are finite; a program needn't handle non-finite values. No bound on the sum of `active` on one device may be relied on, other than what follows from the above.
Results may differ from the reference program's by a relative error of at most 0.0055.
Values sent between devices are 32-bit elements; how exact they have to be, the bound alone decides.
No kernel may reach another device: no remote copies, remote signals or barrier semaphores. Data moves between devices by JAX's collectives and lax.ppermute only.
A program may use at most 64 MiB of HBM per device.

```python
import math
import jax
import jax.numpy as jnp
import numpy as np
from jax import lax

GAP = 256
SLOTS = 8
CASES = 8
ITERS = 4
PATCH_DEV = 64
PATCHES = 1024
CAP = 8
IFACE = 2048
N_SUB = 16


def draw_inverse(key, part):
    keys = jax.random.split(key, 2 * N_SUB)
    index = jnp.arange(IFACE, dtype=jnp.int32)
    reach = 0.06 / (1.0 + jnp.abs(index[:, None] - index[None, :]).astype(jnp.float32))
    diagonal_mask = index[:, None] == index[None, :]

    def one_block(block_key):
        first, second = jax.random.split(block_key)
        rough = 0.3 + 0.7 * jax.random.uniform(first, (IFACE, IFACE), jnp.float32, -1.0, 1.0)
        middle = jnp.exp(jax.random.uniform(second, (IFACE,), jnp.float32, 0.0, math.log(2.0)))
        symmetric = 0.5 * (rough + rough.T) * reach
        return jnp.where(diagonal_mask, middle[None, :], symmetric).astype(jnp.bfloat16)
    return lax.map(one_block, keys).reshape(2, N_SUB, IFACE, IFACE)


def draw_rhs(key, part):
    first, second = jax.random.split(key, 2)
    rising = jnp.exp(math.log(10.0) * jnp.arange(PATCHES).astype(jnp.float32) / max(PATCHES - 1, 1))
    case_scale = jnp.exp(math.log(10.0) * jax.random.uniform(second, (CASES,), jnp.float32))
    base = jnp.clip(jax.random.normal(first, (CASES, PATCHES, GAP), jnp.float32), -5.0, 5.0)
    return base * rising[None, :, None] * case_scale[:, None, None] / 10.0


def set_ends(values, rng, low, largest):
    shape = values.shape
    place = [jax.random.randint(jax.random.fold_in(rng, axis), (), 0, shape[axis]) for axis in range(len(shape))]
    values = values.at[tuple(place)].set(low)
    longest = shape.index(max(shape))
    place[longest] = (place[longest] + 1) % shape[longest]
    return values.at[tuple(place)].set(largest)


def block_levels(own_key, shape, cuts, smallest, largest):
    factor_of, own = 1.0, jax.random.fold_in(own_key, 6)
    for axis_at, shards_of in cuts:
        draws = jnp.exp(jax.random.uniform(jax.random.fold_in(own, axis_at), (shards_of,), jnp.float32, smallest / len(cuts), largest / len(cuts)))
        factor_of = factor_of * jnp.repeat(draws, shape[axis_at] // shards_of).reshape([-1 if axis == axis_at else 1 for axis in range(len(shape))])
    return factor_of


def routed_block(key, own, number, rows, number_of, top, most, lean):
    sequence = jax.random.permutation(key, number_of)
    heavy_load, common = load_shares(number_of, rows * top, most, lean, True), load_shares(number_of, rows * top, most, lean, False)
    places = jnp.arange(number_of)

    def named(sizes, turn):
        used = int((sizes > 0).sum())
        fixed = max(1, used // 4)
        shifted = fixed + (places - fixed + turn * (used - fixed)) % max(1, number_of - fixed)
        return jnp.zeros((number_of,), jnp.int32).at[sequence[jnp.where(places < fixed, places, shifted)]].set(jnp.asarray(sizes, jnp.int32))

    sizes = jnp.where(number % 4 == 0, named(heavy_load, number // 4), named(common, number - number // 4 - 1))
    mixed = jax.random.permutation(jax.random.fold_in(own, 3), number_of)
    donor, taker = mixed[0:number_of // 2 * 2:2], mixed[1:number_of // 2 * 2:2]
    slack = jnp.minimum(sizes[donor] - 1, most - sizes[taker]) // 2
    slack = jnp.where((donor == sequence[0]) | (taker == sequence[0]) | (sizes[taker] == 0), 0, jnp.maximum(slack, 0))
    shifted = jax.random.randint(jax.random.fold_in(own, 4), (number_of // 2,), 0, 1 << 20) % (slack + 1)
    sizes = sizes.at[donor].add(-shifted).at[taker].add(shifted)
    members = jnp.searchsorted(jnp.cumsum(sizes), jnp.arange(rows * top), side="right").astype(jnp.int32)
    listing = members.reshape(top, rows).T
    listing = listing[jax.random.permutation(jax.random.fold_in(own, 1), rows)]
    turn = jax.random.randint(jax.random.fold_in(own, 2), (rows, 1), 0, top)
    return jnp.take_along_axis(listing, (jnp.arange(top)[None, :] + turn) % top, axis=1)


def load_shares(amount, total, limit, lean, full):
    loads = [(1 << 20) // math.isqrt(grade ** lean) + 1 for grade in range(1, amount + 1)]
    largest = limit if full else min(limit, max(-(-total // amount), total * loads[0] // sum(loads)))
    least = 1 if total - largest >= amount - 1 else 0
    holding, surplus = [largest] + [least] * (amount - 1), total - largest - least * (amount - 1)
    while surplus > 0:
        candidates = [i for i in range(1, amount) if holding[i] < largest] or [i for i in range(1, amount) if holding[i] < limit]
        whole, left = sum([loads[i] for i in candidates]), surplus
        for i in candidates:
            addition = min(limit - holding[i], max(1, left * loads[i] // whole), surplus)
            holding[i] = holding[i] + addition
            surplus = surplus - addition
    return np.array(holding)


def setup_inputs(seed: int = 0) -> dict:
    key_list = jax.random.split(jax.random.key(seed), 8)
    rhs = draw_rhs(jax.random.fold_in(key_list[7], 71), 0)
    compliance = jnp.clip(jnp.exp(math.log(2.0) - 1.3862944 * jax.random.uniform(key_list[1], (PATCHES, GAP), jnp.float32) ** block_levels(key_list[1], (PATCHES, GAP), ((0, 16),), -0.2, 0.2)), 0.5, 2.0)
    plate_owner_keys = jax.random.split(jax.random.fold_in(key_list[2], 1), PATCHES // PATCH_DEV)
    plate_owner_turns = jax.random.permutation(jax.random.fold_in(key_list[2], 3), PATCHES // PATCH_DEV)
    plate_owner = jax.vmap(lambda own, number: routed_block(jax.random.fold_in(key_list[2], 2), own, number, PATCH_DEV, N_SUB, 1, CAP, 2))(plate_owner_keys, plate_owner_turns).reshape((PATCHES, 1))
    found_owner_keys = jax.random.split(jax.random.fold_in(key_list[3], 1), PATCHES // PATCH_DEV)
    found_owner_turns = jax.random.permutation(jax.random.fold_in(key_list[3], 3), PATCHES // PATCH_DEV)
    found_owner = jax.vmap(lambda own, number: routed_block(jax.random.fold_in(key_list[3], 2), own, number, PATCH_DEV, N_SUB, 1, CAP, 3))(found_owner_keys, found_owner_turns).reshape((PATCHES, 1))
    slot_pairs = set_ends(jax.random.randint(key_list[4], (PATCHES, 2), 0, SLOTS), jax.random.fold_in(key_list[4], 1), 0, SLOTS - 1).astype(jnp.int32)
    active = set_ends((jax.random.randint(key_list[5], (PATCHES,), 0, 4) < 3).astype(jnp.int32), jax.random.fold_in(key_list[5], 1), 0, 1)
    inverse = draw_inverse(jax.random.fold_in(key_list[7], 71), 0)
    return dict(rhs=rhs, compliance=compliance, plate_owner=plate_owner, found_owner=found_owner, slot_pairs=slot_pairs, active=active, inverse=inverse)


def interface_response(field, owner, slot, block_list):
    rows = jnp.transpose(field, (1, 0, 2))
    target = (owner * SLOTS + slot).astype(jnp.int32)
    summed = jax.ops.segment_sum(rows, target, num_segments=N_SUB * SLOTS)
    summed = summed.reshape(N_SUB, SLOTS, CASES, GAP).transpose(0, 2, 1, 3).reshape(N_SUB, CASES, SLOTS * GAP)
    load_vectors = summed.astype(jnp.bfloat16)

    def apply_block(pair):
        return jnp.dot(pair[0], pair[1], preferred_element_type=jnp.float32)

    response = lax.map(apply_block, (load_vectors, block_list))
    response = response.reshape(N_SUB, CASES, SLOTS, GAP)
    picked = response[owner, :, slot, :]
    return jnp.transpose(picked, (1, 0, 2))


def reference(rhs, compliance, plate_owner, found_owner, slot_pairs, active, inverse):
    keep = active.astype(jnp.float32)[None, :, None]
    owners = (plate_owner[:, 0], found_owner[:, 0])

    def operate(field):
        total = jnp.zeros_like(field)
        for side in range(2):
            total = total + interface_response(field, owners[side], slot_pairs[:, side], inverse[side])
        return keep * (total + compliance[None] * field)

    def products(left, right):
        return jnp.sum(left * right, axis=(1, 2))

    residual = keep * rhs
    solution = jnp.zeros_like(rhs)
    direction = residual
    norm_now = products(residual, residual)
    for step in range(ITERS):
        image = operate(direction)
        alpha = norm_now / products(direction, image)
        solution = solution + alpha[:, None, None] * direction
        residual = residual - alpha[:, None, None] * image
        norm_next = products(residual, residual)
        direction = residual + (norm_next / norm_now)[:, None, None] * direction
        norm_now = norm_next
    return solution
```

```python
import functools

import jax
import jax.numpy as jnp
from jax import lax
from jax.experimental import pallas as pl
from jax.experimental.pallas import tpu as pltpu
from jax.sharding import PartitionSpec as P

ITERS = 4
AXES = ("body", "sub")
VMEM = pl.BlockSpec(memory_space=pltpu.VMEM)
SMEM = pl.BlockSpec(memory_space=pltpu.SMEM)
ANY = pl.BlockSpec(memory_space=pl.ANY)
PARAMS = pltpu.CompilerParams(vmem_limit_bytes=40 * 1024 * 1024)


def f32(*shape):
    return jax.ShapeDtypeStruct(shape, jnp.float32)


def lanes(parts):
    lane = lax.broadcasted_iota(jnp.int32, parts[0].shape, 1)
    tile = jnp.zeros_like(parts[0])
    for i, part in enumerate(parts):
        tile = jnp.where(lane == i, jnp.sum(part, axis=1, keepdims=True), tile)
    return tile


def load_kernel(ndest, per, unroll, place, field, send):
    npatch, ncase, width = field.shape
    send[...] = jnp.zeros_like(send)

    def body(p, carry):
        value = field[p]
        send[place[0, p]] += value
        send[place[1, p]] += value
        return carry

    lax.fori_loop(0, npatch, body, 0, unroll=unroll)


def patch_kernel(
    first, ndest, per, unroll, place, keep, coef, resp, comp, r, d, x, q, r_out, d_out, x_out, q_out, send
):
    npatch, ncase, width = d.shape
    send[...] = jnp.zeros_like(send)
    alpha, beta = coef[0], coef[1]
    zero = jnp.zeros((ncase, width), jnp.float32)

    def body(p, sums):
        rp, dp = r[p], d[p]
        if first:
            x_out[p] = zero
        else:
            x_out[p] = x[p] + alpha * dp
            rp = rp - alpha * q[p]
            dp = rp + beta * dp
        r_out[p] = rp
        d_out[p] = dp
        image = resp[place[2, p]] + resp[place[3, p]] + comp[pl.ds(p, 1), :] * dp
        image = keep[p] * image
        q_out[p] = image
        send[place[0, p]] += image
        send[place[1, p]] += image
        rr, dq, qq, rq = sums
        return rr + rp * rp, dq + dp * image, qq + image * image, rq + rp * image

    sums = lax.fori_loop(0, npatch, body, (zero,) * 4, unroll=unroll)
    tile = lanes(sums)
    for i in range(ndest):
        send[i * per + per - 1] = tile


def last_patch_kernel(unroll, coef, comp, r, d, x, q, d_out, x_out, sums_out):
    npatch, ncase, width = d.shape
    alpha, beta = coef[0], coef[1]
    zero = jnp.zeros((ncase, width), jnp.float32)

    def body(p, sums):
        dp = d[p]
        x_out[p] = x[p] + alpha * dp
        rp = r[p] - alpha * q[p]
        dp = rp + beta * dp
        d_out[p] = dp
        rr, dq = sums
        return rr + rp * rp, dq + comp[pl.ds(p, 1), :] * dp * dp

    sums_out[...] = lanes(lax.fori_loop(0, npatch, body, (zero,) * 2, unroll=unroll))


def owner_kernel(first, last, nsub, nbody, recv, load_r, load_d, block, *refs):
    if last:
        sums_out, held, sems = refs
    else:
        resp, r_out, d_out, coef, held, sems = refs
    if last:
        r_out, d_out, coef = None, None, refs[0]
    per, ncase, width = recv.shape[1:]
    nslot = per - 1
    gap = nbody * width
    copies = []
    for j in range(nslot):
        rows = pl.ds(j * gap, gap)
        copies.append(pltpu.make_async_copy(block.at[rows], held.at[rows], sems.at[j]))
        copies[-1].start()
    if not first:
        dots = recv[0, nslot]
        for i in range(1, nbody * nsub):
            dots = dots + recv[i, nslot]
        rr, dq, qq, rq = (dots[:, i : i + 1] for i in range(4))
        alpha = rr / dq
        beta = (rr - 2.0 * alpha * rq + alpha * alpha * qq) / rr
    total = jnp.zeros((ncase, nslot * gap), jnp.float32)
    loads = []
    for j in range(nslot):
        pieces = []
        for h in range(nbody):
            piece = recv[h * nsub, j]
            for i in range(1, nsub):
                piece = piece + recv[h * nsub + i, j]
            columns = slice(j * gap + h * width, j * gap + (h + 1) * width)
            if not first:
                residual = load_r[:, columns] - alpha * piece
                direction = residual + beta * load_d[:, columns]
            else:
                residual = direction = piece
            if not last:
                r_out[:, columns] = residual
                d_out[:, columns] = direction
            pieces.append(direction)
        load = jnp.concatenate(pieces, axis=1)
        loads.append(load)
        copies[j].wait()
        total = total + jnp.dot(
            load.astype(jnp.bfloat16),
            held[j * gap : (j + 1) * gap, :],
            preferred_element_type=jnp.float32,
        )
    if last:
        product = jnp.concatenate(loads, axis=1) * total
        sums = product[:, :width]
        for i in range(1, nslot * nbody):
            sums = sums + product[:, i * width : (i + 1) * width]
        lane = lax.broadcasted_iota(jnp.int32, sums.shape, 1)
        sums_out[0] = jnp.where(lane == 1, jnp.sum(sums, axis=1, keepdims=True), 0.0)
        sums_out[1] = jnp.broadcast_to(alpha, sums.shape)
        sums_out[2] = jnp.broadcast_to(beta, sums.shape)
        return
    if first:
        coef[...] = jnp.zeros_like(coef)
    else:
        coef[0] = jnp.broadcast_to(alpha, coef.shape[1:])
        coef[1] = jnp.broadcast_to(beta, coef.shape[1:])
    for j in range(nslot):
        for h in range(nbody):
            tile = total[:, j * gap + h * width : j * gap + (h + 1) * width]
            for i in range(nsub):
                resp[h * nsub + i, j] = tile


def exchange(messages):
    return lax.all_to_all(messages, AXES, split_axis=0, concat_axis=0, tiled=True)


def on_device(rhs, compliance, plate_owner, found_owner, slot_pairs, active, inverse):
    nsub = lax.axis_size("sub")
    nbody = lax.axis_size("body")
    side = lax.axis_index("body")
    ncase, npatch, gap = rhs.shape
    block = inverse[0, 0]
    iface = block.shape[0]
    nslot = iface // gap
    width = gap // nbody
    ndest = nbody * nsub
    per = nslot + 1
    unroll = 4

    keep = active.astype(jnp.float32)
    owners = jnp.stack([plate_owner[:, 0], found_owner[:, 0] + nsub])
    slots = slot_pairs.T
    place = jnp.concatenate([owners * per + slots, owners * nslot + slots]).astype(jnp.int32)
    comp = lax.dynamic_slice_in_dim(compliance, side * width, width, axis=1)
    part = lax.dynamic_slice_in_dim(rhs, side * width, width, axis=2)
    start = jnp.transpose(keep[None, :, None] * part, (1, 0, 2))

    field = f32(npatch, ncase, width)
    message = f32(ndest * per, ncase, width)
    coefs = f32(2, ncase, width)
    loads = f32(ncase, iface)
    scratch = [pltpu.VMEM((iface, iface), jnp.bfloat16), pltpu.SemaphoreType.DMA((nslot,))]

    send = pl.pallas_call(
        functools.partial(load_kernel, ndest, per, unroll),
        out_shape=message,
        in_specs=[SMEM, VMEM],
        out_specs=VMEM,
        compiler_params=PARAMS,
    )(place, start)
    r = d = x = q = start
    load_r = load_d = jnp.zeros((ncase, iface), jnp.float32)
    for step in range(ITERS):
        first, last = step == 0, step == ITERS - 1
        recv = exchange(send.reshape(ndest, per, ncase, width))
        owner_call = functools.partial(
            pl.pallas_call,
            functools.partial(owner_kernel, first, last, nsub, nbody),
            in_specs=[VMEM, VMEM, VMEM, ANY],
            scratch_shapes=scratch,
            compiler_params=PARAMS,
        )
        if last:
            ends = owner_call(out_shape=f32(3, ncase, width), out_specs=VMEM)(recv, load_r, load_d, block)
            break
        resp, load_r, load_d, coef = owner_call(
            out_shape=(f32(ndest, nslot, ncase, width), loads, loads, coefs), out_specs=(VMEM,) * 4
        )(recv, load_r, load_d, block)
        resp = exchange(resp).reshape(ndest * nslot, ncase, width)
        r, d, x, q, send = pl.pallas_call(
            functools.partial(patch_kernel, first, ndest, per, unroll),
            out_shape=(field,) * 4 + (message,),
            in_specs=[SMEM, SMEM] + [VMEM] * 7,
            out_specs=(VMEM,) * 5,
            compiler_params=PARAMS,
        )(place, keep, coef, resp, comp, r, d, x, q)
    d, x, sums = pl.pallas_call(
        functools.partial(last_patch_kernel, unroll),
        out_shape=(field, field, f32(ncase, width)),
        in_specs=[VMEM] * 6,
        out_specs=(VMEM,) * 3,
        compiler_params=PARAMS,
    )(ends[1:], comp, r, d, x, q)
    swap = [(i, nbody - 1 - i) for i in range(nbody)]
    other_d, other_x = lax.ppermute(d, "body", swap), lax.ppermute(x, "body", swap)
    sums = exchange(jnp.broadcast_to((sums + ends[0])[None], (ndest, ncase, width)))
    sums = jnp.sum(sums, axis=0)
    alpha = sums[:, 0:1] / sums[:, 1:2]
    mine, other = x + alpha[None] * d, other_x + alpha[None] * other_d
    both = jnp.stack([jnp.where(side == 0, mine, other), jnp.where(side == 0, other, mine)])
    return jnp.transpose(both, (2, 1, 0, 3)).reshape(ncase, npatch, gap)


def solution(mesh):
    in_specs = (
        P(None, "sub", None),
        P("sub", None),
        P("sub", None),
        P("sub", None),
        P("sub", None),
        P("sub"),
        P("body", "sub", None, None),
    )
    out_specs = P(None, "sub", None)
    return jax.shard_map(
        on_device, mesh=mesh, in_specs=in_specs, out_specs=out_specs, check_vma=False
    )
```

```python
import functools

import jax
import jax.numpy as jnp
from jax import lax
from jax.experimental import pallas as pl
from jax.experimental.pallas import tpu as pltpu
from jax.sharding import PartitionSpec as P

ITERS = 4
AXES = ("body", "sub")
VMEM = pl.BlockSpec(memory_space=pltpu.VMEM)
SMEM = pl.BlockSpec(memory_space=pltpu.SMEM)
ANY = pl.BlockSpec(memory_space=pl.ANY)
PARAMS = pltpu.CompilerParams(vmem_limit_bytes=40 * 1024 * 1024)


def f32(*shape):
    return jax.ShapeDtypeStruct(shape, jnp.float32)


def lanes(parts):
    lane = lax.broadcasted_iota(jnp.int32, parts[0].shape, 1)
    tile = jnp.zeros_like(parts[0])
    for i, part in enumerate(parts):
        tile = jnp.where(lane == i, jnp.sum(part, axis=1, keepdims=True), tile)
    return tile


def split_message(total, keep_a, send_a, keep_b, send_b):
    rows = keep_a.shape[0]
    for i, out in enumerate((keep_a, send_a, keep_b, send_b)):
        out[...] = total[i * rows : (i + 1) * rows]


def load_kernel(unroll, place, field, keep_a, send_a, keep_b, send_b, total):
    total[...] = jnp.zeros_like(total)

    def body(p, carry):
        value = field[p]
        total[place[0, p]] += value
        total[place[1, p]] += value
        return carry

    lax.fori_loop(0, field.shape[0], body, 0, unroll=unroll)
    split_message(total, keep_a, send_a, keep_b, send_b)


def patch_kernel(first, per, nparts, unroll, place, keep, coef, comp, r, d, x, q, *refs):
    parts, refs = refs[:nparts], refs[nparts:]
    r_out, d_out, x_out, q_out, keep_a, send_a, keep_b, send_b, total, resp = refs
    npatch, ncase, width = d.shape
    at = 0
    for part in parts:
        resp[at : at + part.shape[0]] = part[...]
        at += part.shape[0]
    total[...] = jnp.zeros_like(total)
    alpha, beta = coef[0], coef[1]
    zero = jnp.zeros((ncase, width), jnp.float32)

    def body(p, sums):
        rp, dp = r[p], d[p]
        if first:
            x_out[p] = zero
        else:
            x_out[p] = x[p] + alpha * dp
            rp = rp - alpha * q[p]
            dp = rp + beta * dp
        r_out[p] = rp
        d_out[p] = dp
        image = resp[place[2, p]] + resp[place[3, p]] + comp[pl.ds(p, 1), :] * dp
        image = keep[p] * image
        q_out[p] = image
        total[place[0, p]] += image
        total[place[1, p]] += image
        rr, dq, qq, rq = sums
        return rr + rp * rp, dq + dp * image, qq + image * image, rq + rp * image

    sums = lax.fori_loop(0, npatch, body, (zero,) * 4, unroll=unroll)
    tile = lanes(sums)
    for i in range(total.shape[0] // per):
        total[i * per + per - 1] = tile
    split_message(total, keep_a, send_a, keep_b, send_b)


def last_patch_kernel(unroll, coef, comp, r, d, x, q, d_out, x_out, sums_out):
    npatch, ncase, width = d.shape
    alpha, beta = coef[0], coef[1]
    zero = jnp.zeros((ncase, width), jnp.float32)

    def body(p, sums):
        dp = d[p]
        x_out[p] = x[p] + alpha * dp
        rp = r[p] - alpha * q[p]
        dp = rp + beta * dp
        d_out[p] = dp
        rr, dq = sums
        return rr + rp * rp, dq + comp[pl.ds(p, 1), :] * dp * dp

    sums_out[...] = lanes(lax.fori_loop(0, npatch, body, (zero,) * 2, unroll=unroll))


def second_kernel(keep_a, recv_a, keep_b, recv_b, send_a, send_b):
    rows = send_a.shape[0]
    send_a[...] = keep_a[rows:] + recv_a[rows:]
    send_b[...] = keep_b[rows:] + recv_b[rows:]


def third_kernel(per, keep_a, one_a, two_a, keep_b, one_b, two_b, *outs):
    nz = len(outs) // 2
    for side, (keep, one, two) in enumerate(((keep_a, one_a, two_a), (keep_b, one_b, two_b))):
        for z in range(nz):
            rows = slice(z * per, (z + 1) * per)
            outs[side * nz + z][...] = keep[rows] + one[rows] + two[rows]


def owner_kernel(first, last, nbody, nz, side, load_r, load_d, block, *refs):
    recv, refs = refs[: nbody * nz], refs[nbody * nz :]
    if last:
        sums_out, held, sems = refs
    else:
        own, other, r_out, d_out, coef, held, sems = refs
    per, ncase, width = recv[0].shape
    nslot = per - 1
    gap = nbody * width
    copies = []
    for j in range(nslot):
        rows = pl.ds(j * gap, gap)
        copies.append(pltpu.make_async_copy(block.at[rows], held.at[rows], sems.at[j]))
        copies[-1].start()
    is_first_half = jnp.full((ncase, width), side[0], jnp.int32) == 0
    if not first:
        dots = recv[0][nslot]
        for part in recv[1:]:
            dots = dots + part[nslot]
        rr, dq, qq, rq = (dots[:, i : i + 1] for i in range(4))
        alpha = rr / dq
        beta = (rr - 2.0 * alpha * rq + alpha * alpha * qq) / rr
    total = jnp.zeros((ncase, nslot * gap), jnp.float32)
    loads = []
    for j in range(nslot):
        mine, far = recv[0][j], recv[nz][j]
        for z in range(1, nz):
            mine, far = mine + recv[z][j], far + recv[nz + z][j]
        piece = jnp.concatenate(
            [jnp.where(is_first_half, mine, far), jnp.where(is_first_half, far, mine)], axis=1
        )
        columns = slice(j * gap, (j + 1) * gap)
        if first:
            residual = direction = piece
        else:
            residual = load_r[:, columns] - alpha * piece
            direction = residual + beta * load_d[:, columns]
        if not last:
            r_out[:, columns] = residual
            d_out[:, columns] = direction
        loads.append(direction)
        copies[j].wait()
        total = total + jnp.dot(
            direction.astype(jnp.bfloat16), held[columns, :], preferred_element_type=jnp.float32
        )
    if last:
        product = jnp.concatenate(loads, axis=1) * total
        sums = product[:, :width]
        for i in range(1, nslot * nbody):
            sums = sums + product[:, i * width : (i + 1) * width]
        lane = lax.broadcasted_iota(jnp.int32, sums.shape, 1)
        sums_out[0] = jnp.where(lane == 1, jnp.sum(sums, axis=1, keepdims=True), 0.0)
        sums_out[1] = jnp.broadcast_to(alpha, sums.shape)
        sums_out[2] = jnp.broadcast_to(beta, sums.shape)
        return
    if first:
        coef[...] = jnp.zeros_like(coef)
    else:
        coef[0] = jnp.broadcast_to(alpha, coef.shape[1:])
        coef[1] = jnp.broadcast_to(beta, coef.shape[1:])
    for j in range(nslot):
        one = total[:, j * gap : j * gap + width]
        two = total[:, j * gap + width : (j + 1) * gap]
        own[j] = jnp.where(is_first_half, one, two)
        other[j] = jnp.where(is_first_half, two, one)


def tree(values):
    while len(values) > 1:
        values = [a + b for a, b in zip(values[::2], values[1::2])]
    return values[0]


def call(kernel, out_shape, specs, *operands, scratch=()):
    several = isinstance(out_shape, (tuple, list))
    return pl.pallas_call(
        kernel,
        out_shape=tuple(out_shape) if several else out_shape,
        in_specs=specs,
        out_specs=(VMEM,) * len(out_shape) if several else VMEM,
        scratch_shapes=list(scratch),
        compiler_params=PARAMS,
    )(*operands)


def on_device(rhs, compliance, plate_owner, found_owner, slot_pairs, active, inverse):
    nsub = lax.axis_size("sub")
    nbody = lax.axis_size("body")
    side = lax.axis_index("body")
    me = lax.axis_index("sub")
    ncase, npatch, gap = rhs.shape
    block = inverse[0, 0]
    iface = block.shape[0]
    nslot = iface // gap
    width = gap // nbody
    per = nslot + 1
    nz = nsub // 4
    unroll = 4

    def swap(value, far_body, far_sub):
        pairs = [
            (b * nsub + s, (b ^ far_body) * nsub + (s ^ far_sub)) for b in range(nbody) for s in range(nsub)
        ]
        return lax.ppermute(value, AXES, pairs)

    keep = active.astype(jnp.float32)
    owners = jnp.stack([plate_owner[:, 0], found_owner[:, 0]])
    slots = slot_pairs.T
    owners = jnp.where(side == 0, owners, owners[::-1])
    slots = jnp.where(side == 0, slots, slots[::-1])
    away = owners ^ me
    x_bit, y_bit, z_part = away & 1, (away >> 1) & 1, away >> 2
    order = jnp.stack([x_bit[0] * 2 + y_bit[0], nbody * 2 + y_bit[1] * 2 + x_bit[1]]) * nz + z_part
    place = jnp.concatenate([order * per + slots, order * nslot + slots]).astype(jnp.int32)
    comp = lax.dynamic_slice_in_dim(compliance, side * width, width, axis=1)
    part = lax.dynamic_slice_in_dim(rhs, side * width, width, axis=2)
    start = jnp.transpose(keep[None, :, None] * part, (1, 0, 2))
    which = side.astype(jnp.int32).reshape(1)

    field = f32(npatch, ncase, width)
    half = f32(2 * nz * per, ncase, width)
    quarter = f32(nz * per, ncase, width)
    one = f32(per, ncase, width)
    answer = f32(nslot, ncase, width)
    coefs = f32(2, ncase, width)
    loads = f32(ncase, iface)
    whole = pltpu.VMEM((nbody * nsub * per, ncase, width), jnp.float32)
    whole_resp = pltpu.VMEM((nbody * nsub * nslot, ncase, width), jnp.float32)

    def gather_loads(parts):
        keep_a, send_a, keep_b, send_b = parts
        one_a, one_b = swap(send_a, 0, 1), swap(send_b, 0, 2)
        send_a, send_b = call(second_kernel, (quarter,) * 2, [VMEM] * 4, keep_a, one_a, keep_b, one_b)
        two_a, two_b = swap(send_a, 0, 2), swap(send_b, 0, 1)
        blocks = call(
            functools.partial(third_kernel, per),
            (one,) * (2 * nz),
            [VMEM] * 6,
            keep_a,
            one_a,
            two_a,
            keep_b,
            one_b,
            two_b,
        )
        mine = [blocks[0]] + [swap(blocks[z], 0, 4 * z) for z in range(1, nz)]
        return mine + [swap(blocks[nz + z], 1, 4 * z) for z in range(nz)]

    def spread(own, other):
        a = jnp.concatenate([own] + [swap(own, 0, 4 * z) for z in range(1, nz)])
        b = jnp.concatenate([swap(other, 1, 4 * z) for z in range(nz)])
        a = jnp.concatenate([a, swap(a, 0, 2)])
        b = jnp.concatenate([b, swap(b, 0, 1)])
        return [a, swap(a, 0, 1), b, swap(b, 0, 2)]

    parts = call(
        functools.partial(load_kernel, unroll), (half,) * 4, [SMEM, VMEM], place, start, scratch=[whole]
    )
    r = d = x = q = start
    load_r = load_d = jnp.zeros((ncase, iface), jnp.float32)
    for step in range(ITERS):
        first, last = step == 0, step == ITERS - 1
        recv = gather_loads(parts)
        owned = call(
            functools.partial(owner_kernel, first, last, nbody, nz),
            f32(3, ncase, width) if last else (answer, answer, loads, loads, coefs),
            [SMEM, VMEM, VMEM, ANY] + [VMEM] * len(recv),
            which,
            load_r,
            load_d,
            block,
            *recv,
            scratch=[pltpu.VMEM((iface, iface), jnp.bfloat16), pltpu.SemaphoreType.DMA((nslot,))],
        )
        if last:
            break
        own, other, load_r, load_d, coef = owned
        resp = spread(own, other)
        r, d, x, q, *parts = call(
            functools.partial(patch_kernel, first, per, len(resp), unroll),
            (field,) * 4 + (half,) * 4,
            [SMEM, SMEM] + [VMEM] * (6 + len(resp)),
            place,
            keep,
            coef,
            comp,
            r,
            d,
            x,
            q,
            *resp,
            scratch=[whole, whole_resp],
        )
    d, x, sums = call(
        functools.partial(last_patch_kernel, unroll),
        (field, field, f32(ncase, width)),
        [VMEM] * 6,
        owned[1:],
        comp,
        r,
        d,
        x,
        q,
    )
    other_d, other_x = swap(d, 1, 0), swap(x, 1, 0)
    sums = sums + owned[0]
    sums = tree([sums] + [swap(sums, b, s) for b in range(nbody) for s in range(4) if b + s > 0])
    sums = tree([sums] + [swap(sums, 0, 4 * z) for z in range(1, nz)])
    alpha = sums[:, 0:1] / sums[:, 1:2]
    mine, theirs = x + alpha[None] * d, other_x + alpha[None] * other_d
    both = jnp.stack([jnp.where(side == 0, mine, theirs), jnp.where(side == 0, theirs, mine)])
    return jnp.transpose(both, (2, 1, 0, 3)).reshape(ncase, npatch, gap)


def solution(mesh):
    in_specs = (
        P(None, "sub", None),
        P("sub", None),
        P("sub", None),
        P("sub", None),
        P("sub", None),
        P("sub"),
        P("body", "sub", None, None),
    )
    out_specs = P(None, "sub", None)
    return jax.shard_map(
        on_device, mesh=mesh, in_specs=in_specs, out_specs=out_specs, check_vma=False
    )
```

```python
import functools

import jax
import jax.numpy as jnp
from jax import lax
from jax.experimental import pallas as pl
from jax.experimental.pallas import tpu as pltpu
from jax.sharding import PartitionSpec as P

ITERS = 4
LANES = 128
SUBLANES = 8
VMEM = pl.BlockSpec(memory_space=pltpu.VMEM)
SMEM = pl.BlockSpec(memory_space=pltpu.SMEM)
ANY = pl.BlockSpec(memory_space=pl.ANY)
PARAMS = pltpu.CompilerParams(vmem_limit_bytes=40 * 1024 * 1024)


def f32(*shape):
    return jax.ShapeDtypeStruct(shape, jnp.float32)


def call(kernel, out_shape, specs, *operands, scratch=()):
    several = isinstance(out_shape, (tuple, list))
    return pl.pallas_call(
        kernel,
        out_shape=tuple(out_shape) if several else out_shape,
        in_specs=specs,
        out_specs=(VMEM,) * len(out_shape) if several else VMEM,
        scratch_shapes=list(scratch),
        compiler_params=PARAMS,
    )(*operands)


def fetch(block, held, sems):
    pieces = sems.shape[0]
    size = block.shape[0] // pieces
    copies = []
    for j in range(pieces):
        rows = pl.ds(j * size, size)
        copies.append(pltpu.make_async_copy(block.at[rows], held.at[rows], sems.at[j]))
        copies[-1].start()
    return copies


def per_case(value):
    return jnp.sum(value, axis=1, keepdims=True)


def respond(copies, held, load, gamma, energy, answer):
    ntile, ncase, width = load.shape
    npiece = len(copies)
    each = ntile // npiece
    total = jnp.zeros((2 * ncase, ntile * width), jnp.float32)
    for j in range(npiece):
        value = jnp.concatenate([load[j * each + i] for i in range(each)], axis=1)
        high = value.astype(jnp.bfloat16)
        low = (value - high.astype(jnp.float32)).astype(jnp.bfloat16)
        copies[j].wait()
        total = total + jnp.dot(
            jnp.concatenate([high, low], axis=0),
            held[j * each * width : (j + 1) * each * width, :],
            preferred_element_type=jnp.float32,
        )
    total = total[:ncase] + total[ncase:]
    work = 0.5 * energy
    for i in range(ntile):
        tile = total[:, i * width : (i + 1) * width]
        answer[i] = tile
        work = work + load[i] * tile
    lane = lax.broadcasted_iota(jnp.int32, work.shape, 1)
    sums = jnp.where(lane == 0, per_case(0.5 * gamma), 0.0)
    answer[ntile] = jnp.where(lane == 1, per_case(work), sums)


def pack_kernel(nh, tiles, place, field, table, message):
    ndest = message.shape[0] // tiles
    extra = table.shape[1]
    message[...] = jnp.zeros_like(message)

    def body(p, carry):
        message[pl.ds(place[p], nh)] = field[p]
        return carry

    lax.fori_loop(0, field.shape[0], body, 0, unroll=4)
    for i in range(ndest):
        message[(i + 1) * tiles - extra : (i + 1) * tiles] = table[i]


def start_kernel(nh, room, tiles, place, comp, message, block, r_out, answer, load, held, sems):
    copies = fetch(block, held, sems)
    load[...] = jnp.zeros_like(load)
    nrow = r_out.shape[0]
    zero = jnp.zeros(r_out.shape[2:], jnp.float32)

    def pair(i, sums):
        gamma, energy = sums
        for j in range(room):
            row = i * room + j
            r = message[pl.ds(i * tiles + j * nh, nh)]
            r_out[row] = r
            load[pl.ds(place[0, row], nh)] += r
            c = comp[row]
            for h in range(nh):
                square = r[h] * r[h]
                gamma = gamma + square
                energy = energy + c[h : h + 1] * square
        return gamma, energy

    gamma, energy = lax.fori_loop(0, nrow // room, pair, (zero, zero))
    respond(copies, held, load, gamma, energy, answer)


def share_kernel(own, other, message):
    last = own.shape[0] - 1
    sums = own[last] + other[last]
    for i in range(message.shape[0]):
        message[i, :last] = other[:last]
        message[i, last] = sums


def steps(first, sums, known):
    gamma, delta = sums[:, 0:1], sums[:, 1:2]
    if first:
        return gamma, gamma / delta, jnp.zeros_like(gamma)
    beta = gamma / known[:, 0:1]
    return gamma, gamma / (delta - beta * gamma / known[:, 1:2]), beta


def home_kernel(first, nh, per, unroll, place, keep, comp, own, recv, known, block, *refs):
    if first:
        r_in, r, d, x, s, answer, known_out, load, held, sems = refs
    else:
        r_in, d_in, x_in, s_in, r, d, x, s, answer, known_out, load, held, sems = refs
    copies = fetch(block, held, sems)
    load[...] = jnp.zeros_like(load)
    ncase, width = r.shape[2:]
    sums = recv[per - 1]
    for i in range(1, recv.shape[0] // per):
        sums = sums + recv[(i + 1) * per - 1]
    gamma, alpha, beta = steps(first, sums, known[...])
    lane = lax.broadcasted_iota(jnp.int32, (ncase, width), 1)
    known_out[...] = jnp.where(lane == 0, gamma, alpha)
    alpha = jnp.broadcast_to(alpha, (ncase, width))
    beta = jnp.broadcast_to(beta, (ncase, width))
    zero = jnp.zeros((ncase, width), jnp.float32)

    def body(row, sums):
        gamma, energy = sums
        near, far, on = place[0, row], place[1, row], keep[row]
        c = comp[row]
        for h in range(nh):
            residual = r_in[row, h]
            image = on * (own[near + h] + recv[far + h] + c[h : h + 1] * residual)
            if first:
                direction, moved = residual, alpha * residual
            else:
                direction = residual + beta * d_in[row, h]
                image = image + beta * s_in[row, h]
                moved = x_in[row, h] + alpha * direction
            residual = residual - alpha * image
            r[row, h], d[row, h], x[row, h], s[row, h] = residual, direction, moved, image
            load[near + h] += residual
            square = residual * residual
            gamma = gamma + square
            energy = energy + c[h : h + 1] * square
        return gamma, energy

    gamma, energy = lax.fori_loop(0, r.shape[0], body, (zero, zero), unroll=unroll)
    respond(copies, held, load, gamma, energy, answer)


def end_kernel(nbody, unroll, side, sums, known, r, d, x, message):
    nrow, nh, ncase, width = r.shape
    total = sums[0]
    for i in range(1, sums.shape[0]):
        total = total + sums[i]
    gamma, alpha, beta = steps(False, total, known[...])
    alpha = jnp.broadcast_to(alpha, (ncase, width))
    beta = jnp.broadcast_to(beta, (ncase, width))
    share = ncase // nbody
    which = jnp.full((nh * share, width), side[0], jnp.int32)

    def body(row, carry):
        moved = [x[row, h] + alpha * (r[row, h] + beta * d[row, h]) for h in range(nh)]
        tile = None
        for b in range(nbody):
            part = jnp.concatenate([value[b * share : (b + 1) * share] for value in moved], axis=0)
            tile = part if tile is None else jnp.where(which == b, part, tile)
        message[row] = tile
        return carry

    lax.fori_loop(0, nrow, body, 0, unroll=unroll)


def take_kernel(row, recv, out):
    def body(p, carry):
        out[p] = recv[row[p]]
        return carry

    lax.fori_loop(0, out.shape[0], body, 0, unroll=8)


def on_device(rhs, compliance, plate_owner, found_owner, slot_pairs, active, inverse):
    nsub = lax.axis_size("sub")
    nbody = lax.axis_size("body")
    side = lax.axis_index("body")
    ncase, npatch, gap = rhs.shape
    block = inverse[0, 0]
    nslot = block.shape[0] // gap
    nh = gap // LANES
    per = nslot * nh + 1
    room = max(2, 2 * npatch // nsub)
    nrow = nsub * room
    lines = -(-room * nh // SUBLANES)
    deep = -(-room // SUBLANES)
    tiles = room * nh + lines + deep
    unroll = 4

    def exchange(message):
        return lax.all_to_all(message, "sub", split_axis=0, concat_axis=0, tiled=True)

    def sibling(value):
        return lax.ppermute(value, "body", [(i, nbody - 1 - i) for i in range(nbody)])

    keep = active.astype(jnp.float32)
    owners = jnp.stack([plate_owner[:, 0], found_owner[:, 0]])
    slots = slot_pairs.T
    owner, other = jnp.where(side == 0, owners, owners[::-1])
    slot, other_slot = jnp.where(side == 0, slots, slots[::-1])
    index = jnp.arange(npatch, dtype=jnp.int32)
    earlier = (owner[None, :] == owner[:, None]) & (index[None, :] < index[:, None])
    rank = jnp.sum(earlier.astype(jnp.int32), axis=1)
    row = owner * room + rank
    place = owner * tiles + rank * nh

    facts = jnp.stack([slot * nh, other * per + other_slot * nh], axis=1).astype(jnp.float32)
    facts = jnp.concatenate([facts, keep[:, None]], axis=1)
    facts = jnp.concatenate([compliance, jnp.pad(facts, ((0, 0), (0, LANES - 3)))], axis=1)
    placed = (row[None, :] == jnp.arange(nrow, dtype=jnp.int32)[:, None]).astype(jnp.float32)
    facts = jnp.dot(placed, facts, precision=lax.Precision.HIGHEST).reshape(nsub, room, gap + LANES)
    lined = facts[:, :, :gap].reshape(nsub, room * nh, LANES)
    lined = jnp.pad(lined, ((0, 0), (0, lines * SUBLANES - room * nh), (0, 0)))
    named = jnp.pad(facts[:, :, gap:], ((0, 0), (0, deep * SUBLANES - room), (0, 0)))
    table = jnp.concatenate([lined, named], axis=1).reshape(nsub, lines + deep, SUBLANES, LANES)
    start = (keep[None, :, None] * rhs).reshape(ncase, npatch, nh, LANES)
    start = jnp.transpose(start, (1, 2, 0, 3))

    message = call(
        functools.partial(pack_kernel, nh, tiles),
        f32(nsub * tiles, ncase, LANES),
        [SMEM, VMEM, VMEM],
        place,
        start,
        table,
    )
    message = exchange(message.reshape(nsub, tiles, ncase, LANES))
    told = message[:, room * nh :].reshape(nsub, (lines + deep) * SUBLANES, LANES)
    comp = told[:, : room * nh].reshape(nrow, nh, LANES)
    named = told[:, lines * SUBLANES : lines * SUBLANES + room, :3].reshape(nrow, 3).T
    home = named[:2].astype(jnp.int32)
    on = named[2]

    field = f32(nrow, nh, ncase, LANES)
    answer = f32(per, ncase, LANES)
    held = [
        pltpu.VMEM((nslot * nh, ncase, LANES), jnp.float32),
        pltpu.VMEM(block.shape, block.dtype),
        pltpu.SemaphoreType.DMA((nslot,)),
    ]
    r, own = call(
        functools.partial(start_kernel, nh, room, tiles),
        (field, answer),
        [SMEM, VMEM, VMEM, ANY],
        home,
        comp,
        message.reshape(nsub * tiles, ncase, LANES),
        block,
        scratch=held,
    )
    known = jnp.zeros((ncase, LANES), jnp.float32)
    state = [r]
    for step in range(ITERS - 1):
        message = call(share_kernel, f32(nsub, per, ncase, LANES), [VMEM] * 2, own, sibling(own))
        recv = exchange(message).reshape(nsub * per, ncase, LANES)
        *state, own, known = call(
            functools.partial(home_kernel, step == 0, nh, per, unroll),
            (field,) * 4 + (answer, f32(ncase, LANES)),
            [SMEM, SMEM] + [VMEM] * 4 + [ANY] + [VMEM] * len(state),
            home,
            on,
            comp,
            own,
            recv,
            known,
            block,
            *state,
            scratch=held,
        )
    r, d, x, _ = state
    sums = own[per - 1]
    sums = sums + sibling(sums)
    sums = exchange(jnp.broadcast_to(sums[None], (nsub, ncase, LANES)))
    message = call(
        functools.partial(end_kernel, nbody, unroll),
        f32(nrow, nh * ncase // nbody, LANES),
        [SMEM] + [VMEM] * 5,
        side.astype(jnp.int32).reshape(1),
        sums,
        known,
        r,
        d,
        x,
    )
    recv = exchange(message)
    mine = call(take_kernel, f32(npatch, nh * ncase // nbody, LANES), [SMEM, VMEM], row, recv)
    theirs = sibling(mine)
    both = jnp.stack([jnp.where(side == 0, mine, theirs), jnp.where(side == 0, theirs, mine)])
    both = both.reshape(nbody, npatch, nh, ncase // nbody, LANES)
    return jnp.transpose(both, (0, 3, 1, 2, 4)).reshape(ncase, npatch, gap)


def solution(mesh):
    in_specs = (
        P(None, "sub", None),
        P("sub", None),
        P("sub", None),
        P("sub", None),
        P("sub", None),
        P("sub"),
        P("body", "sub", None, None),
    )
    out_specs = P(None, "sub", None)
    return jax.shard_map(
        on_device, mesh=mesh, in_specs=in_specs, out_specs=out_specs, check_vma=False
    )
```

```python
import functools

import jax
import jax.numpy as jnp
from jax import lax
from jax.experimental import pallas as pl
from jax.experimental.pallas import tpu as pltpu
from jax.sharding import PartitionSpec as P

ITERS = 4
LANES = 128
SUBLANES = 8
VMEM = pl.BlockSpec(memory_space=pltpu.VMEM)
SMEM = pl.BlockSpec(memory_space=pltpu.SMEM)
PARAMS = pltpu.CompilerParams(vmem_limit_bytes=40 * 1024 * 1024)


def f32(*shape):
    return jax.ShapeDtypeStruct(shape, jnp.float32)


def call(kernel, out_shape, specs, *operands, scratch=()):
    several = isinstance(out_shape, (tuple, list))
    return pl.pallas_call(
        kernel,
        out_shape=tuple(out_shape) if several else out_shape,
        in_specs=specs,
        out_specs=(VMEM,) * len(out_shape) if several else VMEM,
        scratch_shapes=list(scratch),
        compiler_params=PARAMS,
    )(*operands)


def per_case(value):
    return jnp.sum(value, axis=1, keepdims=True)


def respond(block, load, gamma, energy, answer):
    ntile, ncase, width = load.shape
    each = 2
    total = jnp.zeros((2 * ncase, ntile * width), jnp.float32)
    for j in range(ntile // each):
        value = jnp.concatenate([load[j * each + i] for i in range(each)], axis=1)
        high = value.astype(jnp.bfloat16)
        low = (value - high.astype(jnp.float32)).astype(jnp.bfloat16)
        total = total + jnp.dot(
            jnp.concatenate([high, low], axis=0),
            block[j * each * width : (j + 1) * each * width, :],
            preferred_element_type=jnp.float32,
        )
    total = total[:ncase] + total[ncase:]
    work = 0.5 * energy
    for i in range(ntile):
        tile = total[:, i * width : (i + 1) * width]
        answer[i] = tile
        work = work + load[i] * tile
    lane = lax.broadcasted_iota(jnp.int32, work.shape, 1)
    sums = jnp.where(lane == 0, per_case(0.5 * gamma), 0.0)
    answer[ntile] = jnp.where(lane == 1, per_case(work), sums)


def pack_kernel(nh, place, field, message):
    message[...] = jnp.zeros_like(message)

    def body(p, carry):
        message[pl.ds(place[p], nh)] = field[p]
        return carry

    lax.fori_loop(0, field.shape[0], body, 0, unroll=4)


def start_kernel(nh, room, place, comp, message, block, answer, load):
    load[...] = jnp.zeros_like(load)
    nrow = message.shape[0]
    zero = jnp.zeros(message.shape[2:], jnp.float32)

    def pair(i, sums):
        gamma, energy = sums
        for j in range(room):
            row = i * room + j
            r = message[row]
            load[pl.ds(place[0, row], nh)] += r
            c = comp[row]
            for h in range(nh):
                square = r[h] * r[h]
                gamma = gamma + square
                energy = energy + c[h : h + 1] * square
        return gamma, energy

    gamma, energy = lax.fori_loop(0, nrow // room, pair, (zero, zero))
    respond(block, load, gamma, energy, answer)


def tree(values):
    while len(values) > 1:
        values = [a + b for a, b in zip(values[::2], values[1::2])]
    return values[0]


def steps(first, sums, known):
    gamma, delta = sums[:, 0:1], sums[:, 1:2]
    if first:
        return gamma, gamma / delta, jnp.zeros_like(gamma)
    beta = gamma / known[:, 0:1]
    return gamma, gamma / (delta - beta * gamma / known[:, 1:2]), beta


def home_kernel(first, nh, unroll, place, keep, comp, own, near_a, far_a, near_b, far_b, known, block, *refs):
    if first:
        r_in, r, d, x, s, answer, known_out, load, resp = refs
    else:
        r_in, d_in, x_in, s_in, r, d, x, s, answer, known_out, load, resp = refs
    load[...] = jnp.zeros_like(load)
    ncase, width = r.shape[2:]
    at = 0
    for part in (near_a, far_a, near_b, far_b):
        resp[at : at + part.shape[0]] = part[...]
        at += part.shape[0]
    each = own.shape[0] // 2 + 1
    sums = tree([part[i + each - 1] for part in (near_b, far_b) for i in range(0, part.shape[0], each)])
    gamma, alpha, beta = steps(first, sums, known[...])
    lane = lax.broadcasted_iota(jnp.int32, (ncase, width), 1)
    known_out[...] = jnp.where(lane == 0, gamma, alpha)
    alpha = jnp.broadcast_to(alpha, (ncase, width))
    beta = jnp.broadcast_to(beta, (ncase, width))
    zero = jnp.zeros((ncase, width), jnp.float32)

    def body(row, sums):
        gamma, energy = sums
        near, far, on = place[0, row], place[1, row], keep[row]
        c = comp[row]
        for h in range(nh):
            residual = r_in[row, h]
            image = on * (own[near + h] + resp[far + h] + c[h : h + 1] * residual)
            if first:
                direction, moved = residual, alpha * residual
            else:
                direction = residual + beta * d_in[row, h]
                image = image + beta * s_in[row, h]
                moved = x_in[row, h] + alpha * direction
            residual = residual - alpha * image
            r[row, h], d[row, h], x[row, h], s[row, h] = residual, direction, moved, image
            load[near + h] += residual
            square = residual * residual
            gamma = gamma + square
            energy = energy + c[h : h + 1] * square
        return gamma, energy

    gamma, energy = lax.fori_loop(0, r.shape[0], body, (zero, zero), unroll=unroll)
    respond(block, load, gamma, energy, answer)


def end_kernel(nbody, unroll, side, sums, known, r, d, x, message):
    nrow, nh, ncase, width = r.shape
    gamma, alpha, beta = steps(False, sums[...], known[...])
    alpha = jnp.broadcast_to(alpha, (ncase, width))
    beta = jnp.broadcast_to(beta, (ncase, width))
    share = ncase // nbody
    which = jnp.full((nh * share, width), side[0], jnp.int32)

    def body(row, carry):
        moved = [x[row, h] + alpha * (r[row, h] + beta * d[row, h]) for h in range(nh)]
        tile = None
        for b in range(nbody):
            part = jnp.concatenate([value[b * share : (b + 1) * share] for value in moved], axis=0)
            tile = part if tile is None else jnp.where(which == b, part, tile)
        message[row] = tile
        return carry

    lax.fori_loop(0, nrow, body, 0, unroll=unroll)


def take_kernel(row, recv, out):
    def body(p, carry):
        out[p] = recv[row[p]]
        return carry

    lax.fori_loop(0, out.shape[0], body, 0, unroll=8)


def on_device(rhs, compliance, plate_owner, found_owner, slot_pairs, active, inverse):
    nsub = lax.axis_size("sub")
    nbody = lax.axis_size("body")
    side = lax.axis_index("body")
    ncase, npatch, gap = rhs.shape
    block = inverse[0, 0]
    nslot = block.shape[0] // gap
    nh = gap // LANES
    per = nslot * nh + 1
    room = max(2, 2 * npatch // nsub)
    nrow = nsub * room
    lines = -(-room * nh // SUBLANES)
    deep = -(-room // SUBLANES)
    nz = nsub // 4
    half = nslot // 2 * nh
    unroll = 4

    def exchange(message):
        return lax.all_to_all(message, "sub", split_axis=0, concat_axis=0, tiled=True)

    def swap(value, far):
        return lax.ppermute(value, "sub", [(i, i ^ far) for i in range(nsub)])

    def sibling(value):
        return lax.ppermute(value, "body", [(i, nbody - 1 - i) for i in range(nbody)])

    keep = active.astype(jnp.float32)
    owners = jnp.stack([plate_owner[:, 0], found_owner[:, 0]])
    slots = slot_pairs.T
    owner, other = jnp.where(side == 0, owners, owners[::-1])
    slot, other_slot = jnp.where(side == 0, slots, slots[::-1])
    index = jnp.arange(npatch, dtype=jnp.int32)
    earlier = (owner[None, :] == owner[:, None]) & (index[None, :] < index[:, None])
    rank = jnp.sum(earlier.astype(jnp.int32), axis=1)
    row = owner * room + rank
    place = row * nh

    away = owner ^ other
    x_bit, y_bit, z_part = away & 1, (away >> 1) & 1, away >> 2
    found_a = ((y_bit * 2 + x_bit) * nz + z_part) * half + other_slot * nh
    found_b = ((x_bit * 2 + y_bit) * nz + z_part) * (half + 1) + (other_slot - nslot // 2) * nh
    found = jnp.where(other_slot < nslot // 2, found_a, nsub * half + found_b)

    facts = jnp.stack([slot * nh, found], axis=1).astype(jnp.float32)
    facts = jnp.concatenate([facts, keep[:, None]], axis=1)
    facts = jnp.concatenate([compliance, jnp.pad(facts, ((0, 0), (0, LANES - 3)))], axis=1)
    placed = (row[None, :] == jnp.arange(nrow, dtype=jnp.int32)[:, None]).astype(jnp.float32)
    facts = jnp.dot(placed, facts, precision=lax.Precision.HIGHEST).reshape(nsub, room, gap + LANES)
    lined = facts[:, :, :gap].reshape(nsub, room * nh, LANES)
    lined = jnp.pad(lined, ((0, 0), (0, lines * SUBLANES - room * nh), (0, 0)))
    named = jnp.pad(facts[:, :, gap:], ((0, 0), (0, deep * SUBLANES - room), (0, 0)))
    table = jnp.concatenate([lined, named], axis=1).reshape(nsub, lines + deep, SUBLANES, LANES)
    start = (keep[None, :, None] * rhs).reshape(ncase, npatch, nh, LANES)
    start = jnp.transpose(start, (1, 2, 0, 3))

    told = exchange(table).reshape(nsub, (lines + deep) * SUBLANES, LANES)
    comp = told[:, : room * nh].reshape(nrow, nh, LANES)
    named = told[:, lines * SUBLANES : lines * SUBLANES + room, :3].reshape(nrow, 3).T
    home = named[:2].astype(jnp.int32)
    on = named[2]
    message = call(
        functools.partial(pack_kernel, nh), f32(nrow * nh, ncase, LANES), [SMEM, VMEM], place, start
    )
    r = exchange(message).reshape(nrow, nh, ncase, LANES)

    field = f32(nrow, nh, ncase, LANES)
    answer = f32(per, ncase, LANES)
    load = pltpu.VMEM((nslot * nh, ncase, LANES), jnp.float32)
    spread = pltpu.VMEM((nsub * per, ncase, LANES), jnp.float32)
    own = call(
        functools.partial(start_kernel, nh, room),
        answer,
        [SMEM, VMEM, VMEM, VMEM],
        home,
        comp,
        r,
        block,
        scratch=[load],
    )
    known = jnp.zeros((ncase, LANES), jnp.float32)
    state = [r]
    for step in range(ITERS - 1):
        other = sibling(own)
        other = jnp.concatenate([other[: per - 1], own[per - 1 :] + other[per - 1 :]])
        parts = [other] + [swap(other, 4 * z) for z in range(1, nz)]
        a = jnp.concatenate([part[:half] for part in parts])
        b = jnp.concatenate([part[half:] for part in parts])
        far_a, far_b = swap(a, 1), swap(b, 2)
        a, b = jnp.concatenate([a, far_a]), jnp.concatenate([b, far_b])
        far_a, far_b = swap(a, 2), swap(b, 1)
        *state, own, known = call(
            functools.partial(home_kernel, step == 0, nh, unroll),
            (field,) * 4 + (answer, f32(ncase, LANES)),
            [SMEM, SMEM] + [VMEM] * (8 + len(state)),
            home,
            on,
            comp,
            own,
            a,
            far_a,
            b,
            far_b,
            known,
            block,
            *state,
            scratch=[load, spread],
        )
    r, d, x, _ = state
    sums = own[per - 1]
    sums = sums + sibling(sums)
    far = 1
    while far < nsub:
        sums = sums + swap(sums, far)
        far *= 2
    message = call(
        functools.partial(end_kernel, nbody, unroll),
        f32(nrow, nh * ncase // nbody, LANES),
        [SMEM] + [VMEM] * 5,
        side.astype(jnp.int32).reshape(1),
        sums,
        known,
        r,
        d,
        x,
    )
    recv = exchange(message)
    mine = call(take_kernel, f32(npatch, nh * ncase // nbody, LANES), [SMEM, VMEM], row, recv)
    theirs = sibling(mine)
    both = jnp.stack([jnp.where(side == 0, mine, theirs), jnp.where(side == 0, theirs, mine)])
    both = both.reshape(nbody, npatch, nh, ncase // nbody, LANES)
    return jnp.transpose(both, (0, 3, 1, 2, 4)).reshape(ncase, npatch, gap)


def solution(mesh):
    in_specs = (
        P(None, "sub", None),
        P("sub", None),
        P("sub", None),
        P("sub", None),
        P("sub", None),
        P("sub"),
        P("body", "sub", None, None),
    )
    out_specs = P(None, "sub", None)
    return jax.shard_map(
        on_device, mesh=mesh, in_specs=in_specs, out_specs=out_specs, check_vma=False
    )
```

```python
import functools

import jax
import jax.numpy as jnp
from jax import lax
from jax.experimental import pallas as pl
from jax.experimental.pallas import tpu as pltpu
from jax.sharding import PartitionSpec as P

ITERS = 4
LANES = 128
SUBLANES = 8
VMEM = pl.BlockSpec(memory_space=pltpu.VMEM)
SMEM = pl.BlockSpec(memory_space=pltpu.SMEM)
HBM = pl.BlockSpec(memory_space=pltpu.HBM)
PARAMS = pltpu.CompilerParams(vmem_limit_bytes=20 * 1024 * 1024)


def f32(*shape):
    return jax.ShapeDtypeStruct(shape, jnp.float32)


def call(kernel, out_shape, specs, *operands, scratch=()):
    several = isinstance(out_shape, (tuple, list))
    return pl.pallas_call(
        kernel,
        out_shape=tuple(out_shape) if several else out_shape,
        in_specs=specs,
        out_specs=(VMEM,) * len(out_shape) if several else VMEM,
        scratch_shapes=list(scratch),
        compiler_params=PARAMS,
    )(*operands)


def per_case(value):
    return jnp.sum(value, axis=1, keepdims=True)


def respond(block, load, gamma, energy, answer, copies=()):
    ntile, ncase, width = load.shape
    each = 2
    total = jnp.zeros((2 * ncase, ntile * width), jnp.float32)
    for j in range(ntile // each):
        value = jnp.concatenate([load[j * each + i] for i in range(each)], axis=1)
        high = value.astype(jnp.bfloat16)
        low = (value - high.astype(jnp.float32)).astype(jnp.bfloat16)
        if copies:
            copies[j].wait()
        total = total + jnp.dot(
            jnp.concatenate([high, low], axis=0),
            block[j * each * width : (j + 1) * each * width, :],
            preferred_element_type=jnp.float32,
        )
    total = total[:ncase] + total[ncase:]
    work = 0.5 * energy
    for i in range(ntile):
        tile = total[:, i * width : (i + 1) * width]
        answer[i] = tile
        work = work + load[i] * tile
    lane = lax.broadcasted_iota(jnp.int32, work.shape, 1)
    sums = jnp.where(lane == 0, per_case(0.5 * gamma), 0.0)
    answer[ntile] = jnp.where(lane == 1, per_case(work), sums)


def pack_kernel(nh, tiles, place, field, table, message):
    ndest = message.shape[0] // tiles
    extra = table.shape[1]
    message[...] = jnp.zeros_like(message)

    def body(p, carry):
        message[pl.ds(place[p], nh)] = field[p]
        return carry

    lax.fori_loop(0, field.shape[0], body, 0, unroll=4)
    for i in range(ndest):
        message[(i + 1) * tiles - extra : (i + 1) * tiles] = table[i]


def start_kernel(nh, room, tiles, place, comp, message, block, r_out, answer, load, held, sems):
    pieces = sems.shape[0]
    size = block.shape[0] // pieces
    copies = []
    for j in range(pieces):
        rows = pl.ds(j * size, size)
        copies.append(pltpu.make_async_copy(block.at[rows], held.at[rows], sems.at[j]))
        copies[-1].start()
    load[...] = jnp.zeros_like(load)
    nrow = r_out.shape[0]
    zero = jnp.zeros(r_out.shape[2:], jnp.float32)

    def pair(i, sums):
        gamma, energy = sums
        for j in range(room):
            row = i * room + j
            r = message[pl.ds(i * tiles + j * nh, nh)]
            r_out[row] = r
            load[pl.ds(place[0, row], nh)] += r
            c = comp[row]
            for h in range(nh):
                square = r[h] * r[h]
                gamma = gamma + square
                energy = energy + c[h : h + 1] * square
        return gamma, energy

    gamma, energy = lax.fori_loop(0, nrow // room, pair, (zero, zero))
    respond(held, load, gamma, energy, answer, copies)


def tree(values):
    while len(values) > 1:
        values = [a + b for a, b in zip(values[::2], values[1::2])]
    return values[0]


def steps(first, sums, known):
    gamma, delta = sums[:, 0:1], sums[:, 1:2]
    if first:
        return gamma, gamma / delta, jnp.zeros_like(gamma)
    beta = gamma / known[:, 0:1]
    return gamma, gamma / (delta - beta * gamma / known[:, 1:2]), beta


def home_kernel(first, nh, unroll, place, keep, picked, comp, own, near_a, far_a, near_b, far_b, known, block, *refs):
    if first:
        r_in, r, s, answer, part, known_out, load, resp = refs
    else:
        r_in, s_in, r, s, answer, part, known_out, load, resp = refs
    load[...] = jnp.zeros_like(load)
    ncase, width = r.shape[2:]
    at = 0
    for piece in (near_a, far_a, near_b, far_b):
        resp[at : at + piece.shape[0]] = piece[...]
        at += piece.shape[0]
    each = own.shape[0] // 2 + 1
    sums = tree([piece[i + each - 1] for piece in (near_b, far_b) for i in range(0, piece.shape[0], each)])
    gamma, alpha, beta = steps(first, sums, known[...])
    lane = lax.broadcasted_iota(jnp.int32, (ncase, width), 1)
    known_out[...] = jnp.where(lane == 0, gamma, jnp.where(lane == 1, alpha, beta))
    alpha = jnp.broadcast_to(alpha, (ncase, width))
    beta = jnp.broadcast_to(beta, (ncase, width))
    zero = jnp.zeros((ncase, width), jnp.float32)

    def pick(p, carry):
        part[p] = resp[pl.ds(picked[p], nh)]
        return carry

    lax.fori_loop(0, part.shape[0], pick, 0, unroll=8)

    def body(row, sums):
        gamma, energy = sums
        near, far, on = place[0, row], place[1, row], keep[row]
        c = comp[row]
        for h in range(nh):
            residual = r_in[row, h]
            image = on * (own[near + h] + resp[far + h] + c[h : h + 1] * residual)
            if not first:
                image = image + beta * s_in[row, h]
            residual = residual - alpha * image
            r[row, h], s[row, h] = residual, image
            load[near + h] += residual
            square = residual * residual
            gamma = gamma + square
            energy = energy + c[h : h + 1] * square
        return gamma, energy

    gamma, energy = lax.fori_loop(0, r.shape[0], body, (zero, zero), unroll=unroll)
    respond(block, load, gamma, energy, answer)


def on_device(rhs, compliance, plate_owner, found_owner, slot_pairs, active, inverse):
    nsub = lax.axis_size("sub")
    nbody = lax.axis_size("body")
    side = lax.axis_index("body")
    me = lax.axis_index("sub")
    ncase, npatch, gap = rhs.shape
    block = inverse[0, 0]
    nslot = block.shape[0] // gap
    nh = gap // LANES
    per = nslot * nh + 1
    room = max(2, 2 * npatch // nsub)
    nrow = nsub * room
    lines = -(-room * nh // SUBLANES)
    deep = -(-room // SUBLANES)
    tiles = room * nh + lines + deep
    nz = nsub // 4
    half = nslot // 2 * nh
    unroll = 4

    def exchange(message):
        return lax.all_to_all(message, "sub", split_axis=0, concat_axis=0, tiled=True)

    def swap(value, far):
        return lax.ppermute(value, "sub", [(i, i ^ far) for i in range(nsub)])

    def sibling(value):
        return lax.ppermute(value, "body", [(i, nbody - 1 - i) for i in range(nbody)])

    keep = active.astype(jnp.float32)
    owners = jnp.stack([plate_owner[:, 0], found_owner[:, 0]])
    slots = slot_pairs.T
    owner, other = jnp.where(side == 0, owners, owners[::-1])
    slot, other_slot = jnp.where(side == 0, slots, slots[::-1])
    index = jnp.arange(npatch, dtype=jnp.int32)
    earlier = (owner[None, :] == owner[:, None]) & (index[None, :] < index[:, None])
    rank = jnp.sum(earlier.astype(jnp.int32), axis=1)
    row = owner * room + rank
    place = owner * tiles + rank * nh

    def found(away):
        x_bit, y_bit, z_part = away & 1, (away >> 1) & 1, away >> 2
        found_a = ((y_bit * 2 + x_bit) * nz + z_part) * half + other_slot * nh
        found_b = ((x_bit * 2 + y_bit) * nz + z_part) * (half + 1) + (other_slot - nslot // 2) * nh
        return jnp.where(other_slot < nslot // 2, found_a, nsub * half + found_b)

    facts = jnp.stack([slot * nh, found(owner ^ other)], axis=1).astype(jnp.float32)
    facts = jnp.concatenate([facts, keep[:, None]], axis=1)
    facts = jnp.concatenate([compliance, jnp.pad(facts, ((0, 0), (0, LANES - 3)))], axis=1)
    placed = (row[None, :] == jnp.arange(nrow, dtype=jnp.int32)[:, None]).astype(jnp.float32)
    facts = jnp.dot(placed, facts, precision=lax.Precision.HIGHEST).reshape(nsub, room, gap + LANES)
    lined = facts[:, :, :gap].reshape(nsub, room * nh, LANES)
    lined = jnp.pad(lined, ((0, 0), (0, lines * SUBLANES - room * nh), (0, 0)))
    named = jnp.pad(facts[:, :, gap:], ((0, 0), (0, deep * SUBLANES - room), (0, 0)))
    table = jnp.concatenate([lined, named], axis=1).reshape(nsub, lines + deep, SUBLANES, LANES)
    start = keep[None, :, None] * rhs
    by_patch = jnp.transpose(start.reshape(ncase, npatch, nh, LANES), (1, 2, 0, 3))

    message = call(
        functools.partial(pack_kernel, nh, tiles),
        f32(nsub * tiles, ncase, LANES),
        [SMEM, VMEM, VMEM],
        place,
        by_patch,
        table,
    )
    message = exchange(message.reshape(nsub, tiles, ncase, LANES))
    told = message[:, room * nh :].reshape(nsub, (lines + deep) * SUBLANES, LANES)
    comp = told[:, : room * nh].reshape(nrow, nh, LANES)
    named = told[:, lines * SUBLANES : lines * SUBLANES + room, :3].reshape(nrow, 3).T
    home = named[:2].astype(jnp.int32)
    on = named[2]

    field = f32(nrow, nh, ncase, LANES)
    answer = f32(per, ncase, LANES)
    load = pltpu.VMEM((nslot * nh, ncase, LANES), jnp.float32)
    spread = pltpu.VMEM((nsub * per, ncase, LANES), jnp.float32)
    home_r, own = call(
        functools.partial(start_kernel, nh, room, tiles),
        (field, answer),
        [SMEM, VMEM, VMEM, HBM],
        home,
        comp,
        message.reshape(nsub * tiles, ncase, LANES),
        block,
        scratch=[load, pltpu.VMEM(block.shape, block.dtype), pltpu.SemaphoreType.DMA((nslot,))],
    )
    known = jnp.zeros((ncase, LANES), jnp.float32)
    state = [home_r]
    picked = found(me ^ other).astype(jnp.int32)
    r, d, x, s = start, None, None, None
    for step in range(ITERS - 1):
        far = sibling(own)
        far = jnp.concatenate([far[: per - 1], own[per - 1 :] + far[per - 1 :]])
        parts = [far] + [swap(far, 4 * z) for z in range(1, nz)]
        a = jnp.concatenate([part[:half] for part in parts])
        b = jnp.concatenate([part[half:] for part in parts])
        far_a, far_b = swap(a, 1), swap(b, 2)
        a, b = jnp.concatenate([a, far_a]), jnp.concatenate([b, far_b])
        far_a, far_b = swap(a, 2), swap(b, 1)
        *state, own, part, known = call(
            functools.partial(home_kernel, step == 0, nh, unroll),
            (field,) * 2 + (answer, f32(npatch, nh, ncase, LANES), f32(ncase, LANES)),
            [SMEM] * 3 + [VMEM] * (8 + len(state)),
            home,
            on,
            picked,
            comp,
            own,
            a,
            far_a,
            b,
            far_b,
            known,
            block,
            *state,
            scratch=[load, spread],
        )
        image = jnp.transpose(part + sibling(part), (2, 0, 1, 3)).reshape(ncase, npatch, gap)
        image = keep[None, :, None] * (image + compliance[None] * r)
        alpha, beta = known[:, 1].reshape(ncase, 1, 1), known[:, 2].reshape(ncase, 1, 1)
        if step == 0:
            d, s = r, image
            x = alpha * d
        else:
            d, s = r + beta * d, image + beta * s
            x = x + alpha * d
        r = r - alpha * s
    sums = own[per - 1]
    sums = sums + sibling(sums)
    sums = tree([sums] + [swap(sums, i) for i in range(1, 4)])
    sums = tree([sums] + [swap(sums, 4 * z) for z in range(1, nz)])
    _, alpha, beta = steps(False, sums, known)
    return x + alpha[:, :, None] * (r + beta[:, :, None] * d)


def solution(mesh):
    in_specs = (
        P(None, "sub", None),
        P("sub", None),
        P("sub", None),
        P("sub", None),
        P("sub", None),
        P("sub"),
        P("body", "sub", None, None),
    )
    out_specs = P(None, "sub", None)
    return jax.shard_map(
        on_device, mesh=mesh, in_specs=in_specs, out_specs=out_specs, check_vma=False
    )
```

```python
import functools

import jax
import jax.numpy as jnp
from jax import lax
from jax.experimental import pallas as pl
from jax.experimental.pallas import tpu as pltpu
from jax.sharding import PartitionSpec as P

ITERS = 4
LANES = 128
SUBLANES = 8
VMEM = pl.BlockSpec(memory_space=pltpu.VMEM)
SMEM = pl.BlockSpec(memory_space=pltpu.SMEM)
HBM = pl.BlockSpec(memory_space=pltpu.HBM)
PARAMS = pltpu.CompilerParams(vmem_limit_bytes=20 * 1024 * 1024)


def f32(*shape):
    return jax.ShapeDtypeStruct(shape, jnp.float32)


def call(kernel, out_shape, specs, *operands, scratch=()):
    several = isinstance(out_shape, (tuple, list))
    return pl.pallas_call(
        kernel,
        out_shape=tuple(out_shape) if several else out_shape,
        in_specs=specs,
        out_specs=(VMEM,) * len(out_shape) if several else VMEM,
        scratch_shapes=list(scratch),
        compiler_params=PARAMS,
    )(*operands)


def per_case(value):
    return jnp.sum(value, axis=1, keepdims=True)


def respond(block, load, gamma, energy, answer, copies=()):
    ntile, ncase, width = load.shape
    each = 2
    total = jnp.zeros((2 * ncase, ntile * width), jnp.float32)
    for j in range(ntile // each):
        value = jnp.concatenate([load[j * each + i] for i in range(each)], axis=1)
        high = value.astype(jnp.bfloat16)
        low = (value - high.astype(jnp.float32)).astype(jnp.bfloat16)
        if copies:
            copies[j].wait()
        total = total + jnp.dot(
            jnp.concatenate([high, low], axis=0),
            block[j * each * width : (j + 1) * each * width, :],
            preferred_element_type=jnp.float32,
        )
    total = total[:ncase] + total[ncase:]
    work = 0.5 * energy
    for i in range(ntile):
        tile = total[:, i * width : (i + 1) * width]
        answer[i] = tile
        work = work + load[i] * tile
    lane = lax.broadcasted_iota(jnp.int32, work.shape, 1)
    sums = jnp.where(lane == 0, per_case(0.5 * gamma), 0.0)
    answer[ntile] = jnp.where(lane == 1, per_case(work), sums)


def found(away, slot, nh, nz, nslot):
    half = nslot // 2 * nh
    x_bit, y_bit, z_part = away & 1, (away >> 1) & 1, away >> 2
    found_a = ((y_bit * 2 + x_bit) * nz + z_part) * half + slot * nh
    found_b = ((x_bit * 2 + y_bit) * nz + z_part) * (half + 1) + (slot - nslot // 2) * nh
    return jnp.where(slot < nslot // 2, found_a, 4 * nz * half + found_b)


def pack_kernel(nh, nslot, room, tiles, lines, plate, foundation, slots, active, field, comp, picked, *refs):
    *messages, whole, count = refs
    nsub = len(messages)
    nz = nsub // 4
    side, me = lax.axis_index("body"), lax.axis_index("sub")
    whole[...] = jnp.zeros_like(whole)
    lane = lax.broadcasted_iota(jnp.int32, (1, LANES), 1)

    def clear(i, carry):
        count[i] = 0
        return carry

    lax.fori_loop(0, nsub, clear, 0)

    def body(p, carry):
        owners, places = (plate[p], foundation[p]), (slots[2 * p], slots[2 * p + 1])
        owner, other = (jnp.where(side == 0, owners[i], owners[1 - i]) for i in range(2))
        slot, other_slot = (jnp.where(side == 0, places[i], places[1 - i]) for i in range(2))
        rank = count[owner]
        count[owner] = rank + 1
        on = active[p].astype(jnp.float32)
        base = (owner ^ me) * tiles
        whole[pl.ds(base + rank * nh, nh)] = on * field[p]
        base = base + room * nh
        line = rank * nh
        for h in range(nh):
            whole[base + (line + h) // SUBLANES, pl.ds((line + h) % SUBLANES, 1), :] = comp[p, h : h + 1, :]
        base = base + lines
        far = found(owner ^ other, other_slot, nh, nz, nslot).astype(jnp.float32)
        near = (slot * nh).astype(jnp.float32)
        fact = jnp.where(lane == 0, near, jnp.where(lane == 1, far, jnp.where(lane == 2, on, 0.0)))
        whole[base + rank // SUBLANES, pl.ds(rank % SUBLANES, 1), :] = fact
        picked[p] = found(me ^ other, other_slot, nh, nz, nslot)
        return carry

    lax.fori_loop(0, field.shape[0], body, 0)
    for i, message in enumerate(messages):
        message[...] = whole[i * tiles : (i + 1) * tiles]


def start_kernel(nh, room, lines, place, *refs):
    *messages, block, r_out, comp, answer, held, load, sems = refs
    pieces = sems.shape[0]
    size = block.shape[0] // pieces
    copies = []
    for j in range(pieces):
        rows = pl.ds(j * size, size)
        copies.append(pltpu.make_async_copy(block.at[rows], held.at[rows], sems.at[j]))
        copies[-1].start()
    load[...] = jnp.zeros_like(load)
    gamma = energy = jnp.zeros(r_out.shape[2:], jnp.float32)
    for i, message in enumerate(messages):
        comp[i * lines : (i + 1) * lines] = message[room * nh : room * nh + lines]
        for j in range(room):
            row = i * room + j
            r = message[j * nh : (j + 1) * nh]
            r_out[row] = r
            load[pl.ds(place[0, row], nh)] += r
            for h in range(nh):
                line, sub = divmod(j * nh + h, SUBLANES)
                square = r[h] * r[h]
                gamma = gamma + square
                energy = energy + message[room * nh + line, sub : sub + 1, :] * square
    respond(held, load, gamma, energy, answer, copies)


def tree(values):
    while len(values) > 1:
        values = [a + b for a, b in zip(values[::2], values[1::2])]
    return values[0]


def steps(first, sums, known):
    gamma, delta = sums[:, 0:1], sums[:, 1:2]
    if first:
        return gamma, gamma / delta, jnp.zeros_like(gamma)
    beta = gamma / known[:, 0:1]
    return gamma, gamma / (delta - beta * gamma / known[:, 1:2]), beta


def home_kernel(first, nh, room, lines, place, keep, picked, comp, own, near_a, far_a, near_b, far_b, known, block, *refs):
    if first:
        r_in, r, s, answer, part, known_out, load, resp = refs
    else:
        r_in, s_in, r, s, answer, part, known_out, load, resp = refs
    load[...] = jnp.zeros_like(load)
    ncase, width = r.shape[2:]
    at = 0
    for piece in (near_a, far_a, near_b, far_b):
        resp[at : at + piece.shape[0]] = piece[...]
        at += piece.shape[0]
    each = own.shape[0] // 2 + 1
    sums = tree([piece[i + each - 1] for piece in (near_b, far_b) for i in range(0, piece.shape[0], each)])
    gamma, alpha, beta = steps(first, sums, known[...])
    lane = lax.broadcasted_iota(jnp.int32, (ncase, width), 1)
    known_out[...] = jnp.where(lane == 0, gamma, jnp.where(lane == 1, alpha, beta))
    alpha = jnp.broadcast_to(alpha, (ncase, width))
    beta = jnp.broadcast_to(beta, (ncase, width))
    zero = jnp.zeros((ncase, width), jnp.float32)

    def pick(p, carry):
        part[p] = resp[pl.ds(picked[p], nh)]
        return carry

    lax.fori_loop(0, part.shape[0], pick, 0, unroll=8)

    def pair(i, sums):
        gamma, energy = sums
        for j in range(room):
            row = i * room + j
            near, far, on = place[0, row], place[1, row], keep[row]
            for h in range(nh):
                line, sub = divmod(j * nh + h, SUBLANES)
                c = comp[i * lines + line, sub : sub + 1, :]
                residual = r_in[row, h]
                image = on * (own[near + h] + resp[far + h] + c * residual)
                if not first:
                    image = image + beta * s_in[row, h]
                residual = residual - alpha * image
                r[row, h], s[row, h] = residual, image
                load[near + h] += residual
                square = residual * residual
                gamma = gamma + square
                energy = energy + c * square
        return gamma, energy

    gamma, energy = lax.fori_loop(0, r.shape[0] // room, pair, (zero, zero))
    respond(block, load, gamma, energy, answer)


def on_device(rhs, compliance, plate_owner, found_owner, slot_pairs, active, inverse):
    nsub = lax.axis_size("sub")
    nbody = lax.axis_size("body")
    ncase, npatch, gap = rhs.shape
    block = inverse[0, 0]
    nslot = block.shape[0] // gap
    nh = gap // LANES
    per = nslot * nh + 1
    room = max(2, 2 * npatch // nsub)
    nrow = nsub * room
    lines = -(-room * nh // SUBLANES)
    deep = -(-room // SUBLANES)
    tiles = room * nh + lines + deep
    nz = nsub // 4
    half = nslot // 2 * nh

    def exchange(message):
        return lax.all_to_all(message, "sub", split_axis=0, concat_axis=0, tiled=True)

    def swap(value, far):
        return lax.ppermute(value, "sub", [(i, i ^ far) for i in range(nsub)])

    def sibling(value):
        return lax.ppermute(value, "body", [(i, nbody - 1 - i) for i in range(nbody)])

    keep = active.astype(jnp.float32)
    start = keep[None, :, None] * rhs
    by_patch = jnp.transpose(rhs.reshape(ncase, npatch, nh, LANES), (1, 2, 0, 3))
    picked, *messages = pl.pallas_call(
        functools.partial(pack_kernel, nh, nslot, room, tiles, lines),
        out_shape=(jax.ShapeDtypeStruct((npatch,), jnp.int32),) + (f32(tiles, ncase, LANES),) * nsub,
        in_specs=[SMEM] * 4 + [VMEM] * 2,
        out_specs=(SMEM,) + (VMEM,) * nsub,
        scratch_shapes=[pltpu.VMEM((nsub * tiles, ncase, LANES), jnp.float32), pltpu.SMEM((nsub,), jnp.int32)],
        compiler_params=PARAMS,
    )(
        plate_owner.reshape(npatch),
        found_owner.reshape(npatch),
        slot_pairs.reshape(2 * npatch),
        active,
        by_patch,
        compliance.reshape(npatch, nh, LANES),
    )
    sent = [swap(messages[i], i) for i in range(nsub - 1, 0, -1)]
    messages = messages[:1] + sent[::-1]
    facts = jnp.stack([message[room * nh + lines :] for message in messages])
    facts = facts.reshape(nsub, deep * SUBLANES, LANES)[:, :room, :3].reshape(nrow, 3).T
    home = facts[:2].astype(jnp.int32)
    on = facts[2]

    field = f32(nrow, nh, ncase, LANES)
    answer = f32(per, ncase, LANES)
    load = pltpu.VMEM((nslot * nh, ncase, LANES), jnp.float32)
    spread = pltpu.VMEM((nsub * per, ncase, LANES), jnp.float32)
    home_r, comp, own, block = call(
        functools.partial(start_kernel, nh, room, lines),
        (field, f32(nsub * lines, ncase, LANES), answer, jax.ShapeDtypeStruct(block.shape, block.dtype)),
        [SMEM] + [VMEM] * nsub + [HBM],
        home,
        *messages,
        pltpu.with_memory_space_constraint(block, pltpu.HBM),
        scratch=[load, pltpu.SemaphoreType.DMA((nslot,))],
    )
    known = jnp.zeros((ncase, LANES), jnp.float32)
    state = [home_r]
    r, d, x, s = start, None, None, None
    for step in range(ITERS - 1):
        far = sibling(own)
        far = jnp.concatenate([far[: per - 1], own[per - 1 :] + far[per - 1 :]])
        parts = [far] + [swap(far, 4 * z) for z in range(1, nz)]
        a = jnp.concatenate([part[:half] for part in parts])
        b = jnp.concatenate([part[half:] for part in parts])
        far_a, far_b = swap(a, 1), swap(b, 2)
        a, b = jnp.concatenate([a, far_a]), jnp.concatenate([b, far_b])
        far_a, far_b = swap(a, 2), swap(b, 1)
        *state, own, part, known = call(
            functools.partial(home_kernel, step == 0, nh, room, lines),
            (field,) * 2 + (answer, f32(npatch, nh, ncase, LANES), f32(ncase, LANES)),
            [SMEM] * 3 + [VMEM] * (8 + len(state)),
            home,
            on,
            picked,
            comp,
            own,
            a,
            far_a,
            b,
            far_b,
            known,
            block,
            *state,
            scratch=[load, spread],
        )
        image = jnp.transpose(part + sibling(part), (2, 0, 1, 3)).reshape(ncase, npatch, gap)
        image = keep[None, :, None] * (image + compliance[None] * r)
        alpha, beta = known[:, 1].reshape(ncase, 1, 1), known[:, 2].reshape(ncase, 1, 1)
        if step == 0:
            d, s = r, image
            x = alpha * d
        else:
            d, s = r + beta * d, image + beta * s
            x = x + alpha * d
        r = r - alpha * s
    sums = own[per - 1]
    sums = sums + sibling(sums)
    sums = jnp.sum(exchange(jnp.broadcast_to(sums[None], (nsub, ncase, LANES))), axis=0)
    _, alpha, beta = steps(False, sums, known)
    return x + alpha[:, :, None] * (r + beta[:, :, None] * d)


def solution(mesh):
    in_specs = (
        P(None, "sub", None),
        P("sub", None),
        P("sub", None),
        P("sub", None),
        P("sub", None),
        P("sub"),
        P("body", "sub", None, None),
    )
    out_specs = P(None, "sub", None)
    return jax.shard_map(
        on_device, mesh=mesh, in_specs=in_specs, out_specs=out_specs, check_vma=False
    )
```

```python
import functools

import jax
import jax.numpy as jnp
from jax import lax
from jax.experimental import pallas as pl
from jax.experimental.pallas import tpu as pltpu
from jax.sharding import PartitionSpec as P

ITERS = 4
LANES = 128
SUBLANES = 8
VMEM = pl.BlockSpec(memory_space=pltpu.VMEM)
SMEM = pl.BlockSpec(memory_space=pltpu.SMEM)
HBM = pl.BlockSpec(memory_space=pltpu.HBM)
PARAMS = pltpu.CompilerParams(vmem_limit_bytes=20 * 1024 * 1024)


def f32(*shape):
    return jax.ShapeDtypeStruct(shape, jnp.float32)


def call(kernel, out_shape, specs, *operands, scratch=()):
    several = isinstance(out_shape, (tuple, list))
    return pl.pallas_call(
        kernel,
        out_shape=tuple(out_shape) if several else out_shape,
        in_specs=specs,
        out_specs=(VMEM,) * len(out_shape) if several else VMEM,
        scratch_shapes=list(scratch),
        compiler_params=PARAMS,
    )(*operands)


def per_case(value):
    return jnp.sum(value, axis=1, keepdims=True)


def respond(block, load, gamma, energy, answer, copies=()):
    ntile, ncase, width = load.shape
    each = 2
    total = jnp.zeros((2 * ncase, ntile * width), jnp.float32)
    for j in range(ntile // each):
        value = jnp.concatenate([load[j * each + i] for i in range(each)], axis=1)
        high = value.astype(jnp.bfloat16)
        low = (value - high.astype(jnp.float32)).astype(jnp.bfloat16)
        if copies:
            copies[j].wait()
        total = total + jnp.dot(
            jnp.concatenate([high, low], axis=0),
            block[j * each * width : (j + 1) * each * width, :],
            preferred_element_type=jnp.float32,
        )
    total = total[:ncase] + total[ncase:]
    work = 0.5 * energy
    for i in range(ntile):
        tile = total[:, i * width : (i + 1) * width]
        answer[i] = tile
        work = work + load[i] * tile
    lane = lax.broadcasted_iota(jnp.int32, work.shape, 1)
    sums = jnp.where(lane == 0, per_case(0.5 * gamma), 0.0)
    answer[ntile] = jnp.where(lane == 1, per_case(work), sums)


def pack_kernel(nh, tiles, place, field, table, message):
    ndest = message.shape[0] // tiles
    extra = table.shape[1]
    message[...] = jnp.zeros_like(message)

    def body(p, carry):
        message[pl.ds(place[p], nh)] = field[p]
        return carry

    lax.fori_loop(0, field.shape[0], body, 0, unroll=4)
    for i in range(ndest):
        message[(i + 1) * tiles - extra : (i + 1) * tiles] = table[i]


def start_kernel(nh, room, tiles, lines, place, message, block, r_out, comp, answer, held, load, sems):
    pieces = sems.shape[0]
    size = block.shape[0] // pieces
    copies = []
    for j in range(pieces):
        rows = pl.ds(j * size, size)
        copies.append(pltpu.make_async_copy(block.at[rows], held.at[rows], sems.at[j]))
        copies[-1].start()
    load[...] = jnp.zeros_like(load)
    zero = jnp.zeros(r_out.shape[2:], jnp.float32)

    def pair(i, sums):
        gamma, energy = sums
        comp[pl.ds(i * lines, lines)] = message[pl.ds(i * tiles + room * nh, lines)]
        for j in range(room):
            row = i * room + j
            r = message[pl.ds(i * tiles + j * nh, nh)]
            r_out[row] = r
            load[pl.ds(place[0, row], nh)] += r
            for h in range(nh):
                line, sub = divmod(j * nh + h, SUBLANES)
                c = message[i * tiles + room * nh + line, sub : sub + 1, :]
                square = r[h] * r[h]
                gamma = gamma + square
                energy = energy + c * square
        return gamma, energy

    gamma, energy = lax.fori_loop(0, r_out.shape[0] // room, pair, (zero, zero))
    respond(held, load, gamma, energy, answer, copies)


def tree(values):
    while len(values) > 1:
        values = [a + b for a, b in zip(values[::2], values[1::2])]
    return values[0]


def steps(first, sums, known):
    gamma, delta = sums[:, 0:1], sums[:, 1:2]
    if first:
        return gamma, gamma / delta, jnp.zeros_like(gamma)
    beta = gamma / known[:, 0:1]
    return gamma, gamma / (delta - beta * gamma / known[:, 1:2]), beta


def home_kernel(first, last, nh, room, lines, place, keep, picked, comp, own, near_a, far_a, near_b, far_b, known, block, *refs):
    r_in, *refs = refs
    if not first:
        s_in, *refs = refs
    if not last:
        r, s, *refs = refs
    answer, part, known_out, load, resp = refs
    load[...] = jnp.zeros_like(load)
    nrow, _, ncase, width = r_in.shape
    at = 0
    for piece in (near_a, far_a, near_b, far_b):
        resp[at : at + piece.shape[0]] = piece[...]
        at += piece.shape[0]
    each = own.shape[0] // 2 + 1
    sums = tree([piece[i + each - 1] for piece in (near_b, far_b) for i in range(0, piece.shape[0], each)])
    gamma, alpha, beta = steps(first, sums, known[...])
    lane = lax.broadcasted_iota(jnp.int32, (ncase, width), 1)
    known_out[...] = jnp.where(lane == 0, gamma, jnp.where(lane == 1, alpha, beta))
    alpha = jnp.broadcast_to(alpha, (ncase, width))
    beta = jnp.broadcast_to(beta, (ncase, width))
    zero = jnp.zeros((ncase, width), jnp.float32)

    def pick(p, carry):
        part[p] = resp[pl.ds(picked[p], nh)]
        return carry

    lax.fori_loop(0, part.shape[0], pick, 0, unroll=8)

    def pair(i, sums):
        gamma, energy = sums
        for j in range(room):
            row = i * room + j
            near, far, on = place[0, row], place[1, row], keep[row]
            for h in range(nh):
                line, sub = divmod(j * nh + h, SUBLANES)
                c = comp[i * lines + line, sub : sub + 1, :]
                residual = r_in[row, h]
                image = on * (own[near + h] + resp[far + h] + c * residual)
                if not first:
                    image = image + beta * s_in[row, h]
                residual = residual - alpha * image
                if not last:
                    r[row, h], s[row, h] = residual, image
                load[near + h] += residual
                square = residual * residual
                gamma = gamma + square
                energy = energy + c * square
        return gamma, energy

    gamma, energy = lax.fori_loop(0, nrow // room, pair, (zero, zero))
    respond(block, load, gamma, energy, answer)


def on_device(rhs, compliance, plate_owner, found_owner, slot_pairs, active, inverse):
    nsub = lax.axis_size("sub")
    nbody = lax.axis_size("body")
    side = lax.axis_index("body")
    me = lax.axis_index("sub")
    ncase, npatch, gap = rhs.shape
    block = inverse[0, 0]
    nslot = block.shape[0] // gap
    nh = gap // LANES
    per = nslot * nh + 1
    room = max(2, 2 * npatch // nsub)
    nrow = nsub * room
    lines = -(-room * nh // SUBLANES)
    deep = -(-room // SUBLANES)
    tiles = room * nh + lines + deep
    nz = nsub // 4
    half = nslot // 2 * nh

    def exchange(message):
        return lax.all_to_all(message, "sub", split_axis=0, concat_axis=0, tiled=True)

    def swap(value, far):
        return lax.ppermute(value, "sub", [(i, i ^ far) for i in range(nsub)])

    def sibling(value):
        return lax.ppermute(value, "body", [(i, nbody - 1 - i) for i in range(nbody)])

    keep = active.astype(jnp.float32)
    plate, foundation = plate_owner[:, 0], found_owner[:, 0]
    owner, other = jnp.where(side == 0, plate, foundation), jnp.where(side == 0, foundation, plate)
    slot, other_slot = (jnp.where(side == i, slot_pairs[:, 0], slot_pairs[:, 1]) for i in range(2))
    index = jnp.arange(npatch, dtype=jnp.int32)
    earlier = (owner[None, :] == owner[:, None]) & (index[None, :] < index[:, None])
    rank = jnp.sum(earlier.astype(jnp.int32), axis=1)
    row = owner * room + rank
    place = owner * tiles + rank * nh

    def found(away):
        x_bit, y_bit, z_part = away & 1, (away >> 1) & 1, away >> 2
        found_a = ((y_bit * 2 + x_bit) * nz + z_part) * half + other_slot * nh
        found_b = ((x_bit * 2 + y_bit) * nz + z_part) * (half + 1) + (other_slot - nslot // 2) * nh
        return jnp.where(other_slot < nslot // 2, found_a, nsub * half + found_b)

    facts = jnp.stack([slot * nh, found(owner ^ other)], axis=1).astype(jnp.float32)
    facts = jnp.concatenate([facts, keep[:, None]], axis=1)
    facts = jnp.concatenate([compliance, jnp.pad(facts, ((0, 0), (0, LANES - 3)))], axis=1)
    placed = (row[None, :] == jnp.arange(nrow, dtype=jnp.int32)[:, None]).astype(jnp.float32)
    facts = jnp.dot(placed, facts, precision=lax.Precision.HIGHEST).reshape(nsub, room, gap + LANES)
    lined = facts[:, :, :gap].reshape(nsub, room * nh, LANES)
    lined = jnp.pad(lined, ((0, 0), (0, lines * SUBLANES - room * nh), (0, 0)))
    named = jnp.pad(facts[:, :, gap:], ((0, 0), (0, deep * SUBLANES - room), (0, 0)))
    table = jnp.concatenate([lined, named], axis=1).reshape(nsub, lines + deep, SUBLANES, LANES)
    start = keep[None, :, None] * rhs
    by_patch = jnp.transpose(start.reshape(ncase, npatch, nh, LANES), (1, 2, 0, 3))

    message = call(
        functools.partial(pack_kernel, nh, tiles),
        f32(nsub * tiles, ncase, LANES),
        [SMEM, VMEM, VMEM],
        place,
        by_patch,
        table,
    )
    message = exchange(message.reshape(nsub, tiles, ncase, LANES))
    told = message[:, room * nh :].reshape(nsub, (lines + deep) * SUBLANES, LANES)
    named = told[:, lines * SUBLANES : lines * SUBLANES + room, :3].reshape(nrow, 3).T
    home = named[:2].astype(jnp.int32)
    on = named[2]

    field = f32(nrow, nh, ncase, LANES)
    answer = f32(per, ncase, LANES)
    load = pltpu.VMEM((nslot * nh, ncase, LANES), jnp.float32)
    spread = pltpu.VMEM((nsub * per, ncase, LANES), jnp.float32)
    home_r, comp, own, block = call(
        functools.partial(start_kernel, nh, room, tiles, lines),
        (field, f32(nsub * lines, ncase, LANES), answer, jax.ShapeDtypeStruct(block.shape, block.dtype)),
        [SMEM, VMEM, HBM],
        home,
        message.reshape(nsub * tiles, ncase, LANES),
        pltpu.with_memory_space_constraint(block, pltpu.HBM),
        scratch=[load, pltpu.SemaphoreType.DMA((nslot,))],
    )
    known = jnp.zeros((ncase, LANES), jnp.float32)
    state = [home_r]
    picked = found(me ^ other).astype(jnp.int32)
    r, d, x, s = start, None, None, None
    for step in range(ITERS - 1):
        last = step == ITERS - 2
        far = sibling(own)
        far = jnp.concatenate([far[: per - 1], own[per - 1 :] + far[per - 1 :]])
        parts = [far] + [swap(far, 4 * z) for z in range(1, nz)]
        a = jnp.concatenate([part[:half] for part in parts])
        b = jnp.concatenate([part[half:] for part in parts])
        far_a, far_b = swap(a, 1), swap(b, 2)
        a, b = jnp.concatenate([a, far_a]), jnp.concatenate([b, far_b])
        far_a, far_b = swap(a, 2), swap(b, 1)
        *state, own, part, known = call(
            functools.partial(home_kernel, step == 0, last, nh, room, lines),
            (field,) * (0 if last else 2) + (answer, f32(npatch, nh, ncase, LANES), f32(ncase, LANES)),
            [SMEM] * 3 + [VMEM] * (8 + len(state)),
            home,
            on,
            picked,
            comp,
            own,
            a,
            far_a,
            b,
            far_b,
            known,
            block,
            *state,
            scratch=[load, spread],
        )
        image = jnp.transpose(part + sibling(part), (2, 0, 1, 3)).reshape(ncase, npatch, gap)
        image = keep[None, :, None] * (image + compliance[None] * r)
        alpha, beta = known[:, 1].reshape(ncase, 1, 1), known[:, 2].reshape(ncase, 1, 1)
        if step == 0:
            d, s = r, image
            x = alpha * d
        else:
            d, s = r + beta * d, image + beta * s
            x = x + alpha * d
        r = r - alpha * s
        r, d, x, s = lax.optimization_barrier((r, d, x, s))
    sums = own[per - 1]
    sums = sums + sibling(sums)
    sums = tree([sums] + [swap(sums, i) for i in range(1, 4)])
    sums = tree([sums] + [swap(sums, 4 * z) for z in range(1, nz)])
    _, alpha, beta = steps(False, sums, known)
    return x + alpha[:, :, None] * (r + beta[:, :, None] * d)


def solution(mesh):
    in_specs = (
        P(None, "sub", None),
        P("sub", None),
        P("sub", None),
        P("sub", None),
        P("sub", None),
        P("sub"),
        P("body", "sub", None, None),
    )
    out_specs = P(None, "sub", None)
    return jax.shard_map(
        on_device, mesh=mesh, in_specs=in_specs, out_specs=out_specs, check_vma=False
    )
```

```python
import functools

import jax
import jax.numpy as jnp
from jax import lax
from jax.experimental import pallas as pl
from jax.experimental.pallas import tpu as pltpu
from jax.sharding import PartitionSpec as P

ITERS = 4
LANES = 128
SUBLANES = 8
VMEM = pl.BlockSpec(memory_space=pltpu.VMEM)
SMEM = pl.BlockSpec(memory_space=pltpu.SMEM)
HBM = pl.BlockSpec(memory_space=pltpu.HBM)
PARAMS = pltpu.CompilerParams(vmem_limit_bytes=16 * 1024 * 1024)


def f32(*shape):
    return jax.ShapeDtypeStruct(shape, jnp.float32)


def call(kernel, out_shape, specs, *operands, scratch=()):
    several = isinstance(out_shape, (tuple, list))
    return pl.pallas_call(
        kernel,
        out_shape=tuple(out_shape) if several else out_shape,
        in_specs=specs,
        out_specs=(VMEM,) * len(out_shape) if several else VMEM,
        scratch_shapes=list(scratch),
        compiler_params=PARAMS,
    )(*operands)


def per_case(value):
    return jnp.sum(value, axis=1, keepdims=True)


def respond(block, load, gamma, energy, answer, copies=()):
    ntile, ncase, width = load.shape
    each = 2
    total = jnp.zeros((2 * ncase, ntile * width), jnp.float32)
    for j in range(ntile // each):
        value = jnp.concatenate([load[j * each + i] for i in range(each)], axis=1)
        high = value.astype(jnp.bfloat16)
        low = (value - high.astype(jnp.float32)).astype(jnp.bfloat16)
        if copies:
            copies[j].wait()
        total = total + jnp.dot(
            jnp.concatenate([high, low], axis=0),
            block[j * each * width : (j + 1) * each * width, :],
            preferred_element_type=jnp.float32,
        )
    total = total[:ncase] + total[ncase:]
    work = 0.5 * energy
    for i in range(ntile):
        tile = total[:, i * width : (i + 1) * width]
        answer[i] = tile
        work = work + load[i] * tile
    lane = lax.broadcasted_iota(jnp.int32, work.shape, 1)
    sums = jnp.where(lane == 0, per_case(0.5 * gamma), 0.0)
    answer[ntile] = jnp.where(lane == 1, per_case(work), sums)


def pack_kernel(nh, tiles, place, field, table, message):
    ndest = message.shape[0] // tiles
    extra = table.shape[1]
    message[...] = jnp.zeros_like(message)

    def body(p, carry):
        message[pl.ds(place[p], nh)] = field[p]
        return carry

    lax.fori_loop(0, field.shape[0], body, 0, unroll=4)
    for i in range(ndest):
        message[(i + 1) * tiles - extra : (i + 1) * tiles] = table[i]


def start_kernel(nh, room, tiles, lines, place, message, block, r_out, comp, answer, held, load, sems):
    pieces = sems.shape[0]
    size = block.shape[0] // pieces
    copies = []
    for j in range(pieces):
        rows = pl.ds(j * size, size)
        copies.append(pltpu.make_async_copy(block.at[rows], held.at[rows], sems.at[j]))
        copies[-1].start()
    load[...] = jnp.zeros_like(load)
    zero = jnp.zeros(r_out.shape[2:], jnp.float32)

    def pair(i, sums):
        gamma, energy = sums
        comp[pl.ds(i * lines, lines)] = message[pl.ds(i * tiles + room * nh, lines)]
        for j in range(room):
            row = i * room + j
            r = message[pl.ds(i * tiles + j * nh, nh)]
            r_out[row] = r
            load[pl.ds(place[row], nh)] += r
            for h in range(nh):
                line, sub = divmod(j * nh + h, SUBLANES)
                c = message[i * tiles + room * nh + line, sub : sub + 1, :]
                square = r[h] * r[h]
                gamma = gamma + square
                energy = energy + c * square
        return gamma, energy

    gamma, energy = lax.fori_loop(0, r_out.shape[0] // room, pair, (zero, zero))
    respond(held, load, gamma, energy, answer, copies)


def tree(values):
    while len(values) > 1:
        values = [a + b for a, b in zip(values[::2], values[1::2])]
    return values[0]


def steps(first, sums, known):
    gamma, delta = sums[:, 0:1], sums[:, 1:2]
    if first:
        return gamma, gamma / delta, jnp.zeros_like(gamma)
    beta = gamma / known[:, 0:1]
    return gamma, gamma / (delta - beta * gamma / known[:, 1:2]), beta


def home_kernel(first, last, nh, room, lines, place, away, keep, picked, comp, own, near_a, far_a, near_b, far_b, known, block, *refs):
    r_in, *refs = refs
    if not first:
        s_in, *refs = refs
    if not last:
        r, s, *refs = refs
    answer, part, known_out, load, resp = refs
    load[...] = jnp.zeros_like(load)
    nrow, _, ncase, width = r_in.shape
    at = 0
    for piece in (near_a, far_a, near_b, far_b):
        resp[at : at + piece.shape[0]] = piece[...]
        at += piece.shape[0]
    each = own.shape[0] // 2 + 1
    sums = tree([piece[i + each - 1] for piece in (near_b, far_b) for i in range(0, piece.shape[0], each)])
    gamma, alpha, beta = steps(first, sums, known[...])
    lane = lax.broadcasted_iota(jnp.int32, (ncase, width), 1)
    known_out[...] = jnp.where(lane == 0, gamma, jnp.where(lane == 1, alpha, beta))
    alpha = jnp.broadcast_to(alpha, (ncase, width))
    beta = jnp.broadcast_to(beta, (ncase, width))
    zero = jnp.zeros((ncase, width), jnp.float32)

    def pick(p, carry):
        part[p] = resp[pl.ds(picked[p], nh)]
        return carry

    lax.fori_loop(0, part.shape[0], pick, 0, unroll=8)

    def pair(i, sums):
        gamma, energy = sums
        for j in range(room):
            row = i * room + j
            near, far, on = place[row], away[row], keep[row]
            for h in range(nh):
                line, sub = divmod(j * nh + h, SUBLANES)
                c = comp[i * lines + line, sub : sub + 1, :]
                residual = r_in[row, h]
                image = on * (own[near + h] + resp[far + h] + c * residual)
                if not first:
                    image = image + beta * s_in[row, h]
                residual = residual - alpha * image
                if not last:
                    r[row, h], s[row, h] = residual, image
                load[near + h] += residual
                square = residual * residual
                gamma = gamma + square
                energy = energy + c * square
        return gamma, energy

    gamma, energy = lax.fori_loop(0, nrow // room, pair, (zero, zero))
    respond(block, load, gamma, energy, answer)


def list_kernel(first, keep, known, comp, mine, theirs, *refs):
    if first:
        r_in, r, d, x, s = refs
    else:
        r_in, d_in, x_in, s_in, r, d, x, s = refs
    npatch, nh, ncase, width = r.shape
    alpha = jnp.broadcast_to(known[:, 1:2], (ncase, width))
    beta = jnp.broadcast_to(known[:, 2:3], (ncase, width))

    def body(p, carry):
        on, row = keep[p], comp[pl.ds(p, 1), :]
        for h in range(nh):
            residual = r_in[p, h]
            c = row[:, h * width : (h + 1) * width]
            image = on * (mine[p, h] + theirs[p, h] + c * residual)
            if first:
                direction, moved = residual, alpha * residual
            else:
                direction = residual + beta * d_in[p, h]
                image = image + beta * s_in[p, h]
                moved = x_in[p, h] + alpha * direction
            r[p, h], d[p, h], x[p, h], s[p, h] = residual - alpha * image, direction, moved, image
        return carry

    lax.fori_loop(0, npatch, body, 0, unroll=4)


def end_kernel(sums, known, r, d, x, out):
    npatch, nh, ncase, width = r.shape
    _, alpha, beta = steps(False, sums[...], known[...])
    alpha = jnp.broadcast_to(alpha, (ncase, width))[None]
    beta = jnp.broadcast_to(beta, (ncase, width))[None]
    for h in range(nh):
        moved = x[:, h] + alpha * (r[:, h] + beta * d[:, h])
        out[:, :, h * width : (h + 1) * width] = jnp.swapaxes(moved, 0, 1)


def on_device(rhs, compliance, plate_owner, found_owner, slot_pairs, active, inverse):
    nsub = lax.axis_size("sub")
    nbody = lax.axis_size("body")
    side = lax.axis_index("body")
    me = lax.axis_index("sub")
    ncase, npatch, gap = rhs.shape
    block = inverse[0, 0]
    nslot = block.shape[0] // gap
    nh = gap // LANES
    per = nslot * nh + 1
    room = max(2, 2 * npatch // nsub)
    nrow = nsub * room
    lines = -(-room * nh // SUBLANES)
    deep = -(-room // SUBLANES)
    tiles = room * nh + lines + deep
    nz = nsub // 4
    half = nslot // 2 * nh

    def exchange(message):
        return lax.all_to_all(message, "sub", split_axis=0, concat_axis=0, tiled=True)

    def swap(value, far):
        return lax.ppermute(value, "sub", [(i, i ^ far) for i in range(nsub)])

    def sibling(value):
        return lax.ppermute(value, "body", [(i, nbody - 1 - i) for i in range(nbody)])

    keep = active.astype(jnp.float32)
    plate, foundation = plate_owner[:, 0], found_owner[:, 0]
    owner, other = jnp.where(side == 0, plate, foundation), jnp.where(side == 0, foundation, plate)
    slot, other_slot = (jnp.where(side == i, slot_pairs[:, 0], slot_pairs[:, 1]) for i in range(2))
    index = jnp.arange(npatch, dtype=jnp.int32)
    earlier = (owner[None, :] == owner[:, None]) & (index[None, :] < index[:, None])
    rank = jnp.sum(earlier.astype(jnp.int32), axis=1)
    row = owner * room + rank
    place = owner * tiles + rank * nh

    def found(away):
        x_bit, y_bit, z_part = away & 1, (away >> 1) & 1, away >> 2
        found_a = ((y_bit * 2 + x_bit) * nz + z_part) * half + other_slot * nh
        found_b = ((x_bit * 2 + y_bit) * nz + z_part) * (half + 1) + (other_slot - nslot // 2) * nh
        return jnp.where(other_slot < nslot // 2, found_a, nsub * half + found_b)

    facts = jnp.stack([slot * nh, found(owner ^ other)], axis=1).astype(jnp.float32)
    facts = jnp.concatenate([facts, keep[:, None]], axis=1)
    facts = jnp.concatenate([compliance, jnp.pad(facts, ((0, 0), (0, LANES - 3)))], axis=1)
    placed = (row[None, :] == jnp.arange(nrow, dtype=jnp.int32)[:, None]).astype(jnp.float32)
    facts = jnp.dot(placed, facts, precision=lax.Precision.HIGHEST).reshape(nsub, room, gap + LANES)
    lined = facts[:, :, :gap].reshape(nsub, room * nh, LANES)
    lined = jnp.pad(lined, ((0, 0), (0, lines * SUBLANES - room * nh), (0, 0)))
    named = jnp.pad(facts[:, :, gap:], ((0, 0), (0, deep * SUBLANES - room), (0, 0)))
    table = jnp.concatenate([lined, named], axis=1).reshape(nsub, lines + deep, SUBLANES, LANES)
    start = (keep[None, :, None] * rhs).reshape(ncase, npatch, nh, LANES)
    start = jnp.transpose(start, (1, 2, 0, 3))
    picked = found(me ^ other).astype(jnp.int32)
    place, picked = lax.optimization_barrier((place, picked))

    message = call(
        functools.partial(pack_kernel, nh, tiles),
        f32(nsub * tiles, ncase, LANES),
        [SMEM, VMEM, VMEM],
        place,
        start,
        table,
    )
    message = exchange(message.reshape(nsub, tiles, ncase, LANES))
    facts = message[:, room * nh + lines :].reshape(nsub, deep * SUBLANES, LANES)[:, :room]
    near, far, on = (facts[:, :, i].reshape(nrow) for i in range(3))
    near, far = near.astype(jnp.int32), far.astype(jnp.int32)
    message, near, far, on = lax.optimization_barrier((message, near, far, on))

    field = f32(nrow, nh, ncase, LANES)
    answer = f32(per, ncase, LANES)
    load = pltpu.VMEM((nslot * nh, ncase, LANES), jnp.float32)
    spread = pltpu.VMEM((nsub * per, ncase, LANES), jnp.float32)
    home_r, comp, own, block = call(
        functools.partial(start_kernel, nh, room, tiles, lines),
        (field, f32(nsub * lines, ncase, LANES), answer, jax.ShapeDtypeStruct(block.shape, block.dtype)),
        [SMEM, VMEM, HBM],
        near,
        message.reshape(nsub * tiles, ncase, LANES),
        pltpu.with_memory_space_constraint(block, pltpu.HBM),
        scratch=[load, pltpu.SemaphoreType.DMA((nslot,))],
    )
    def update(step, lists, known, part):
        return call(
            functools.partial(list_kernel, step == 0),
            (f32(npatch, nh, ncase, LANES),) * 4,
            [SMEM] + [VMEM] * (4 + len(lists)),
            keep,
            known,
            compliance,
            part,
            sibling(part),
            *lists,
        )

    known = jnp.zeros((ncase, LANES), jnp.float32)
    state = [home_r]
    lists = [start]
    for step in range(ITERS - 1):
        last = step == ITERS - 2
        spread_out = sibling(own)
        if step > 0:
            spread_out, part = lax.optimization_barrier((spread_out, part))
            lists = update(step - 1, lists, known, part)
        spread_out = jnp.concatenate([spread_out[: per - 1], own[per - 1 :] + spread_out[per - 1 :]])
        parts = [spread_out] + [swap(spread_out, 4 * z) for z in range(1, nz)]
        a = jnp.concatenate([part[:half] for part in parts])
        b = jnp.concatenate([part[half:] for part in parts])
        far_a, far_b = swap(a, 1), swap(b, 2)
        a, b = jnp.concatenate([a, far_a]), jnp.concatenate([b, far_b])
        if step > 0:
            a, b, lists = lax.optimization_barrier((a, b, lists))
        far_a, far_b = swap(a, 2), swap(b, 1)
        *state, own, part, known = call(
            functools.partial(home_kernel, step == 0, last, nh, room, lines),
            (field,) * (0 if last else 2) + (answer, f32(npatch, nh, ncase, LANES), f32(ncase, LANES)),
            [SMEM] * 4 + [VMEM] * (8 + len(state)),
            near,
            far,
            on,
            picked,
            comp,
            own,
            a,
            far_a,
            b,
            far_b,
            known,
            block,
            *state,
            scratch=[load, spread],
        )
    sums = own[per - 1]
    others = sibling(sums)
    others, part = lax.optimization_barrier((others, part))
    sums = sums + others
    r, d, x, _ = update(ITERS - 2, lists, known, part)
    sums = tree([sums] + [swap(sums, i) for i in range(1, 4)])
    sums = tree([sums] + [swap(sums, 4 * z) for z in range(1, nz)])
    return call(end_kernel, f32(ncase, npatch, gap), [VMEM] * 5, sums, known, r, d, x)


def solution(mesh):
    in_specs = (
        P(None, "sub", None),
        P("sub", None),
        P("sub", None),
        P("sub", None),
        P("sub", None),
        P("sub"),
        P("body", "sub", None, None),
    )
    out_specs = P(None, "sub", None)
    return jax.shard_map(
        on_device, mesh=mesh, in_specs=in_specs, out_specs=out_specs, check_vma=False
    )
```

```python
import functools

import jax
import jax.numpy as jnp
from jax import lax
from jax.experimental import pallas as pl
from jax.experimental.pallas import tpu as pltpu
from jax.sharding import PartitionSpec as P

ITERS = 4
LANES = 128
SUBLANES = 8
VMEM = pl.BlockSpec(memory_space=pltpu.VMEM)
SMEM = pl.BlockSpec(memory_space=pltpu.SMEM)
HBM = pl.BlockSpec(memory_space=pltpu.HBM)
PARAMS = pltpu.CompilerParams(vmem_limit_bytes=16 * 1024 * 1024)


def f32(*shape):
    return jax.ShapeDtypeStruct(shape, jnp.float32)


def call(kernel, out_shape, specs, *operands, scratch=(), cost=None):
    several = isinstance(out_shape, (tuple, list))
    return pl.pallas_call(
        kernel,
        out_shape=tuple(out_shape) if several else out_shape,
        in_specs=specs,
        out_specs=(VMEM,) * len(out_shape) if several else VMEM,
        scratch_shapes=list(scratch),
        compiler_params=PARAMS,
        cost_estimate=cost,
    )(*operands)


def per_case(value):
    return jnp.sum(value, axis=1, keepdims=True)


def respond(block, load, gamma, energy, answer, copies=(), last=False):
    ntile, ncase, width = load.shape
    each = 2
    total = jnp.zeros((2 * ncase, ntile * width), jnp.float32)
    for j in range(ntile // each):
        value = jnp.concatenate([load[j * each + i] for i in range(each)], axis=1)
        high = value.astype(jnp.bfloat16)
        low = (value - high.astype(jnp.float32)).astype(jnp.bfloat16)
        if copies:
            copies[j].wait()
        total = total + jnp.dot(
            jnp.concatenate([high, low], axis=0),
            block[j * each * width : (j + 1) * each * width, :],
            preferred_element_type=jnp.float32,
        )
    total = total[:ncase] + total[ncase:]
    work = 0.5 * energy
    for i in range(ntile):
        tile = total[:, i * width : (i + 1) * width]
        if not last:
            answer[i] = tile
        work = work + load[i] * tile
    lane = lax.broadcasted_iota(jnp.int32, work.shape, 1)
    sums = jnp.where(lane == 0, per_case(0.5 * gamma), 0.0)
    sums = jnp.where(lane == 1, per_case(work), sums)
    if last:
        answer[...] = jnp.broadcast_to(sums[None], answer.shape)
    else:
        answer[ntile] = sums


def pack_kernel(nh, tiles, place, field, table, message):
    ndest = message.shape[0] // tiles
    extra = table.shape[1]
    message[...] = jnp.zeros_like(message)

    def body(p, carry):
        message[pl.ds(place[p], nh)] = field[p]
        return carry

    lax.fori_loop(0, field.shape[0], body, 0, unroll=4)
    for i in range(ndest):
        message[(i + 1) * tiles - extra : (i + 1) * tiles] = table[i]


def start_kernel(nh, room, tiles, lines, place, message, block, r_out, comp, answer, held, load, sems):
    pieces = sems.shape[0]
    size = block.shape[0] // pieces
    copies = []
    for j in range(pieces):
        rows = pl.ds(j * size, size)
        copies.append(pltpu.make_async_copy(block.at[rows], held.at[rows], sems.at[j]))
        copies[-1].start()
    load[...] = jnp.zeros_like(load)
    zero = jnp.zeros(r_out.shape[2:], jnp.float32)

    def pair(i, sums):
        gamma, energy = sums
        comp[pl.ds(i * lines, lines)] = message[pl.ds(i * tiles + room * nh, lines)]
        for j in range(room):
            row = i * room + j
            r = message[pl.ds(i * tiles + j * nh, nh)]
            r_out[row] = r
            load[pl.ds(place[row], nh)] += r
            for h in range(nh):
                line, sub = divmod(j * nh + h, SUBLANES)
                c = message[i * tiles + room * nh + line, sub : sub + 1, :]
                square = r[h] * r[h]
                gamma = gamma + square
                energy = energy + c * square
        return gamma, energy

    gamma, energy = lax.fori_loop(0, r_out.shape[0] // room, pair, (zero, zero))
    respond(held, load, gamma, energy, answer, copies)


def tree(values):
    while len(values) > 1:
        values = [a + b for a, b in zip(values[::2], values[1::2])]
    return values[0]


def steps(first, sums, known):
    gamma, delta = sums[:, 0:1], sums[:, 1:2]
    if first:
        return gamma, gamma / delta, jnp.zeros_like(gamma)
    beta = gamma / known[:, 0:1]
    return gamma, gamma / (delta - beta * gamma / known[:, 1:2]), beta


def home_kernel(first, last, nh, room, lines, place, away, keep, picked, comp, own, near_a, far_a, near_b, far_b, known, block, *refs):
    r_in, *refs = refs
    if not first:
        s_in, *refs = refs
    if not last:
        r, s, *refs = refs
    answer, part, known_out, load, resp = refs
    load[...] = jnp.zeros_like(load)
    nrow, _, ncase, width = r_in.shape
    at = 0
    for piece in (near_a, far_a, near_b, far_b):
        resp[at : at + piece.shape[0]] = piece[...]
        at += piece.shape[0]
    each = own.shape[0] // 2 + 1
    sums = tree([piece[i + each - 1] for piece in (near_b, far_b) for i in range(0, piece.shape[0], each)])
    gamma, alpha, beta = steps(first, sums, known[...])
    lane = lax.broadcasted_iota(jnp.int32, (ncase, width), 1)
    known_out[...] = jnp.where(lane == 0, gamma, jnp.where(lane == 1, alpha, beta))
    alpha = jnp.broadcast_to(alpha, (ncase, width))
    beta = jnp.broadcast_to(beta, (ncase, width))
    zero = jnp.zeros((ncase, width), jnp.float32)

    def pick(p, carry):
        part[p] = resp[pl.ds(picked[p], nh)]
        return carry

    lax.fori_loop(0, part.shape[0], pick, 0, unroll=8)

    def pair(i, sums):
        gamma, energy = sums
        for j in range(room):
            row = i * room + j
            near, far, on = place[row], away[row], keep[row]
            for h in range(nh):
                line, sub = divmod(j * nh + h, SUBLANES)
                c = comp[i * lines + line, sub : sub + 1, :]
                residual = r_in[row, h]
                image = on * (own[near + h] + resp[far + h] + c * residual)
                if not first:
                    image = image + beta * s_in[row, h]
                residual = residual - alpha * image
                if not last:
                    r[row, h], s[row, h] = residual, image
                load[near + h] += residual
                square = residual * residual
                gamma = gamma + square
                energy = energy + c * square
        return gamma, energy

    gamma, energy = lax.fori_loop(0, nrow // room, pair, (zero, zero))
    respond(block, load, gamma, energy, answer, last=last)


def list_kernel(first, keep, known, comp, mine, theirs, *refs):
    if first:
        r_in, r, d, x, s = refs
    else:
        r_in, d_in, x_in, s_in, r, d, x, s = refs
    npatch, nh, ncase, width = r.shape
    alpha = jnp.broadcast_to(known[:, 1:2], (ncase, width))
    beta = jnp.broadcast_to(known[:, 2:3], (ncase, width))

    def body(p, carry):
        on, row = keep[p], comp[pl.ds(p, 1), :]
        for h in range(nh):
            residual = r_in[p, h]
            c = row[:, h * width : (h + 1) * width]
            image = on * (mine[p, h] + theirs[p, h] + c * residual)
            if first:
                direction, moved = residual, alpha * residual
            else:
                direction = residual + beta * d_in[p, h]
                image = image + beta * s_in[p, h]
                moved = x_in[p, h] + alpha * direction
            r[p, h], d[p, h], x[p, h], s[p, h] = residual - alpha * image, direction, moved, image
        return carry

    lax.fori_loop(0, npatch, body, 0, unroll=4)


def end_kernel(keep, sums, known, comp, mine, theirs, r_in, d_in, x_in, s_in, out, moved):
    npatch, nh, ncase, width = r_in.shape
    total = sums[0]
    for i in range(1, sums.shape[0]):
        total = total + sums[i]
    _, alpha, beta = steps(False, total, known[...])
    one, two = jnp.broadcast_to(alpha, (ncase, width)), jnp.broadcast_to(beta, (ncase, width))
    alpha = jnp.broadcast_to(known[:, 1:2], (ncase, width))
    beta = jnp.broadcast_to(known[:, 2:3], (ncase, width))

    def body(p, carry):
        on, row = keep[p], comp[pl.ds(p, 1), :]
        for h in range(nh):
            residual = r_in[p, h]
            c = row[:, h * width : (h + 1) * width]
            image = on * (mine[p, h] + theirs[p, h] + c * residual) + beta * s_in[p, h]
            direction = residual + beta * d_in[p, h]
            residual = residual - alpha * image
            moved[h, p] = x_in[p, h] + alpha * direction + one * (residual + two * direction)
        return carry

    lax.fori_loop(0, npatch, body, 0, unroll=4)
    for h in range(nh):
        out[:, :, h * width : (h + 1) * width] = jnp.swapaxes(moved[h], 0, 1)


def on_device(rhs, compliance, plate_owner, found_owner, slot_pairs, active, inverse):
    nsub = lax.axis_size("sub")
    nbody = lax.axis_size("body")
    side = lax.axis_index("body")
    me = lax.axis_index("sub")
    ncase, npatch, gap = rhs.shape
    block = inverse[0, 0]
    nslot = block.shape[0] // gap
    nh = gap // LANES
    per = nslot * nh + 1
    room = max(2, 2 * npatch // nsub)
    nrow = nsub * room
    lines = -(-room * nh // SUBLANES)
    deep = -(-room // SUBLANES)
    tiles = room * nh + lines + deep
    nz = nsub // 4
    half = nslot // 2 * nh

    def exchange(message):
        return lax.all_to_all(message, "sub", split_axis=0, concat_axis=0, tiled=True)

    def swap(value, far):
        return lax.ppermute(value, "sub", [(i, i ^ far) for i in range(nsub)])

    def sibling(value):
        return lax.ppermute(value, "body", [(i, nbody - 1 - i) for i in range(nbody)])

    keep = active.astype(jnp.float32)
    plate, foundation = plate_owner[:, 0], found_owner[:, 0]
    owner, other = jnp.where(side == 0, plate, foundation), jnp.where(side == 0, foundation, plate)
    slot, other_slot = (jnp.where(side == i, slot_pairs[:, 0], slot_pairs[:, 1]) for i in range(2))
    index = jnp.arange(npatch, dtype=jnp.int32)
    earlier = (owner[None, :] == owner[:, None]) & (index[None, :] < index[:, None])
    rank = jnp.sum(earlier.astype(jnp.int32), axis=1)
    row = owner * room + rank
    place = owner * tiles + rank * nh

    def found(away):
        x_bit, y_bit, z_part = away & 1, (away >> 1) & 1, away >> 2
        found_a = ((y_bit * 2 + x_bit) * nz + z_part) * half + other_slot * nh
        found_b = ((x_bit * 2 + y_bit) * nz + z_part) * (half + 1) + (other_slot - nslot // 2) * nh
        return jnp.where(other_slot < nslot // 2, found_a, nsub * half + found_b)

    facts = jnp.stack([slot * nh, found(owner ^ other)], axis=1).astype(jnp.float32)
    facts = jnp.concatenate([facts, keep[:, None]], axis=1)
    facts = jnp.concatenate([compliance, jnp.pad(facts, ((0, 0), (0, LANES - 3)))], axis=1)
    placed = (row[None, :] == jnp.arange(nrow, dtype=jnp.int32)[:, None]).astype(jnp.float32)
    facts = jnp.dot(placed, facts, precision=lax.Precision.HIGHEST).reshape(nsub, room, gap + LANES)
    lined = facts[:, :, :gap].reshape(nsub, room * nh, LANES)
    lined = jnp.pad(lined, ((0, 0), (0, lines * SUBLANES - room * nh), (0, 0)))
    named = jnp.pad(facts[:, :, gap:], ((0, 0), (0, deep * SUBLANES - room), (0, 0)))
    table = jnp.concatenate([lined, named], axis=1).reshape(nsub, lines + deep, SUBLANES, LANES)
    start = (keep[None, :, None] * rhs).reshape(ncase, npatch, nh, LANES)
    start = jnp.transpose(start, (1, 2, 0, 3))
    picked = found(me ^ other).astype(jnp.int32)
    place, picked = lax.optimization_barrier((place, picked))

    message = call(
        functools.partial(pack_kernel, nh, tiles),
        f32(nsub * tiles, ncase, LANES),
        [SMEM, VMEM, VMEM],
        place,
        start,
        table,
    )
    message = exchange(message.reshape(nsub, tiles, ncase, LANES))
    facts = message[:, room * nh + lines :].reshape(nsub, deep * SUBLANES, LANES)[:, :room]
    near, far, on = (facts[:, :, i].reshape(nrow) for i in range(3))
    near, far = near.astype(jnp.int32), far.astype(jnp.int32)
    message, near, far, on = lax.optimization_barrier((message, near, far, on))

    field = f32(nrow, nh, ncase, LANES)
    answer = f32(per, ncase, LANES)
    load = pltpu.VMEM((nslot * nh, ncase, LANES), jnp.float32)
    spread = pltpu.VMEM((nsub * per, ncase, LANES), jnp.float32)
    home_r, comp, own, block = call(
        functools.partial(start_kernel, nh, room, tiles, lines),
        (field, f32(nsub * lines, ncase, LANES), answer, jax.ShapeDtypeStruct(block.shape, block.dtype)),
        [SMEM, VMEM, HBM],
        near,
        message.reshape(nsub * tiles, ncase, LANES),
        pltpu.with_memory_space_constraint(block, pltpu.HBM),
        scratch=[load, pltpu.SemaphoreType.DMA((nslot,))],
    )
    def update(step, lists, known, part):
        return call(
            functools.partial(list_kernel, step == 0),
            (f32(npatch, nh, ncase, LANES),) * 4,
            [SMEM] + [VMEM] * (4 + len(lists)),
            keep,
            known,
            compliance,
            part,
            sibling(part),
            *lists,
            cost=pl.CostEstimate(flops=16 * rhs.size, bytes_accessed=44 * rhs.size, transcendentals=0),
        )

    known = jnp.zeros((ncase, LANES), jnp.float32)
    state = [home_r]
    lists = [start]
    for step in range(ITERS - 1):
        last = step == ITERS - 2
        spread_out = sibling(own)
        if step > 0:
            spread_out, part = lax.optimization_barrier((spread_out, part))
            lists = update(step - 1, lists, known, part)
        spread_out = jnp.concatenate([spread_out[: per - 1], own[per - 1 :] + spread_out[per - 1 :]])
        parts = [spread_out] + [swap(spread_out, 4 * z) for z in range(1, nz)]
        a = jnp.concatenate([part[:half] for part in parts])
        b = jnp.concatenate([part[half:] for part in parts])
        far_a, far_b = swap(a, 1), swap(b, 2)
        a, b = jnp.concatenate([a, far_a]), jnp.concatenate([b, far_b])
        far_a, far_b = swap(a, 2), swap(b, 1)
        if step > 0:
            far_a, far_b, lists = lax.optimization_barrier((far_a, far_b, lists))
        *state, own, part, known = call(
            functools.partial(home_kernel, step == 0, last, nh, room, lines),
            (field,) * (0 if last else 2) + (f32(nbody * nsub, ncase, LANES) if last else answer, f32(npatch, nh, ncase, LANES), f32(ncase, LANES)),
            [SMEM] * 4 + [VMEM] * (8 + len(state)),
            near,
            far,
            on,
            picked,
            comp,
            own,
            a,
            far_a,
            b,
            far_b,
            known,
            block,
            *state,
            scratch=[load, spread],
        )
    sums = lax.all_to_all(own, ("body", "sub"), split_axis=0, concat_axis=0, tiled=True)
    return call(
        end_kernel,
        f32(ncase, npatch, gap),
        [SMEM] + [VMEM] * 9,
        keep,
        sums,
        known,
        compliance,
        part,
        sibling(part),
        *lists,
        scratch=[pltpu.VMEM((nh, npatch, ncase, LANES), jnp.float32)],
    )


def solution(mesh):
    in_specs = (
        P(None, "sub", None),
        P("sub", None),
        P("sub", None),
        P("sub", None),
        P("sub", None),
        P("sub"),
        P("body", "sub", None, None),
    )
    out_specs = P(None, "sub", None)
    return jax.shard_map(
        on_device, mesh=mesh, in_specs=in_specs, out_specs=out_specs, check_vma=False
    )
```

```python
import functools

import jax
import jax.numpy as jnp
from jax import lax
from jax.experimental import pallas as pl
from jax.experimental.pallas import tpu as pltpu
from jax.sharding import PartitionSpec as P

ITERS = 4
LANES = 128
SUBLANES = 8
VMEM = pl.BlockSpec(memory_space=pltpu.VMEM)
SMEM = pl.BlockSpec(memory_space=pltpu.SMEM)
HBM = pl.BlockSpec(memory_space=pltpu.HBM)
PARAMS = pltpu.CompilerParams(vmem_limit_bytes=16 * 1024 * 1024)


def f32(*shape):
    return jax.ShapeDtypeStruct(shape, jnp.float32)


def call(kernel, out_shape, specs, *operands, scratch=(), cost=None):
    several = isinstance(out_shape, (tuple, list))
    return pl.pallas_call(
        kernel,
        out_shape=tuple(out_shape) if several else out_shape,
        in_specs=specs,
        out_specs=(VMEM,) * len(out_shape) if several else VMEM,
        scratch_shapes=list(scratch),
        compiler_params=PARAMS,
        cost_estimate=cost,
    )(*operands)


def per_case(value):
    return jnp.sum(value, axis=1, keepdims=True)


def respond(block, load, gamma, energy, answer, last=False):
    ntile, ncase, width = load.shape
    each = 2
    total = jnp.zeros((2 * ncase, ntile * width), jnp.float32)
    for j in range(ntile // each):
        value = jnp.concatenate([load[j * each + i] for i in range(each)], axis=1)
        high = value.astype(jnp.bfloat16)
        low = (value - high.astype(jnp.float32)).astype(jnp.bfloat16)
        total = total + jnp.dot(
            jnp.concatenate([high, low], axis=0),
            block[j * each * width : (j + 1) * each * width, :],
            preferred_element_type=jnp.float32,
        )
    total = total[:ncase] + total[ncase:]
    work = 0.5 * energy
    for i in range(ntile):
        tile = total[:, i * width : (i + 1) * width]
        if not last:
            answer[i] = tile
        work = work + load[i] * tile
    lane = lax.broadcasted_iota(jnp.int32, work.shape, 1)
    sums = jnp.where(lane == 0, per_case(0.5 * gamma), 0.0)
    sums = jnp.where(lane == 1, per_case(work), sums)
    if last:
        answer[...] = jnp.broadcast_to(sums[None], answer.shape)
    else:
        answer[ntile] = sums


def pack_kernel(nh, cut, room, place, field, table, *refs):
    *outs, whole = refs
    nz = len(outs) - 4
    extra = table.shape[1]
    tiles = room * nh
    whole[...] = jnp.zeros_like(whole)

    def body(p, carry):
        whole[pl.ds(place[p], nh)] = field[p]
        return carry

    lax.fori_loop(0, field.shape[0], body, 0, unroll=4)
    first, second = cut * nh, tiles - cut * nh
    for z in range(nz):
        for m in range(4):
            at = (z * 4 + m) * tiles
            one, two = m * (first + extra), z * second
            outs[z][one : one + first] = whole[at : at + first]
            outs[z][one + first : one + first + extra] = table[z * 4 + m]
            outs[nz + m][two : two + second] = whole[at + first : at + tiles]


def block_kernel(block, held, sems):
    pieces = sems.shape[0]
    size = block.shape[0] // pieces
    copies = []
    for j in range(pieces):
        rows = pl.ds(j * size, size)
        copies.append(pltpu.make_async_copy(block.at[rows], held.at[rows], sems.at[j]))
        copies[-1].start()
    for copy in copies:
        copy.wait()


def start_kernel(nh, cut, room, lines, extra, nz, block, *refs):
    a_z, refs = refs[:nz], refs[nz:]
    a_far, refs = refs[:3], refs[3:]
    b_near, refs = refs[:4], refs[4:]
    b_far, refs = refs[: nz - 1], refs[nz - 1 :]
    near, far, on, r_out, comp, answer, load, facts, sems = refs
    copies = []
    for z in range(nz):
        for m in range(4):
            part, at = (a_z[z], 0) if m == 0 else (a_far[m - 1], z * (cut * nh + extra))
            rows = pl.ds(at + cut * nh + lines, extra - lines)
            copies.append(pltpu.make_async_copy(part.at[rows], facts.at[z * 4 + m], sems.at[z * 4 + m]))
            copies[-1].start()
    load[...] = jnp.zeros_like(load)
    gamma = energy = jnp.zeros(r_out.shape[2:], jnp.float32)
    first, second = cut * nh, (room - cut) * nh
    for z in range(nz):
        for m in range(4):
            i = z * 4 + m
            one, at_one = (a_z[z], 0) if m == 0 else (a_far[m - 1], z * (first + extra))
            two, at_two = (b_near[m], 0) if z == 0 else (b_far[z - 1], m * second)
            comp[i * lines : (i + 1) * lines] = one[at_one + first : at_one + first + lines]
            copies[i].wait()
            for j in range(room):
                row = i * room + j
                slot = facts[i, j // SUBLANES, j % SUBLANES, 0].astype(jnp.int32)
                near[i, j] = slot
                far[i, j] = facts[i, j // SUBLANES, j % SUBLANES, 1].astype(jnp.int32)
                on[i, j] = facts[i, j // SUBLANES, j % SUBLANES, 2]
                if j < cut:
                    r = one[at_one + j * nh : at_one + (j + 1) * nh]
                else:
                    r = two[at_two + (j - cut) * nh : at_two + (j - cut + 1) * nh]
                r_out[row] = r
                load[pl.ds(slot, nh)] += r
                for h in range(nh):
                    line, sub = divmod(j * nh + h, SUBLANES)
                    square = r[h] * r[h]
                    gamma = gamma + square
                    energy = energy + one[at_one + first + line, sub : sub + 1, :] * square
    respond(block, load, gamma, energy, answer)


def tree(values):
    while len(values) > 1:
        values = [a + b for a, b in zip(values[::2], values[1::2])]
    return values[0]


def steps(first, sums, known):
    gamma, delta = sums[:, 0:1], sums[:, 1:2]
    if first:
        return gamma, gamma / delta, jnp.zeros_like(gamma)
    beta = gamma / known[:, 0:1]
    return gamma, gamma / (delta - beta * gamma / known[:, 1:2]), beta


def home_kernel(first, last, nh, room, lines, place, away, keep, picked, comp, own, near_a, far_a, near_b, far_b, known, block, *refs):
    r_in, *refs = refs
    if not first:
        s_in, *refs = refs
    if not last:
        r, s, *refs = refs
    answer, part, known_out, load, resp = refs
    load[...] = jnp.zeros_like(load)
    nrow, _, ncase, width = r_in.shape
    at = 0
    for piece in (near_a, far_a, near_b, far_b):
        resp[at : at + piece.shape[0]] = piece[...]
        at += piece.shape[0]
    each = own.shape[0] // 2 + 1
    sums = tree([piece[i + each - 1] for piece in (near_b, far_b) for i in range(0, piece.shape[0], each)])
    gamma, alpha, beta = steps(first, sums, known[...])
    lane = lax.broadcasted_iota(jnp.int32, (ncase, width), 1)
    known_out[...] = jnp.where(lane == 0, gamma, jnp.where(lane == 1, alpha, beta))
    alpha = jnp.broadcast_to(alpha, (ncase, width))
    beta = jnp.broadcast_to(beta, (ncase, width))
    zero = jnp.zeros((ncase, width), jnp.float32)

    def pick(p, carry):
        part[p] = resp[pl.ds(picked[p], nh)]
        return carry

    lax.fori_loop(0, part.shape[0], pick, 0, unroll=8)

    def pair(i, sums):
        gamma, energy = sums
        for j in range(room):
            row = i * room + j
            near, far, on = place[i, j], away[i, j], keep[i, j]
            for h in range(nh):
                line, sub = divmod(j * nh + h, SUBLANES)
                c = comp[i * lines + line, sub : sub + 1, :]
                residual = r_in[row, h]
                image = on * (own[near + h] + resp[far + h] + c * residual)
                if not first:
                    image = image + beta * s_in[row, h]
                residual = residual - alpha * image
                if not last:
                    r[row, h], s[row, h] = residual, image
                load[near + h] += residual
                square = residual * residual
                gamma = gamma + square
                energy = energy + c * square
        return gamma, energy

    gamma, energy = lax.fori_loop(0, nrow // room, pair, (zero, zero))
    respond(block, load, gamma, energy, answer, last=last)


def list_kernel(first, keep, known, comp, mine, theirs, *refs):
    if first:
        r_in, r, d, x, s = refs
    else:
        r_in, d_in, x_in, s_in, r, d, x, s = refs
    npatch, nh, ncase, width = r.shape
    alpha = jnp.broadcast_to(known[:, 1:2], (ncase, width))
    beta = jnp.broadcast_to(known[:, 2:3], (ncase, width))

    def body(p, carry):
        on, row = keep[p], comp[pl.ds(p, 1), :]
        for h in range(nh):
            residual = r_in[p, h]
            c = row[:, h * width : (h + 1) * width]
            image = on * (mine[p, h] + theirs[p, h] + c * residual)
            if first:
                direction, moved = residual, alpha * residual
            else:
                direction = residual + beta * d_in[p, h]
                image = image + beta * s_in[p, h]
                moved = x_in[p, h] + alpha * direction
            r[p, h], d[p, h], x[p, h], s[p, h] = residual - alpha * image, direction, moved, image
        return carry

    lax.fori_loop(0, npatch, body, 0, unroll=4)


def end_kernel(keep, sums, known, comp, mine, theirs, r_in, d_in, x_in, s_in, out, moved):
    npatch, nh, ncase, width = r_in.shape
    total = sums[0]
    for i in range(1, sums.shape[0]):
        total = total + sums[i]
    _, alpha, beta = steps(False, total, known[...])
    one, two = jnp.broadcast_to(alpha, (ncase, width)), jnp.broadcast_to(beta, (ncase, width))
    alpha = jnp.broadcast_to(known[:, 1:2], (ncase, width))
    beta = jnp.broadcast_to(known[:, 2:3], (ncase, width))

    def body(p, carry):
        on, row = keep[p], comp[pl.ds(p, 1), :]
        for h in range(nh):
            residual = r_in[p, h]
            c = row[:, h * width : (h + 1) * width]
            image = on * (mine[p, h] + theirs[p, h] + c * residual) + beta * s_in[p, h]
            direction = residual + beta * d_in[p, h]
            residual = residual - alpha * image
            moved[h, p] = x_in[p, h] + alpha * direction + one * (residual + two * direction)
        return carry

    lax.fori_loop(0, npatch, body, 0, unroll=4)
    for h in range(nh):
        out[:, :, h * width : (h + 1) * width] = jnp.swapaxes(moved[h], 0, 1)


def on_device(rhs, compliance, plate_owner, found_owner, slot_pairs, active, inverse):
    nsub = lax.axis_size("sub")
    nbody = lax.axis_size("body")
    side = lax.axis_index("body")
    me = lax.axis_index("sub")
    ncase, npatch, gap = rhs.shape
    block = inverse[0, 0]
    nslot = block.shape[0] // gap
    nh = gap // LANES
    per = nslot * nh + 1
    room = max(2, 2 * npatch // nsub)
    nrow = nsub * room
    lines = -(-room * nh // SUBLANES)
    deep = -(-room // SUBLANES)
    extra = lines + deep
    cut = room // 2
    first = cut * nh + extra
    second = (room - cut) * nh
    nz = nsub // 4
    half = nslot // 2 * nh

    def swap(value, far):
        return lax.ppermute(value, "sub", [(i, i ^ far) for i in range(nsub)])

    def sibling(value):
        return lax.ppermute(value, "body", [(i, nbody - 1 - i) for i in range(nbody)])

    keep = active.astype(jnp.float32)
    plate, foundation = plate_owner[:, 0], found_owner[:, 0]
    owner, other = jnp.where(side == 0, plate, foundation), jnp.where(side == 0, foundation, plate)
    slot, other_slot = (jnp.where(side == i, slot_pairs[:, 0], slot_pairs[:, 1]) for i in range(2))
    index = jnp.arange(npatch, dtype=jnp.int32)
    earlier = (owner[None, :] == owner[:, None]) & (index[None, :] < index[:, None])
    rank = jnp.sum(earlier.astype(jnp.int32), axis=1)
    place = (owner ^ me) * room * nh + rank * nh

    def found(away):
        x_bit, y_bit, z_part = away & 1, (away >> 1) & 1, away >> 2
        found_a = ((y_bit * 2 + x_bit) * nz + z_part) * half + other_slot * nh
        found_b = ((x_bit * 2 + y_bit) * nz + z_part) * (half + 1) + (other_slot - nslot // 2) * nh
        return jnp.where(other_slot < nslot // 2, found_a, nsub * half + found_b)

    facts = jnp.stack([slot * nh, found(owner ^ other)], axis=1).astype(jnp.float32)
    facts = jnp.concatenate([facts, keep[:, None]], axis=1)
    facts = jnp.concatenate([compliance, jnp.pad(facts, ((0, 0), (0, LANES - 3)))], axis=1)
    row = (owner ^ me) * room + rank
    placed = (row[None, :] == jnp.arange(nrow, dtype=jnp.int32)[:, None]).astype(jnp.float32)
    facts = jnp.dot(placed, facts, precision=lax.Precision.HIGHEST).reshape(nsub, room, gap + LANES)
    lined = facts[:, :, :gap].reshape(nsub, room * nh, LANES)
    lined = jnp.pad(lined, ((0, 0), (0, lines * SUBLANES - room * nh), (0, 0)))
    named = jnp.pad(facts[:, :, gap:], ((0, 0), (0, deep * SUBLANES - room), (0, 0)))
    table = jnp.concatenate([lined, named], axis=1).reshape(nsub, lines + deep, SUBLANES, LANES)
    start = (keep[None, :, None] * rhs).reshape(ncase, npatch, nh, LANES)
    start = jnp.transpose(start, (1, 2, 0, 3))
    picked = found(me ^ other).astype(jnp.int32)
    place, picked = lax.optimization_barrier((place, picked))

    packed = call(
        functools.partial(pack_kernel, nh, cut, room),
        (f32(4 * first, ncase, LANES),) * nz + (f32(nz * second, ncase, LANES),) * 4,
        [SMEM, VMEM, VMEM],
        place,
        start,
        table,
        scratch=[pltpu.VMEM((nrow * nh, ncase, LANES), jnp.float32)],
    )
    a_z = [packed[0]] + [swap(packed[z], 4 * z) for z in range(1, nz)]
    b_near = [packed[nz]] + [swap(packed[nz + m], m) for m in range(1, 4)]
    b_far = [
        swap(jnp.concatenate([part[z * second : (z + 1) * second] for part in b_near]), 4 * z)
        for z in range(1, nz)
    ]
    a_far = [
        swap(jnp.concatenate([part[m * first : (m + 1) * first] for part in a_z]), m) for m in range(1, 4)
    ]
    held = call(
        block_kernel,
        jax.ShapeDtypeStruct(block.shape, block.dtype),
        [HBM],
        pltpu.with_memory_space_constraint(block, pltpu.HBM),
        scratch=[pltpu.SemaphoreType.DMA((nslot,))],
        cost=pl.CostEstimate(flops=0, bytes_accessed=4 * block.size, transcendentals=0),
    )
    a_far, block = lax.optimization_barrier((a_far, held))
    field = f32(nrow, nh, ncase, LANES)
    answer = f32(per, ncase, LANES)
    load = pltpu.VMEM((nslot * nh, ncase, LANES), jnp.float32)
    spread = pltpu.VMEM((nsub * per, ncase, LANES), jnp.float32)
    near, far, on, home_r, comp, own = pl.pallas_call(
        functools.partial(start_kernel, nh, cut, room, lines, extra, nz),
        out_shape=(jax.ShapeDtypeStruct((nsub, room), jnp.int32),) * 2
        + (f32(nsub, room), field, f32(nsub * lines, ncase, LANES), answer),
        in_specs=[VMEM] * (2 * nz + 7),
        out_specs=(SMEM,) * 3 + (VMEM,) * 3,
        scratch_shapes=[
            load,
            pltpu.SMEM((nsub, deep, SUBLANES, LANES), jnp.float32),
            pltpu.SemaphoreType.DMA((nsub,)),
        ],
        compiler_params=PARAMS,
    )(block, *a_z, *a_far, *b_near, *b_far)
    def update(step, lists, known, part):
        return call(
            functools.partial(list_kernel, step == 0),
            (f32(npatch, nh, ncase, LANES),) * 4,
            [SMEM] + [VMEM] * (4 + len(lists)),
            keep,
            known,
            compliance,
            part,
            sibling(part),
            *lists,
            cost=pl.CostEstimate(flops=16 * rhs.size, bytes_accessed=44 * rhs.size, transcendentals=0),
        )

    known = jnp.zeros((ncase, LANES), jnp.float32)
    state = [home_r]
    lists = [start]
    for step in range(ITERS - 1):
        last = step == ITERS - 2
        spread_out = sibling(own)
        if step > 0:
            spread_out, part = lax.optimization_barrier((spread_out, part))
            lists = update(step - 1, lists, known, part)
        spread_out = jnp.concatenate([spread_out[: per - 1], own[per - 1 :] + spread_out[per - 1 :]])
        parts = [spread_out] + [swap(spread_out, 4 * z) for z in range(1, nz)]
        a = jnp.concatenate([part[:half] for part in parts])
        b = jnp.concatenate([part[half:] for part in parts])
        far_a, far_b = swap(a, 1), swap(b, 2)
        a, b = jnp.concatenate([a, far_a]), jnp.concatenate([b, far_b])
        far_a, far_b = swap(a, 2), swap(b, 1)
        if step > 0:
            far_a, far_b, lists = lax.optimization_barrier((far_a, far_b, lists))
        *state, own, part, known = call(
            functools.partial(home_kernel, step == 0, last, nh, room, lines),
            (field,) * (0 if last else 2) + (f32(nbody * nsub, ncase, LANES) if last else answer, f32(npatch, nh, ncase, LANES), f32(ncase, LANES)),
            [SMEM] * 4 + [VMEM] * (8 + len(state)),
            near,
            far,
            on,
            picked,
            comp,
            own,
            a,
            far_a,
            b,
            far_b,
            known,
            block,
            *state,
            scratch=[load, spread],
        )
    sums = lax.all_to_all(own, ("body", "sub"), split_axis=0, concat_axis=0, tiled=True)
    return call(
        end_kernel,
        f32(ncase, npatch, gap),
        [SMEM] + [VMEM] * 9,
        keep,
        sums,
        known,
        compliance,
        part,
        sibling(part),
        *lists,
        scratch=[pltpu.VMEM((nh, npatch, ncase, LANES), jnp.float32)],
    )


def solution(mesh):
    in_specs = (
        P(None, "sub", None),
        P("sub", None),
        P("sub", None),
        P("sub", None),
        P("sub", None),
        P("sub"),
        P("body", "sub", None, None),
    )
    out_specs = P(None, "sub", None)
    return jax.shard_map(
        on_device, mesh=mesh, in_specs=in_specs, out_specs=out_specs, check_vma=False
    )
```

```python
import functools

import jax
import jax.numpy as jnp
from jax import lax
from jax.experimental import pallas as pl
from jax.experimental.pallas import tpu as pltpu
from jax.sharding import PartitionSpec as P

ITERS = 4
LANES = 128
SUBLANES = 8
VMEM = pl.BlockSpec(memory_space=pltpu.VMEM)
SMEM = pl.BlockSpec(memory_space=pltpu.SMEM)
HBM = pl.BlockSpec(memory_space=pltpu.HBM)
PARAMS = pltpu.CompilerParams(vmem_limit_bytes=16 * 1024 * 1024)


def f32(*shape):
    return jax.ShapeDtypeStruct(shape, jnp.float32)


def call(kernel, out_shape, specs, *operands, scratch=(), cost=None):
    several = isinstance(out_shape, (tuple, list))
    return pl.pallas_call(
        kernel,
        out_shape=tuple(out_shape) if several else out_shape,
        in_specs=specs,
        out_specs=(VMEM,) * len(out_shape) if several else VMEM,
        scratch_shapes=list(scratch),
        compiler_params=PARAMS,
        cost_estimate=cost,
    )(*operands)


def per_case(value):
    return jnp.sum(value, axis=1, keepdims=True)


def respond(block, load, gamma, energy, answer, last=False):
    ntile, ncase, width = load.shape
    each = 2
    total = jnp.zeros((2 * ncase, ntile * width), jnp.float32)
    for j in range(ntile // each):
        value = jnp.concatenate([load[j * each + i] for i in range(each)], axis=1)
        high = value.astype(jnp.bfloat16)
        low = (value - high.astype(jnp.float32)).astype(jnp.bfloat16)
        total = total + jnp.dot(
            jnp.concatenate([high, low], axis=0),
            block[j * each * width : (j + 1) * each * width, :],
            preferred_element_type=jnp.float32,
        )
    total = total[:ncase] + total[ncase:]
    work = 0.5 * energy
    for i in range(ntile):
        tile = total[:, i * width : (i + 1) * width]
        if not last:
            answer[i] = tile
        work = work + load[i] * tile
    lane = lax.broadcasted_iota(jnp.int32, work.shape, 1)
    sums = jnp.where(lane == 0, per_case(0.5 * gamma), 0.0)
    sums = jnp.where(lane == 1, per_case(work), sums)
    if last:
        answer[...] = jnp.broadcast_to(sums[None], answer.shape)
    else:
        answer[ntile] = sums


def pack_kernel(nh, nz, by_z, place, field, *refs):
    if not by_z:
        table, *refs = refs
    *outs, whole = refs
    tiles = whole.shape[0] // (4 * nz + 1)
    whole[...] = jnp.zeros_like(whole)

    def body(p, carry):
        whole[pl.ds(place[p], nh)] = field[p]
        return carry

    lax.fori_loop(0, field.shape[0], body, 0, unroll=4)
    for i, out in enumerate(outs):
        size = out.shape[0] // (4 * nz // len(outs))
        for k in range(out.shape[0] // size):
            owner = i * 4 + k if by_z else k * 4 + i
            out[k * size : k * size + tiles] = whole[owner * tiles : (owner + 1) * tiles]
            if not by_z:
                out[k * size + tiles : (k + 1) * size] = table[owner]


def block_kernel(block, held, sems):
    pieces = sems.shape[0]
    size = block.shape[0] // pieces
    copies = []
    for j in range(pieces):
        rows = pl.ds(j * size, size)
        copies.append(pltpu.make_async_copy(block.at[rows], held.at[rows], sems.at[j]))
        copies[-1].start()
    for copy in copies:
        copy.wait()


def start_kernel(nh, cut, room, lines, extra, nz, block, *refs):
    a_z, refs = refs[:nz], refs[nz:]
    a_far, refs = refs[:3], refs[3:]
    b_near, refs = refs[:4], refs[4:]
    b_far, refs = refs[: nz - 1], refs[nz - 1 :]
    near, far, on, r_out, comp, answer, load, facts, sems = refs
    first, second = cut * nh, (room - cut) * nh
    blocks = []
    for z in range(nz):
        for m in range(4):
            one = (a_z[z], 0) if m == 0 else (a_far[m - 1], z * first)
            two = (b_near[m], 0) if z == 0 else (b_far[z - 1], m * (second + extra))
            blocks.append((*one, *two))
    copies = []
    for i, (_, _, two, at_two) in enumerate(blocks):
        rows = pl.ds(at_two + second + lines, extra - lines)
        copies.append(pltpu.make_async_copy(two.at[rows], facts.at[i], sems.at[i]))
        copies[-1].start()
    load[...] = jnp.zeros_like(load)
    gamma = energy = jnp.zeros(r_out.shape[2:], jnp.float32)
    for i, (one, at_one, two, at_two) in enumerate(blocks):
        at_comp = at_two + second
        comp[i * lines : (i + 1) * lines] = two[at_comp : at_comp + lines]
        copies[i].wait()
        for j in range(room):
            row = i * room + j
            slot = facts[i, j // SUBLANES, j % SUBLANES, 0].astype(jnp.int32)
            near[row] = slot
            far[row] = facts[i, j // SUBLANES, j % SUBLANES, 1].astype(jnp.int32)
            on[row] = facts[i, j // SUBLANES, j % SUBLANES, 2]
            if j < cut:
                r = one[at_one + j * nh : at_one + (j + 1) * nh]
            else:
                r = two[at_two + (j - cut) * nh : at_two + (j - cut + 1) * nh]
            r_out[row] = r
            load[pl.ds(slot, nh)] += r
            for h in range(nh):
                line, sub = divmod(j * nh + h, SUBLANES)
                square = r[h] * r[h]
                gamma = gamma + square
                energy = energy + two[at_comp + line, sub : sub + 1, :] * square
    respond(block, load, gamma, energy, answer)


def tree(values):
    while len(values) > 1:
        values = [a + b for a, b in zip(values[::2], values[1::2])]
    return values[0]


def steps(first, sums, known):
    gamma, delta = sums[:, 0:1], sums[:, 1:2]
    if first:
        return gamma, gamma / delta, jnp.zeros_like(gamma)
    beta = gamma / known[:, 0:1]
    return gamma, gamma / (delta - beta * gamma / known[:, 1:2]), beta


def home_kernel(first, last, nh, room, lines, place, away, keep, picked, comp, own, near_a, far_a, near_b, far_b, known, block, *refs):
    r_in, *refs = refs
    if not first:
        s_in, *refs = refs
    if not last:
        r, s, *refs = refs
    answer, part, known_out, load, resp = refs
    load[...] = jnp.zeros_like(load)
    nrow, _, ncase, width = r_in.shape
    at = 0
    for piece in (near_a, far_a, near_b, far_b):
        resp[at : at + piece.shape[0]] = piece[...]
        at += piece.shape[0]
    each = own.shape[0] // 2 + 1
    sums = tree([piece[i + each - 1] for piece in (near_b, far_b) for i in range(0, piece.shape[0], each)])
    gamma, alpha, beta = steps(first, sums, known[...])
    lane = lax.broadcasted_iota(jnp.int32, (ncase, width), 1)
    known_out[...] = jnp.where(lane == 0, gamma, jnp.where(lane == 1, alpha, beta))
    alpha = jnp.broadcast_to(alpha, (ncase, width))
    beta = jnp.broadcast_to(beta, (ncase, width))
    zero = jnp.zeros((ncase, width), jnp.float32)

    def pick(p, carry):
        part[p] = resp[pl.ds(picked[p], nh)]
        return carry

    lax.fori_loop(0, part.shape[0], pick, 0, unroll=8)

    def pair(i, sums):
        gamma, energy = sums
        for j in range(room):
            row = i * room + j
            near, far, on = place[row], away[row], keep[row]
            for h in range(nh):
                line, sub = divmod(j * nh + h, SUBLANES)
                c = comp[i * lines + line, sub : sub + 1, :]
                residual = r_in[row, h]
                image = on * (own[near + h] + resp[far + h] + c * residual)
                if not first:
                    image = image + beta * s_in[row, h]
                residual = residual - alpha * image
                if not last:
                    r[row, h], s[row, h] = residual, image
                load[near + h] += residual
                square = residual * residual
                gamma = gamma + square
                energy = energy + c * square
        return gamma, energy

    gamma, energy = lax.fori_loop(0, nrow // room, pair, (zero, zero))
    respond(block, load, gamma, energy, answer, last=last)


def list_kernel(first, keep, known, comp, mine, theirs, *refs):
    if first:
        r_in, r, d, x, s = refs
    else:
        r_in, d_in, x_in, s_in, r, d, x, s = refs
    npatch, nh, ncase, width = r.shape
    alpha = jnp.broadcast_to(known[:, 1:2], (ncase, width))
    beta = jnp.broadcast_to(known[:, 2:3], (ncase, width))

    def body(p, carry):
        on, row = keep[p], comp[pl.ds(p, 1), :]
        for h in range(nh):
            residual = r_in[p, h]
            c = row[:, h * width : (h + 1) * width]
            image = on * (mine[p, h] + theirs[p, h] + c * residual)
            if first:
                direction, moved = residual, alpha * residual
            else:
                direction = residual + beta * d_in[p, h]
                image = image + beta * s_in[p, h]
                moved = x_in[p, h] + alpha * direction
            r[p, h], d[p, h], x[p, h], s[p, h] = residual - alpha * image, direction, moved, image
        return carry

    lax.fori_loop(0, npatch, body, 0, unroll=4)


def end_kernel(keep, sums, known, comp, mine, theirs, r_in, d_in, x_in, s_in, out, moved):
    npatch, nh, ncase, width = r_in.shape
    total = sums[0]
    for i in range(1, sums.shape[0]):
        total = total + sums[i]
    _, alpha, beta = steps(False, total, known[...])
    one, two = jnp.broadcast_to(alpha, (ncase, width)), jnp.broadcast_to(beta, (ncase, width))
    alpha = jnp.broadcast_to(known[:, 1:2], (ncase, width))
    beta = jnp.broadcast_to(known[:, 2:3], (ncase, width))

    def body(p, carry):
        on, row = keep[p], comp[pl.ds(p, 1), :]
        for h in range(nh):
            residual = r_in[p, h]
            c = row[:, h * width : (h + 1) * width]
            image = on * (mine[p, h] + theirs[p, h] + c * residual) + beta * s_in[p, h]
            direction = residual + beta * d_in[p, h]
            residual = residual - alpha * image
            moved[h, p] = x_in[p, h] + alpha * direction + one * (residual + two * direction)
        return carry

    lax.fori_loop(0, npatch, body, 0, unroll=4)
    for h in range(nh):
        out[:, :, h * width : (h + 1) * width] = jnp.swapaxes(moved[h], 0, 1)


def on_device(rhs, compliance, plate_owner, found_owner, slot_pairs, active, inverse):
    nsub = lax.axis_size("sub")
    nbody = lax.axis_size("body")
    side = lax.axis_index("body")
    me = lax.axis_index("sub")
    ncase, npatch, gap = rhs.shape
    block = inverse[0, 0]
    nslot = block.shape[0] // gap
    nh = gap // LANES
    per = nslot * nh + 1
    room = max(2, 2 * npatch // nsub)
    nrow = nsub * room
    lines = -(-room * nh // SUBLANES)
    deep = -(-room // SUBLANES)
    extra = lines + deep
    cut = room // 2
    first = cut * nh
    second = (room - cut) * nh + extra
    nz = nsub // 4
    half = nslot // 2 * nh

    def swap(value, far):
        return lax.ppermute(value, "sub", [(i, i ^ far) for i in range(nsub)])

    def sibling(value):
        return lax.ppermute(value, "body", [(i, nbody - 1 - i) for i in range(nbody)])

    keep = active.astype(jnp.float32)
    plate, foundation = plate_owner[:, 0], found_owner[:, 0]
    owner, other = jnp.where(side == 0, plate, foundation), jnp.where(side == 0, foundation, plate)
    slot, other_slot = (jnp.where(side == i, slot_pairs[:, 0], slot_pairs[:, 1]) for i in range(2))
    index = jnp.arange(npatch, dtype=jnp.int32)
    earlier = (owner[None, :] == owner[:, None]) & (index[None, :] < index[:, None])
    rank = jnp.sum(earlier.astype(jnp.int32), axis=1)
    base, none = owner ^ me, 4 * nz
    place_a = jnp.where(rank < cut, base * cut + rank, none * cut) * nh
    place_b = jnp.where(rank < cut, none * (room - cut), base * (room - cut) + rank - cut) * nh

    def found(away):
        x_bit, y_bit, z_part = away & 1, (away >> 1) & 1, away >> 2
        found_a = ((y_bit * 2 + x_bit) * nz + z_part) * half + other_slot * nh
        found_b = ((x_bit * 2 + y_bit) * nz + z_part) * (half + 1) + (other_slot - nslot // 2) * nh
        return jnp.where(other_slot < nslot // 2, found_a, nsub * half + found_b)

    facts = jnp.stack([slot * nh, found(owner ^ other)], axis=1).astype(jnp.float32)
    facts = jnp.concatenate([facts, keep[:, None]], axis=1)
    facts = jnp.concatenate([compliance, jnp.pad(facts, ((0, 0), (0, LANES - 3)))], axis=1)
    row = (owner ^ me) * room + rank
    placed = (row[None, :] == jnp.arange(nrow, dtype=jnp.int32)[:, None]).astype(jnp.float32)
    facts = jnp.dot(placed, facts, precision=lax.Precision.HIGHEST).reshape(nsub, room, gap + LANES)
    lined = facts[:, :, :gap].reshape(nsub, room * nh, LANES)
    lined = jnp.pad(lined, ((0, 0), (0, lines * SUBLANES - room * nh), (0, 0)))
    named = jnp.pad(facts[:, :, gap:], ((0, 0), (0, deep * SUBLANES - room), (0, 0)))
    table = jnp.concatenate([lined, named], axis=1).reshape(nsub, lines + deep, SUBLANES, LANES)
    start = (keep[None, :, None] * rhs).reshape(ncase, npatch, nh, LANES)
    start = jnp.transpose(start, (1, 2, 0, 3))
    picked = found(me ^ other).astype(jnp.int32)
    place_a, place_b, picked = lax.optimization_barrier((place_a, place_b, picked))

    a_z = call(
        functools.partial(pack_kernel, nh, nz, True),
        (f32(4 * first, ncase, LANES),) * nz,
        [SMEM, VMEM],
        place_a,
        start,
        scratch=[pltpu.VMEM(((nsub + 1) * cut * nh, ncase, LANES), jnp.float32)],
    )
    b_near = call(
        functools.partial(pack_kernel, nh, nz, False),
        (f32(nz * second, ncase, LANES),) * 4,
        [SMEM, VMEM, VMEM],
        place_b,
        start,
        table,
        scratch=[pltpu.VMEM(((nsub + 1) * (room - cut) * nh, ncase, LANES), jnp.float32)],
    )
    a_z = [a_z[0]] + [swap(a_z[z], 4 * z) for z in range(1, nz)]
    b_near = [b_near[0]] + [swap(b_near[m], m) for m in range(1, 4)]
    block = call(
        block_kernel,
        jax.ShapeDtypeStruct(block.shape, block.dtype),
        [HBM],
        pltpu.with_memory_space_constraint(block, pltpu.HBM),
        scratch=[pltpu.SemaphoreType.DMA((nslot,))],
        cost=pl.CostEstimate(flops=0, bytes_accessed=4 * block.size, transcendentals=0),
    )
    a_z, b_near, block = lax.optimization_barrier((a_z, b_near, block))
    b_far = [
        swap(jnp.concatenate([part[z * second : (z + 1) * second] for part in b_near]), 4 * z)
        for z in range(1, nz)
    ]
    a_far = [
        swap(jnp.concatenate([part[m * first : (m + 1) * first] for part in a_z]), m) for m in range(1, 4)
    ]
    field = f32(nrow, nh, ncase, LANES)
    answer = f32(per, ncase, LANES)
    load = pltpu.VMEM((nslot * nh, ncase, LANES), jnp.float32)
    spread = pltpu.VMEM((nsub * per, ncase, LANES), jnp.float32)
    near, far, on, home_r, comp, own = pl.pallas_call(
        functools.partial(start_kernel, nh, cut, room, lines, extra, nz),
        out_shape=(jax.ShapeDtypeStruct((nrow,), jnp.int32),) * 2
        + (f32(nrow), field, f32(nsub * lines, ncase, LANES), answer),
        in_specs=[VMEM] * (2 * nz + 7),
        out_specs=(SMEM,) * 3 + (VMEM,) * 3,
        scratch_shapes=[
            load,
            pltpu.SMEM((nsub, deep, SUBLANES, LANES), jnp.float32),
            pltpu.SemaphoreType.DMA((nsub,)),
        ],
        compiler_params=PARAMS,
    )(block, *a_z, *a_far, *b_near, *b_far)
    def update(step, lists, known, part):
        return call(
            functools.partial(list_kernel, step == 0),
            (f32(npatch, nh, ncase, LANES),) * 4,
            [SMEM] + [VMEM] * (4 + len(lists)),
            keep,
            known,
            compliance,
            part,
            sibling(part),
            *lists,
            cost=pl.CostEstimate(flops=16 * rhs.size, bytes_accessed=44 * rhs.size, transcendentals=0),
        )

    known = jnp.zeros((ncase, LANES), jnp.float32)
    state = [home_r]
    lists = [start]
    for step in range(ITERS - 1):
        last = step == ITERS - 2
        spread_out = sibling(own)
        if step > 0:
            spread_out, part = lax.optimization_barrier((spread_out, part))
            lists = update(step - 1, lists, known, part)
        spread_out = jnp.concatenate([spread_out[: per - 1], own[per - 1 :] + spread_out[per - 1 :]])
        parts = [spread_out] + [swap(spread_out, 4 * z) for z in range(1, nz)]
        a = jnp.concatenate([part[:half] for part in parts])
        b = jnp.concatenate([part[half:] for part in parts])
        far_a, far_b = swap(a, 1), swap(b, 2)
        a, b = jnp.concatenate([a, far_a]), jnp.concatenate([b, far_b])
        far_a, far_b = swap(a, 2), swap(b, 1)
        if step > 0:
            far_a, far_b, lists = lax.optimization_barrier((far_a, far_b, lists))
        *state, own, part, known = call(
            functools.partial(home_kernel, step == 0, last, nh, room, lines),
            (field,) * (0 if last else 2) + (f32(nbody * nsub, ncase, LANES) if last else answer, f32(npatch, nh, ncase, LANES), f32(ncase, LANES)),
            [SMEM] * 4 + [VMEM] * (8 + len(state)),
            near,
            far,
            on,
            picked,
            comp,
            own,
            a,
            far_a,
            b,
            far_b,
            known,
            block,
            *state,
            scratch=[load, spread],
        )
    sums = lax.all_to_all(own, ("body", "sub"), split_axis=0, concat_axis=0, tiled=True)
    return call(
        end_kernel,
        f32(ncase, npatch, gap),
        [SMEM] + [VMEM] * 9,
        keep,
        sums,
        known,
        compliance,
        part,
        sibling(part),
        *lists,
        scratch=[pltpu.VMEM((nh, npatch, ncase, LANES), jnp.float32)],
    )


def solution(mesh):
    in_specs = (
        P(None, "sub", None),
        P("sub", None),
        P("sub", None),
        P("sub", None),
        P("sub", None),
        P("sub"),
        P("body", "sub", None, None),
    )
    out_specs = P(None, "sub", None)
    return jax.shard_map(
        on_device, mesh=mesh, in_specs=in_specs, out_specs=out_specs, check_vma=False
    )
```

```python
import functools
import math

import jax
import jax.numpy as jnp
from jax import lax
from jax.experimental import pallas as pl
from jax.experimental.pallas import tpu as pltpu
from jax.sharding import PartitionSpec as P

ITERS = 4
LANES = 128
SUBLANES = 8
VMEM = pl.BlockSpec(memory_space=pltpu.VMEM)
SMEM = pl.BlockSpec(memory_space=pltpu.SMEM)
HBM = pl.BlockSpec(memory_space=pltpu.HBM)
PARAMS = pltpu.CompilerParams(vmem_limit_bytes=16 * 1024 * 1024)


def f32(*shape):
    return jax.ShapeDtypeStruct(shape, jnp.float32)


def call(kernel, out_shape, specs, *operands, scratch=(), cost=None):
    several = isinstance(out_shape, (tuple, list))
    return pl.pallas_call(
        kernel,
        out_shape=tuple(out_shape) if several else out_shape,
        in_specs=specs,
        out_specs=(VMEM,) * len(out_shape) if several else VMEM,
        scratch_shapes=list(scratch),
        compiler_params=PARAMS,
        cost_estimate=cost,
    )(*operands)


def per_case(value):
    return jnp.sum(value, axis=1, keepdims=True)


def respond(block, load, gamma, energy, answer, last=False):
    ntile, ncase, width = load.shape
    each = 2
    total = jnp.zeros((2 * ncase, ntile * width), jnp.float32)
    for j in range(ntile // each):
        value = jnp.concatenate([load[j * each + i] for i in range(each)], axis=1)
        high = value.astype(jnp.bfloat16)
        low = (value - high.astype(jnp.float32)).astype(jnp.bfloat16)
        total = total + jnp.dot(
            jnp.concatenate([high, low], axis=0),
            block[j * each * width : (j + 1) * each * width, :],
            preferred_element_type=jnp.float32,
        )
    total = total[:ncase] + total[ncase:]
    work = 0.5 * energy
    for i in range(ntile):
        tile = total[:, i * width : (i + 1) * width]
        if not last:
            answer[i] = tile
        work = work + load[i] * tile
    lane = lax.broadcasted_iota(jnp.int32, work.shape, 1)
    sums = jnp.where(lane == 0, per_case(0.5 * gamma), 0.0)
    sums = jnp.where(lane == 1, per_case(work), sums)
    if last:
        answer[...] = jnp.broadcast_to(sums[None], answer.shape)
    else:
        answer[ntile] = sums


def pack_kernel(nh, tiles, place, field, table, *refs):
    *outs, whole = refs
    extra = table.shape[1]
    whole[...] = jnp.zeros_like(whole)

    def body(p, carry):
        whole[pl.ds(place[p], nh)] = field[p]
        return carry

    lax.fori_loop(0, field.shape[0], body, 0, unroll=4)
    for i, out in enumerate(outs):
        for k in range(len(outs)):
            owner = i * len(outs) + k
            out[k * tiles : (k + 1) * tiles - extra] = whole[owner * tiles : (owner + 1) * tiles - extra]
            out[(k + 1) * tiles - extra : (k + 1) * tiles] = table[owner]


def block_kernel(block, held, sems):
    pieces = sems.shape[0]
    size = block.shape[0] // pieces
    copies = []
    for j in range(pieces):
        rows = pl.ds(j * size, size)
        copies.append(pltpu.make_async_copy(block.at[rows], held.at[rows], sems.at[j]))
        copies[-1].start()
    for copy in copies:
        copy.wait()


def start_kernel(nh, room, lines, tiles, side, block, *refs):
    near_parts, refs = refs[:side], refs[side:]
    far_parts, refs = refs[: side - 1], refs[side - 1 :]
    near, far, on, r_out, comp, answer, load, facts, sems = refs
    blocks = [
        (near_parts[i], 0) if k == 0 else (far_parts[k - 1], i * tiles) for i in range(side) for k in range(side)
    ]
    copies = []
    for i, (part, at) in enumerate(blocks):
        rows = pl.ds(at + room * nh + lines, tiles - room * nh - lines)
        copies.append(pltpu.make_async_copy(part.at[rows], facts.at[i], sems.at[i]))
        copies[-1].start()
    load[...] = jnp.zeros_like(load)
    gamma = energy = jnp.zeros(r_out.shape[2:], jnp.float32)
    for i, (part, at) in enumerate(blocks):
        at_comp = at + room * nh
        comp[i * lines : (i + 1) * lines] = part[at_comp : at_comp + lines]
        copies[i].wait()
        for j in range(room):
            row = i * room + j
            slot = facts[i, j // SUBLANES, j % SUBLANES, 0].astype(jnp.int32)
            near[row] = slot
            far[row] = facts[i, j // SUBLANES, j % SUBLANES, 1].astype(jnp.int32)
            on[row] = facts[i, j // SUBLANES, j % SUBLANES, 2]
            r = part[at + j * nh : at + (j + 1) * nh]
            r_out[row] = r
            load[pl.ds(slot, nh)] += r
            for h in range(nh):
                line, sub = divmod(j * nh + h, SUBLANES)
                square = r[h] * r[h]
                gamma = gamma + square
                energy = energy + part[at_comp + line, sub : sub + 1, :] * square
    respond(block, load, gamma, energy, answer)


def tree(values):
    while len(values) > 1:
        values = [a + b for a, b in zip(values[::2], values[1::2])]
    return values[0]


def steps(first, sums, known):
    gamma, delta = sums[:, 0:1], sums[:, 1:2]
    if first:
        return gamma, gamma / delta, jnp.zeros_like(gamma)
    beta = gamma / known[:, 0:1]
    return gamma, gamma / (delta - beta * gamma / known[:, 1:2]), beta


def home_kernel(first, last, nh, room, lines, place, away, keep, picked, comp, own, near, far, known, block, *refs):
    r_in, *refs = refs
    if not first:
        s_in, *refs = refs
    if not last:
        r, s, *refs = refs
    answer, part, known_out, load, resp = refs
    load[...] = jnp.zeros_like(load)
    nrow, _, ncase, width = r_in.shape
    size, each = near.shape[0], own.shape[0]
    resp[:size], resp[size:] = near[...], far[...]
    shares = [[part[i + each - 1] for i in range(0, size, each)] for part in (near, far)]
    (one, two), (three, four) = [[tree(part[: len(part) // 2]), tree(part[len(part) // 2 :])] for part in shares]
    sums = (one + four) + (two + three)
    gamma, alpha, beta = steps(first, sums, known[...])
    lane = lax.broadcasted_iota(jnp.int32, (ncase, width), 1)
    known_out[...] = jnp.where(lane == 0, gamma, jnp.where(lane == 1, alpha, beta))
    alpha = jnp.broadcast_to(alpha, (ncase, width))
    beta = jnp.broadcast_to(beta, (ncase, width))
    zero = jnp.zeros((ncase, width), jnp.float32)

    def pick(p, carry):
        part[p] = resp[pl.ds(picked[p], nh)]
        return carry

    lax.fori_loop(0, part.shape[0], pick, 0, unroll=8)

    def pair(i, sums):
        gamma, energy = sums
        for j in range(room):
            row = i * room + j
            close, apart, on = place[row], away[row], keep[row]
            for h in range(nh):
                line, sub = divmod(j * nh + h, SUBLANES)
                c = comp[i * lines + line, sub : sub + 1, :]
                residual = r_in[row, h]
                image = on * (own[close + h] + resp[apart + h] + c * residual)
                if not first:
                    image = image + beta * s_in[row, h]
                residual = residual - alpha * image
                if not last:
                    r[row, h], s[row, h] = residual, image
                load[close + h] += residual
                square = residual * residual
                gamma = gamma + square
                energy = energy + c * square
        return gamma, energy

    gamma, energy = lax.fori_loop(0, nrow // room, pair, (zero, zero))
    respond(block, load, gamma, energy, answer, last=last)


def list_kernel(first, keep, known, comp, mine, theirs, *refs):
    if first:
        r_in, r, d, x, s = refs
    else:
        r_in, d_in, x_in, s_in, r, d, x, s = refs
    npatch, nh, ncase, width = r.shape
    alpha = jnp.broadcast_to(known[:, 1:2], (ncase, width))
    beta = jnp.broadcast_to(known[:, 2:3], (ncase, width))

    def body(p, carry):
        on, row = keep[p], comp[pl.ds(p, 1), :]
        for h in range(nh):
            residual = r_in[p, h]
            c = row[:, h * width : (h + 1) * width]
            image = on * (mine[p, h] + theirs[p, h] + c * residual)
            if first:
                direction, moved = residual, alpha * residual
            else:
                direction = residual + beta * d_in[p, h]
                image = image + beta * s_in[p, h]
                moved = x_in[p, h] + alpha * direction
            r[p, h], d[p, h], x[p, h], s[p, h] = residual - alpha * image, direction, moved, image
        return carry

    lax.fori_loop(0, npatch, body, 0, unroll=4)


def end_kernel(keep, sums, known, comp, mine, theirs, r_in, d_in, x_in, s_in, out, moved):
    npatch, nh, ncase, width = r_in.shape
    total = sums[0]
    for i in range(1, sums.shape[0]):
        total = total + sums[i]
    _, alpha, beta = steps(False, total, known[...])
    one, two = jnp.broadcast_to(alpha, (ncase, width)), jnp.broadcast_to(beta, (ncase, width))
    alpha = jnp.broadcast_to(known[:, 1:2], (ncase, width))
    beta = jnp.broadcast_to(known[:, 2:3], (ncase, width))

    def body(p, carry):
        on, row = keep[p], comp[pl.ds(p, 1), :]
        for h in range(nh):
            residual = r_in[p, h]
            c = row[:, h * width : (h + 1) * width]
            image = on * (mine[p, h] + theirs[p, h] + c * residual) + beta * s_in[p, h]
            direction = residual + beta * d_in[p, h]
            residual = residual - alpha * image
            moved[h, p] = x_in[p, h] + alpha * direction + one * (residual + two * direction)
        return carry

    lax.fori_loop(0, npatch, body, 0, unroll=4)
    for h in range(nh):
        out[:, :, h * width : (h + 1) * width] = jnp.swapaxes(moved[h], 0, 1)


def on_device(rhs, compliance, plate_owner, found_owner, slot_pairs, active, inverse):
    nsub = lax.axis_size("sub")
    nbody = lax.axis_size("body")
    side = lax.axis_index("body")
    me = lax.axis_index("sub")
    ncase, npatch, gap = rhs.shape
    block = inverse[0, 0]
    nslot = block.shape[0] // gap
    nh = gap // LANES
    per = nslot * nh + 1
    room = max(2, 2 * npatch // nsub)
    nrow = nsub * room
    lines = -(-room * nh // SUBLANES)
    deep = -(-room // SUBLANES)
    tiles = room * nh + lines + deep
    nz = nsub // 4
    width = math.isqrt(nsub)

    def swap(value, far):
        return lax.ppermute(value, "sub", [(i, i ^ far) for i in range(nsub)])

    def cross(value, far_0, far_1):
        pairs = [(b * nsub + i, b * nsub + (i ^ far)) for b, far in enumerate((far_0, far_1)) for i in range(nsub)]
        return lax.ppermute(value, ("body", "sub"), pairs)

    def sibling(value):
        return lax.ppermute(value, "body", [(i, nbody - 1 - i) for i in range(nbody)])

    keep = active.astype(jnp.float32)
    plate, foundation = plate_owner[:, 0], found_owner[:, 0]
    owner, other = jnp.where(side == 0, plate, foundation), jnp.where(side == 0, foundation, plate)
    slot, other_slot = (jnp.where(side == i, slot_pairs[:, 0], slot_pairs[:, 1]) for i in range(2))
    index = jnp.arange(npatch, dtype=jnp.int32)
    earlier = (owner[None, :] == owner[:, None]) & (index[None, :] < index[:, None])
    rank = jnp.sum(earlier.astype(jnp.int32), axis=1)
    away = owner ^ me
    high, low = away // width, away % width
    order = jnp.where(side == 0, high * width + low, low * width + high)
    place = order * tiles + rank * nh

    def found(away):
        x_bit, y_bit, z_part = away & 1, (away >> 1) & 1, away >> 2
        plane = jnp.where(side == 0, y_bit * 2 + x_bit, x_bit * 2 + y_bit)
        return (plane * nz + z_part) * per + other_slot * nh

    facts = jnp.stack([slot * nh, found(owner ^ other)], axis=1).astype(jnp.float32)
    facts = jnp.concatenate([facts, keep[:, None]], axis=1)
    facts = jnp.concatenate([compliance, jnp.pad(facts, ((0, 0), (0, LANES - 3)))], axis=1)
    row = order * room + rank
    placed = (row[None, :] == jnp.arange(nrow, dtype=jnp.int32)[:, None]).astype(jnp.float32)
    facts = jnp.dot(placed, facts, precision=lax.Precision.HIGHEST).reshape(nsub, room, gap + LANES)
    lined = facts[:, :, :gap].reshape(nsub, room * nh, LANES)
    lined = jnp.pad(lined, ((0, 0), (0, lines * SUBLANES - room * nh), (0, 0)))
    named = jnp.pad(facts[:, :, gap:], ((0, 0), (0, deep * SUBLANES - room), (0, 0)))
    table = jnp.concatenate([lined, named], axis=1).reshape(nsub, lines + deep, SUBLANES, LANES)
    start = (keep[None, :, None] * rhs).reshape(ncase, npatch, nh, LANES)
    start = jnp.transpose(start, (1, 2, 0, 3))
    picked = found(me ^ other).astype(jnp.int32)
    place, picked = lax.optimization_barrier((place, picked))

    packed = call(
        functools.partial(pack_kernel, nh, tiles),
        (f32(width * tiles, ncase, LANES),) * width,
        [SMEM, VMEM, VMEM],
        place,
        start,
        table,
        scratch=[pltpu.VMEM((nsub * tiles, ncase, LANES), jnp.float32)],
    )
    near_parts = [packed[0]] + [cross(packed[i], i * width, i) for i in range(1, width)]
    block = call(
        block_kernel,
        jax.ShapeDtypeStruct(block.shape, block.dtype),
        [HBM],
        pltpu.with_memory_space_constraint(block, pltpu.HBM),
        scratch=[pltpu.SemaphoreType.DMA((nslot,))],
        cost=pl.CostEstimate(flops=0, bytes_accessed=4 * block.size, transcendentals=0),
    )
    near_parts, block = lax.optimization_barrier((near_parts, block))
    far_parts = [
        cross(jnp.concatenate([part[k * tiles : (k + 1) * tiles] for part in near_parts]), k, k * width)
        for k in range(1, width)
    ]

    field = f32(nrow, nh, ncase, LANES)
    answer = f32(per, ncase, LANES)
    load = pltpu.VMEM((nslot * nh, ncase, LANES), jnp.float32)
    spread = pltpu.VMEM((nsub * per, ncase, LANES), jnp.float32)
    near, far, on, home_r, comp, own = pl.pallas_call(
        functools.partial(start_kernel, nh, room, lines, tiles, width),
        out_shape=(jax.ShapeDtypeStruct((nrow,), jnp.int32),) * 2
        + (f32(nrow), field, f32(nsub * lines, ncase, LANES), answer),
        in_specs=[VMEM] * (2 * width),
        out_specs=(SMEM,) * 3 + (VMEM,) * 3,
        scratch_shapes=[
            load,
            pltpu.SMEM((nsub, deep, SUBLANES, LANES), jnp.float32),
            pltpu.SemaphoreType.DMA((nsub,)),
        ],
        compiler_params=PARAMS,
    )(block, *near_parts, *far_parts)
    def update(step, lists, known, part):
        return call(
            functools.partial(list_kernel, step == 0),
            (f32(npatch, nh, ncase, LANES),) * 4,
            [SMEM] + [VMEM] * (4 + len(lists)),
            keep,
            known,
            compliance,
            part,
            sibling(part),
            *lists,
            cost=pl.CostEstimate(flops=16 * rhs.size, bytes_accessed=44 * rhs.size, transcendentals=0),
        )

    known = jnp.zeros((ncase, LANES), jnp.float32)
    state = [home_r]
    lists = [start]
    for step in range(ITERS - 1):
        last = step == ITERS - 2
        spread_out = sibling(own)
        if step > 0:
            spread_out, part = lax.optimization_barrier((spread_out, part))
            lists = update(step - 1, lists, known, part)
        spread_out = jnp.concatenate([spread_out[: per - 1], own[per - 1 :] + spread_out[per - 1 :]])
        parts = [spread_out] + [swap(spread_out, 4 * z) for z in range(1, nz)]
        close = jnp.concatenate(parts)
        close = jnp.concatenate([close, cross(close, 1, 2)])
        apart = cross(close, 2, 1)
        if step > 0:
            apart, lists = lax.optimization_barrier((apart, lists))
        *state, own, part, known = call(
            functools.partial(home_kernel, step == 0, last, nh, room, lines),
            (field,) * (0 if last else 2) + (f32(nbody * nsub, ncase, LANES) if last else answer, f32(npatch, nh, ncase, LANES), f32(ncase, LANES)),
            [SMEM] * 4 + [VMEM] * (6 + len(state)),
            near,
            far,
            on,
            picked,
            comp,
            own,
            close,
            apart,
            known,
            block,
            *state,
            scratch=[load, spread],
        )
    sums = lax.all_to_all(own, ("body", "sub"), split_axis=0, concat_axis=0, tiled=True)
    return call(
        end_kernel,
        f32(ncase, npatch, gap),
        [SMEM] + [VMEM] * 9,
        keep,
        sums,
        known,
        compliance,
        part,
        sibling(part),
        *lists,
        scratch=[pltpu.VMEM((nh, npatch, ncase, LANES), jnp.float32)],
    )


def solution(mesh):
    in_specs = (
        P(None, "sub", None),
        P("sub", None),
        P("sub", None),
        P("sub", None),
        P("sub", None),
        P("sub"),
        P("body", "sub", None, None),
    )
    out_specs = P(None, "sub", None)
    return jax.shard_map(
        on_device, mesh=mesh, in_specs=in_specs, out_specs=out_specs, check_vma=False
    )
```

```python
import functools
import math

import jax
import jax.numpy as jnp
from jax import lax
from jax.experimental import pallas as pl
from jax.experimental.pallas import tpu as pltpu
from jax.sharding import PartitionSpec as P

ITERS = 4
LANES = 128
SUBLANES = 8
VMEM = pl.BlockSpec(memory_space=pltpu.VMEM)
SMEM = pl.BlockSpec(memory_space=pltpu.SMEM)
HBM = pl.BlockSpec(memory_space=pltpu.HBM)
PARAMS = pltpu.CompilerParams(vmem_limit_bytes=16 * 1024 * 1024)


def f32(*shape):
    return jax.ShapeDtypeStruct(shape, jnp.float32)


def call(kernel, out_shape, specs, *operands, scratch=(), cost=None):
    several = isinstance(out_shape, (tuple, list))
    return pl.pallas_call(
        kernel,
        out_shape=tuple(out_shape) if several else out_shape,
        in_specs=specs,
        out_specs=(VMEM,) * len(out_shape) if several else VMEM,
        scratch_shapes=list(scratch),
        compiler_params=PARAMS,
        cost_estimate=cost,
    )(*operands)


def per_case(value):
    return jnp.sum(value, axis=1, keepdims=True)


def respond(block, load, gamma, energy, answer, last=False):
    ntile, ncase, width = load.shape
    each = 2
    total = jnp.zeros((2 * ncase, ntile * width), jnp.float32)
    for j in range(ntile // each):
        value = jnp.concatenate([load[j * each + i] for i in range(each)], axis=1)
        high = value.astype(jnp.bfloat16)
        low = (value - high.astype(jnp.float32)).astype(jnp.bfloat16)
        total = total + jnp.dot(
            jnp.concatenate([high, low], axis=0),
            block[j * each * width : (j + 1) * each * width, :],
            preferred_element_type=jnp.float32,
        )
    total = total[:ncase] + total[ncase:]
    work = 0.5 * energy
    for i in range(ntile):
        tile = total[:, i * width : (i + 1) * width]
        if not last:
            answer[i] = tile
        work = work + load[i] * tile
    lane = lax.broadcasted_iota(jnp.int32, work.shape, 1)
    sums = jnp.where(lane == 0, per_case(0.5 * gamma), 0.0)
    sums = jnp.where(lane == 1, per_case(work), sums)
    if last:
        answer[...] = jnp.broadcast_to(sums[None], answer.shape)
    else:
        answer[ntile] = sums


def pack_kernel(nh, tiles, place, field, table, *refs):
    *outs, whole = refs
    extra = table.shape[1]
    whole[...] = jnp.zeros_like(whole)

    def body(p, carry):
        whole[pl.ds(place[p], nh)] = field[p]
        return carry

    lax.fori_loop(0, field.shape[0], body, 0, unroll=4)
    for i, out in enumerate(outs):
        for k in range(len(outs)):
            owner = i * len(outs) + k
            out[k * tiles : (k + 1) * tiles - extra] = whole[owner * tiles : (owner + 1) * tiles - extra]
            out[(k + 1) * tiles - extra : (k + 1) * tiles] = table[owner]


def block_kernel(block, held, sems):
    pieces = sems.shape[0]
    size = block.shape[0] // pieces
    copies = []
    for j in range(pieces):
        rows = pl.ds(j * size, size)
        copies.append(pltpu.make_async_copy(block.at[rows], held.at[rows], sems.at[j]))
        copies[-1].start()
    for copy in copies:
        copy.wait()


def start_kernel(nh, room, lines, tiles, side, block, *refs):
    near_parts, refs = refs[:side], refs[side:]
    far_parts, refs = refs[: side - 1], refs[side - 1 :]
    near, far, on, r_out, comp, answer, load, facts, sems = refs
    blocks = [
        (near_parts[i], 0) if k == 0 else (far_parts[k - 1], i * tiles) for i in range(side) for k in range(side)
    ]
    copies = []
    for i, (part, at) in enumerate(blocks):
        rows = pl.ds(at + room * nh + lines, tiles - room * nh - lines)
        copies.append(pltpu.make_async_copy(part.at[rows], facts.at[i], sems.at[i]))
        copies[-1].start()
    load[...] = jnp.zeros_like(load)
    gamma = energy = jnp.zeros(r_out.shape[2:], jnp.float32)
    for i, (part, at) in enumerate(blocks):
        at_comp = at + room * nh
        comp[i * lines : (i + 1) * lines] = part[at_comp : at_comp + lines]
        copies[i].wait()
        for j in range(room):
            row = i * room + j
            slot = facts[i, j // SUBLANES, j % SUBLANES, 0].astype(jnp.int32)
            near[row] = slot
            far[row] = facts[i, j // SUBLANES, j % SUBLANES, 1].astype(jnp.int32)
            on[row] = facts[i, j // SUBLANES, j % SUBLANES, 2]
            r = part[at + j * nh : at + (j + 1) * nh]
            r_out[row] = r
            load[pl.ds(slot, nh)] += r
            for h in range(nh):
                line, sub = divmod(j * nh + h, SUBLANES)
                square = r[h] * r[h]
                gamma = gamma + square
                energy = energy + part[at_comp + line, sub : sub + 1, :] * square
    respond(block, load, gamma, energy, answer)


def tree(values):
    while len(values) > 1:
        values = [a + b for a, b in zip(values[::2], values[1::2])]
    return values[0]


def steps(first, sums, known):
    gamma, delta = sums[:, 0:1], sums[:, 1:2]
    if first:
        return gamma, gamma / delta, jnp.zeros_like(gamma)
    beta = gamma / known[:, 0:1]
    return gamma, gamma / (delta - beta * gamma / known[:, 1:2]), beta


def home_kernel(first, last, nh, room, lines, place, away, keep, picked, comp, own, near_a, far_a, near_b, far_b, known, block, *refs):
    r_in, *refs = refs
    if not first:
        s_in, *refs = refs
    if not last:
        r, s, *refs = refs
    answer, part, known_out, load, resp = refs
    load[...] = jnp.zeros_like(load)
    nrow, _, ncase, width = r_in.shape
    at = 0
    for piece in (near_a, far_a, near_b, far_b):
        resp[at : at + piece.shape[0]] = piece[...]
        at += piece.shape[0]
    each = own.shape[0] // 2 + 1
    sums = tree([piece[i + each - 1] for piece in (near_b, far_b) for i in range(0, piece.shape[0], each)])
    gamma, alpha, beta = steps(first, sums, known[...])
    lane = lax.broadcasted_iota(jnp.int32, (ncase, width), 1)
    known_out[...] = jnp.where(lane == 0, gamma, jnp.where(lane == 1, alpha, beta))
    alpha = jnp.broadcast_to(alpha, (ncase, width))
    beta = jnp.broadcast_to(beta, (ncase, width))
    zero = jnp.zeros((ncase, width), jnp.float32)

    def pick(p, carry):
        part[p] = resp[pl.ds(picked[p], nh)]
        return carry

    lax.fori_loop(0, part.shape[0], pick, 0, unroll=8)

    def pair(i, sums):
        gamma, energy = sums
        for j in range(room):
            row = i * room + j
            close, apart, on = place[row], away[row], keep[row]
            for h in range(nh):
                line, sub = divmod(j * nh + h, SUBLANES)
                c = comp[i * lines + line, sub : sub + 1, :]
                residual = r_in[row, h]
                image = on * (own[close + h] + resp[apart + h] + c * residual)
                if not first:
                    image = image + beta * s_in[row, h]
                residual = residual - alpha * image
                if not last:
                    r[row, h], s[row, h] = residual, image
                load[close + h] += residual
                square = residual * residual
                gamma = gamma + square
                energy = energy + c * square
        return gamma, energy

    gamma, energy = lax.fori_loop(0, nrow // room, pair, (zero, zero))
    respond(block, load, gamma, energy, answer, last=last)


def list_kernel(first, keep, known, comp, mine, theirs, *refs):
    if first:
        r_in, r, d, x, s = refs
    else:
        r_in, d_in, x_in, s_in, r, d, x, s = refs
    npatch, nh, ncase, width = r.shape
    alpha = jnp.broadcast_to(known[:, 1:2], (ncase, width))
    beta = jnp.broadcast_to(known[:, 2:3], (ncase, width))

    def body(p, carry):
        on, row = keep[p], comp[pl.ds(p, 1), :]
        for h in range(nh):
            residual = r_in[p, h]
            c = row[:, h * width : (h + 1) * width]
            image = on * (mine[p, h] + theirs[p, h] + c * residual)
            if first:
                direction, moved = residual, alpha * residual
            else:
                direction = residual + beta * d_in[p, h]
                image = image + beta * s_in[p, h]
                moved = x_in[p, h] + alpha * direction
            r[p, h], d[p, h], x[p, h], s[p, h] = residual - alpha * image, direction, moved, image
        return carry

    lax.fori_loop(0, npatch, body, 0, unroll=4)


def end_kernel(keep, sums, known, comp, mine, theirs, r_in, d_in, x_in, s_in, out, moved):
    npatch, nh, ncase, width = r_in.shape
    total = sums[0]
    for i in range(1, sums.shape[0]):
        total = total + sums[i]
    _, alpha, beta = steps(False, total, known[...])
    one, two = jnp.broadcast_to(alpha, (ncase, width)), jnp.broadcast_to(beta, (ncase, width))
    alpha = jnp.broadcast_to(known[:, 1:2], (ncase, width))
    beta = jnp.broadcast_to(known[:, 2:3], (ncase, width))

    def body(p, carry):
        on, row = keep[p], comp[pl.ds(p, 1), :]
        for h in range(nh):
            residual = r_in[p, h]
            c = row[:, h * width : (h + 1) * width]
            image = on * (mine[p, h] + theirs[p, h] + c * residual) + beta * s_in[p, h]
            direction = residual + beta * d_in[p, h]
            residual = residual - alpha * image
            moved[h, p] = x_in[p, h] + alpha * direction + one * (residual + two * direction)
        return carry

    lax.fori_loop(0, npatch, body, 0, unroll=4)
    for h in range(nh):
        out[:, :, h * width : (h + 1) * width] = jnp.swapaxes(moved[h], 0, 1)


def on_device(rhs, compliance, plate_owner, found_owner, slot_pairs, active, inverse):
    nsub = lax.axis_size("sub")
    nbody = lax.axis_size("body")
    side = lax.axis_index("body")
    me = lax.axis_index("sub")
    ncase, npatch, gap = rhs.shape
    block = inverse[0, 0]
    nslot = block.shape[0] // gap
    nh = gap // LANES
    per = nslot * nh + 1
    room = max(2, 2 * npatch // nsub)
    nrow = nsub * room
    lines = -(-room * nh // SUBLANES)
    deep = -(-room // SUBLANES)
    tiles = room * nh + lines + deep
    nz = nsub // 4
    half = nslot // 2 * nh
    width = math.isqrt(nsub)

    def swap(value, far):
        return lax.ppermute(value, "sub", [(i, i ^ far) for i in range(nsub)])

    def cross(value, far_0, far_1):
        pairs = [(b * nsub + i, b * nsub + (i ^ far)) for b, far in enumerate((far_0, far_1)) for i in range(nsub)]
        return lax.ppermute(value, ("body", "sub"), pairs)

    def sibling(value):
        return lax.ppermute(value, "body", [(i, nbody - 1 - i) for i in range(nbody)])

    keep = active.astype(jnp.float32)
    plate, foundation = plate_owner[:, 0], found_owner[:, 0]
    owner, other = jnp.where(side == 0, plate, foundation), jnp.where(side == 0, foundation, plate)
    slot, other_slot = (jnp.where(side == i, slot_pairs[:, 0], slot_pairs[:, 1]) for i in range(2))
    index = jnp.arange(npatch, dtype=jnp.int32)
    earlier = (owner[None, :] == owner[:, None]) & (index[None, :] < index[:, None])
    rank = jnp.sum(earlier.astype(jnp.int32), axis=1)
    away = owner ^ me
    high, low = away // width, away % width
    order = jnp.where(side == 0, high * width + low, low * width + high)
    place = order * tiles + rank * nh

    def found(away):
        x_bit, y_bit, z_part = away & 1, (away >> 1) & 1, away >> 2
        found_a = ((y_bit * 2 + x_bit) * nz + z_part) * half + other_slot * nh
        found_b = ((x_bit * 2 + y_bit) * nz + z_part) * (half + 1) + (other_slot - nslot // 2) * nh
        return jnp.where(other_slot < nslot // 2, found_a, nsub * half + found_b)

    facts = jnp.stack([slot * nh, found(owner ^ other)], axis=1).astype(jnp.float32)
    facts = jnp.concatenate([facts, keep[:, None]], axis=1)
    facts = jnp.concatenate([compliance, jnp.pad(facts, ((0, 0), (0, LANES - 3)))], axis=1)
    row = order * room + rank
    placed = (row[None, :] == jnp.arange(nrow, dtype=jnp.int32)[:, None]).astype(jnp.float32)
    facts = jnp.dot(placed, facts, precision=lax.Precision.HIGHEST).reshape(nsub, room, gap + LANES)
    lined = facts[:, :, :gap].reshape(nsub, room * nh, LANES)
    lined = jnp.pad(lined, ((0, 0), (0, lines * SUBLANES - room * nh), (0, 0)))
    named = jnp.pad(facts[:, :, gap:], ((0, 0), (0, deep * SUBLANES - room), (0, 0)))
    table = jnp.concatenate([lined, named], axis=1).reshape(nsub, lines + deep, SUBLANES, LANES)
    start = (keep[None, :, None] * rhs).reshape(ncase, npatch, nh, LANES)
    start = jnp.transpose(start, (1, 2, 0, 3))
    picked = found(me ^ other).astype(jnp.int32)
    place, picked = lax.optimization_barrier((place, picked))

    packed = call(
        functools.partial(pack_kernel, nh, tiles),
        (f32(width * tiles, ncase, LANES),) * width,
        [SMEM, VMEM, VMEM],
        place,
        start,
        table,
        scratch=[pltpu.VMEM((nsub * tiles, ncase, LANES), jnp.float32)],
    )
    near_parts = [packed[0]] + [cross(packed[i], i * width, i) for i in range(1, width)]
    block = call(
        block_kernel,
        jax.ShapeDtypeStruct(block.shape, block.dtype),
        [HBM],
        pltpu.with_memory_space_constraint(block, pltpu.HBM),
        scratch=[pltpu.SemaphoreType.DMA((nslot,))],
        cost=pl.CostEstimate(flops=0, bytes_accessed=4 * block.size, transcendentals=0),
    )
    near_parts, block = lax.optimization_barrier((near_parts, block))
    signal = sibling(near_parts[width - 1][:1])
    far_parts = [
        cross(jnp.concatenate([part[k * tiles : (k + 1) * tiles] for part in near_parts] + [signal]), k, k * width)
        for k in range(1, width)
    ]

    field = f32(nrow, nh, ncase, LANES)
    answer = f32(per, ncase, LANES)
    load = pltpu.VMEM((nslot * nh, ncase, LANES), jnp.float32)
    spread = pltpu.VMEM((nsub * per, ncase, LANES), jnp.float32)
    near, far, on, home_r, comp, own = pl.pallas_call(
        functools.partial(start_kernel, nh, room, lines, tiles, width),
        out_shape=(jax.ShapeDtypeStruct((nrow,), jnp.int32),) * 2
        + (f32(nrow), field, f32(nsub * lines, ncase, LANES), answer),
        in_specs=[VMEM] * (2 * width),
        out_specs=(SMEM,) * 3 + (VMEM,) * 3,
        scratch_shapes=[
            load,
            pltpu.SMEM((nsub, deep, SUBLANES, LANES), jnp.float32),
            pltpu.SemaphoreType.DMA((nsub,)),
        ],
        compiler_params=PARAMS,
    )(block, *near_parts, *far_parts)
    def update(step, lists, known, part):
        return call(
            functools.partial(list_kernel, step == 0),
            (f32(npatch, nh, ncase, LANES),) * 4,
            [SMEM] + [VMEM] * (4 + len(lists)),
            keep,
            known,
            compliance,
            part,
            sibling(part),
            *lists,
            cost=pl.CostEstimate(flops=16 * rhs.size, bytes_accessed=44 * rhs.size, transcendentals=0),
        )

    known = jnp.zeros((ncase, LANES), jnp.float32)
    state = [home_r]
    lists = [start]
    for step in range(ITERS - 1):
        last = step == ITERS - 2
        spread_out = sibling(own)
        if step > 0:
            spread_out, part = lax.optimization_barrier((spread_out, part))
            lists = update(step - 1, lists, known, part)
        spread_out = jnp.concatenate([spread_out[: per - 1], own[per - 1 :] + spread_out[per - 1 :]])
        parts = [spread_out] + [swap(spread_out, 4 * z) for z in range(1, nz)]
        a = jnp.concatenate([part[:half] for part in parts])
        b = jnp.concatenate([part[half:] for part in parts])
        far_a, far_b = swap(a, 1), swap(b, 2)
        a, b = jnp.concatenate([a, far_a]), jnp.concatenate([b, far_b])
        far_a, far_b = swap(a, 2), swap(b, 1)
        if step > 0:
            far_a, far_b, lists = lax.optimization_barrier((far_a, far_b, lists))
        *state, own, part, known = call(
            functools.partial(home_kernel, step == 0, last, nh, room, lines),
            (field,) * (0 if last else 2) + (f32(nbody * nsub, ncase, LANES) if last else answer, f32(npatch, nh, ncase, LANES), f32(ncase, LANES)),
            [SMEM] * 4 + [VMEM] * (8 + len(state)),
            near,
            far,
            on,
            picked,
            comp,
            own,
            a,
            far_a,
            b,
            far_b,
            known,
            block,
            *state,
            scratch=[load, spread],
        )
    sums = lax.all_to_all(own, ("body", "sub"), split_axis=0, concat_axis=0, tiled=True)
    return call(
        end_kernel,
        f32(ncase, npatch, gap),
        [SMEM] + [VMEM] * 9,
        keep,
        sums,
        known,
        compliance,
        part,
        sibling(part),
        *lists,
        scratch=[pltpu.VMEM((nh, npatch, ncase, LANES), jnp.float32)],
    )


def solution(mesh):
    in_specs = (
        P(None, "sub", None),
        P("sub", None),
        P("sub", None),
        P("sub", None),
        P("sub", None),
        P("sub"),
        P("body", "sub", None, None),
    )
    out_specs = P(None, "sub", None)
    return jax.shard_map(
        on_device, mesh=mesh, in_specs=in_specs, out_specs=out_specs, check_vma=False
    )
```

```python
import functools

import jax
import jax.numpy as jnp
from jax import lax
from jax.experimental import pallas as pl
from jax.experimental.pallas import tpu as pltpu
from jax.sharding import PartitionSpec as P

ITERS = 4
LANES = 128
SUBLANES = 8
VMEM = pl.BlockSpec(memory_space=pltpu.VMEM)
SMEM = pl.BlockSpec(memory_space=pltpu.SMEM)
HBM = pl.BlockSpec(memory_space=pltpu.HBM)
PARAMS = pltpu.CompilerParams(vmem_limit_bytes=16 * 1024 * 1024)


def f32(*shape):
    return jax.ShapeDtypeStruct(shape, jnp.float32)


def call(kernel, out_shape, specs, *operands, scratch=(), cost=None):
    several = isinstance(out_shape, (tuple, list))
    return pl.pallas_call(
        kernel,
        out_shape=tuple(out_shape) if several else out_shape,
        in_specs=specs,
        out_specs=(VMEM,) * len(out_shape) if several else VMEM,
        scratch_shapes=list(scratch),
        compiler_params=PARAMS,
        cost_estimate=cost,
    )(*operands)


def per_case(value):
    return jnp.sum(value, axis=1, keepdims=True)


def respond(block, load, gamma, energy, answer, last=False):
    ntile, ncase, width = load.shape
    each = 2
    total = jnp.zeros((2 * ncase, ntile * width), jnp.float32)
    for j in range(ntile // each):
        value = jnp.concatenate([load[j * each + i] for i in range(each)], axis=1)
        high = value.astype(jnp.bfloat16)
        low = (value - high.astype(jnp.float32)).astype(jnp.bfloat16)
        total = total + jnp.dot(
            jnp.concatenate([high, low], axis=0),
            block[j * each * width : (j + 1) * each * width, :],
            preferred_element_type=jnp.float32,
        )
    total = total[:ncase] + total[ncase:]
    work = 0.5 * energy
    for i in range(ntile):
        tile = total[:, i * width : (i + 1) * width]
        if not last:
            answer[i] = tile
        work = work + load[i] * tile
    lane = lax.broadcasted_iota(jnp.int32, work.shape, 1)
    sums = jnp.where(lane == 0, per_case(0.5 * gamma), 0.0)
    sums = jnp.where(lane == 1, per_case(work), sums)
    if last:
        answer[...] = jnp.broadcast_to(sums[None], answer.shape)
    else:
        answer[ntile] = sums


def pack_kernel(nh, nz, by_z, place, field, *refs):
    if not by_z:
        table, *refs = refs
    *outs, whole = refs
    tiles = whole.shape[0] // (4 * nz + 1)
    whole[...] = jnp.zeros_like(whole)

    def body(p, carry):
        whole[pl.ds(place[p], nh)] = field[p]
        return carry

    lax.fori_loop(0, field.shape[0], body, 0, unroll=4)
    for i, out in enumerate(outs):
        size = out.shape[0] // (4 * nz // len(outs))
        for k in range(out.shape[0] // size):
            owner = i * 4 + k if by_z else k * 4 + i
            out[k * size : k * size + tiles] = whole[owner * tiles : (owner + 1) * tiles]
            if not by_z:
                out[k * size + tiles : (k + 1) * size] = table[owner]


def block_kernel(block, held, sems):
    pieces = sems.shape[0]
    size = block.shape[0] // pieces
    copies = []
    for j in range(pieces):
        rows = pl.ds(j * size, size)
        copies.append(pltpu.make_async_copy(block.at[rows], held.at[rows], sems.at[j]))
        copies[-1].start()
    for copy in copies:
        copy.wait()


def start_kernel(nh, cut, room, lines, extra, nz, block, *refs):
    a_z, refs = refs[:nz], refs[nz:]
    a_far, refs = refs[:3], refs[3:]
    b_near, refs = refs[:4], refs[4:]
    b_far, refs = refs[: nz - 1], refs[nz - 1 :]
    near, far, on, r_out, comp, answer, load, facts, sems = refs
    first, second = cut * nh, (room - cut) * nh
    blocks = []
    for z in range(nz):
        for m in range(4):
            one = (a_z[z], 0) if m == 0 else (a_far[m - 1], z * first)
            two = (b_near[m], 0) if z == 0 else (b_far[z - 1], m * (second + extra))
            blocks.append((*one, *two))
    copies = []
    for i, (_, _, two, at_two) in enumerate(blocks):
        rows = pl.ds(at_two + second + lines, extra - lines)
        copies.append(pltpu.make_async_copy(two.at[rows], facts.at[i], sems.at[i]))
        copies[-1].start()
    load[...] = jnp.zeros_like(load)
    gamma = energy = jnp.zeros(r_out.shape[2:], jnp.float32)
    for i, (one, at_one, two, at_two) in enumerate(blocks):
        at_comp = at_two + second
        comp[i * lines : (i + 1) * lines] = two[at_comp : at_comp + lines]
        copies[i].wait()
        for j in range(room):
            row = i * room + j
            slot = facts[i, j // SUBLANES, j % SUBLANES, 0].astype(jnp.int32)
            near[row] = slot
            far[row] = facts[i, j // SUBLANES, j % SUBLANES, 1].astype(jnp.int32)
            on[row] = facts[i, j // SUBLANES, j % SUBLANES, 2]
            if j < cut:
                r = one[at_one + j * nh : at_one + (j + 1) * nh]
            else:
                r = two[at_two + (j - cut) * nh : at_two + (j - cut + 1) * nh]
            r_out[row] = r
            load[pl.ds(slot, nh)] += r
            for h in range(nh):
                line, sub = divmod(j * nh + h, SUBLANES)
                square = r[h] * r[h]
                gamma = gamma + square
                energy = energy + two[at_comp + line, sub : sub + 1, :] * square
    respond(block, load, gamma, energy, answer)


def tree(values):
    while len(values) > 1:
        values = [a + b for a, b in zip(values[::2], values[1::2])]
    return values[0]


def steps(first, sums, known):
    gamma, delta = sums[:, 0:1], sums[:, 1:2]
    if first:
        return gamma, gamma / delta, jnp.zeros_like(gamma)
    beta = gamma / known[:, 0:1]
    return gamma, gamma / (delta - beta * gamma / known[:, 1:2]), beta


def home_kernel(first, last, nh, room, lines, place, away, keep, picked, comp, own, near_a, far_a, near_b, far_b, known, block, *refs):
    r_in, *refs = refs
    if not first:
        s_in, *refs = refs
    if not last:
        r, s, *refs = refs
    answer, part, known_out, load, resp = refs
    load[...] = jnp.zeros_like(load)
    nrow, _, ncase, width = r_in.shape
    at = 0
    for piece in (near_a, far_a, near_b, far_b):
        resp[at : at + piece.shape[0]] = piece[...]
        at += piece.shape[0]
    each = own.shape[0] // 2 + 1
    sums = tree([piece[i + each - 1] for piece in (near_b, far_b) for i in range(0, piece.shape[0], each)])
    gamma, alpha, beta = steps(first, sums, known[...])
    lane = lax.broadcasted_iota(jnp.int32, (ncase, width), 1)
    known_out[...] = jnp.where(lane == 0, gamma, jnp.where(lane == 1, alpha, beta))
    alpha = jnp.broadcast_to(alpha, (ncase, width))
    beta = jnp.broadcast_to(beta, (ncase, width))
    zero = jnp.zeros((ncase, width), jnp.float32)

    def pick(p, carry):
        part[p] = resp[pl.ds(picked[p], nh)]
        return carry

    lax.fori_loop(0, part.shape[0], pick, 0, unroll=8)

    def pair(i, sums):
        gamma, energy = sums
        for j in range(room):
            row = i * room + j
            near, far, on = place[row], away[row], keep[row]
            for h in range(nh):
                line, sub = divmod(j * nh + h, SUBLANES)
                c = comp[i * lines + line, sub : sub + 1, :]
                residual = r_in[row, h]
                image = on * (own[near + h] + resp[far + h] + c * residual)
                if not first:
                    image = image + beta * s_in[row, h]
                residual = residual - alpha * image
                if not last:
                    r[row, h], s[row, h] = residual, image
                load[near + h] += residual
                square = residual * residual
                gamma = gamma + square
                energy = energy + c * square
        return gamma, energy

    gamma, energy = lax.fori_loop(0, nrow // room, pair, (zero, zero))
    respond(block, load, gamma, energy, answer, last=last)


def list_kernel(first, keep, known, comp, mine, theirs, *refs):
    if first:
        r_in, r, d, x, s = refs
    else:
        r_in, d_in, x_in, s_in, r, d, x, s = refs
    npatch, nh, ncase, width = r.shape
    alpha = jnp.broadcast_to(known[:, 1:2], (ncase, width))
    beta = jnp.broadcast_to(known[:, 2:3], (ncase, width))

    def body(p, carry):
        on, row = keep[p], comp[pl.ds(p, 1), :]
        for h in range(nh):
            residual = r_in[p, h]
            c = row[:, h * width : (h + 1) * width]
            image = on * (mine[p, h] + theirs[p, h] + c * residual)
            if first:
                direction, moved = residual, alpha * residual
            else:
                direction = residual + beta * d_in[p, h]
                image = image + beta * s_in[p, h]
                moved = x_in[p, h] + alpha * direction
            r[p, h], d[p, h], x[p, h], s[p, h] = residual - alpha * image, direction, moved, image
        return carry

    lax.fori_loop(0, npatch, body, 0, unroll=4)


def end_kernel(keep, sums, known, comp, mine, theirs, r_in, d_in, x_in, s_in, out, moved):
    npatch, nh, ncase, width = r_in.shape
    total = sums[0]
    for i in range(1, sums.shape[0]):
        total = total + sums[i]
    _, alpha, beta = steps(False, total, known[...])
    one, two = jnp.broadcast_to(alpha, (ncase, width)), jnp.broadcast_to(beta, (ncase, width))
    alpha = jnp.broadcast_to(known[:, 1:2], (ncase, width))
    beta = jnp.broadcast_to(known[:, 2:3], (ncase, width))

    def body(p, carry):
        on, row = keep[p], comp[pl.ds(p, 1), :]
        for h in range(nh):
            residual = r_in[p, h]
            c = row[:, h * width : (h + 1) * width]
            image = on * (mine[p, h] + theirs[p, h] + c * residual) + beta * s_in[p, h]
            direction = residual + beta * d_in[p, h]
            residual = residual - alpha * image
            moved[h, p] = x_in[p, h] + alpha * direction + one * (residual + two * direction)
        return carry

    lax.fori_loop(0, npatch, body, 0, unroll=4)
    for h in range(nh):
        out[:, :, h * width : (h + 1) * width] = jnp.swapaxes(moved[h], 0, 1)


def on_device(rhs, compliance, plate_owner, found_owner, slot_pairs, active, inverse):
    nsub = lax.axis_size("sub")
    nbody = lax.axis_size("body")
    side = lax.axis_index("body")
    me = lax.axis_index("sub")
    ncase, npatch, gap = rhs.shape
    block = inverse[0, 0]
    nslot = block.shape[0] // gap
    nh = gap // LANES
    per = nslot * nh + 1
    room = max(2, 2 * npatch // nsub)
    nrow = nsub * room
    lines = -(-room * nh // SUBLANES)
    deep = -(-room // SUBLANES)
    extra = lines + deep
    cut = max(1, 5 * room // 8)
    first = cut * nh
    second = (room - cut) * nh + extra
    nz = nsub // 4
    half = nslot // 2 * nh

    def swap(value, far):
        return lax.ppermute(value, "sub", [(i, i ^ far) for i in range(nsub)])

    def sibling(value):
        return lax.ppermute(value, "body", [(i, nbody - 1 - i) for i in range(nbody)])

    keep = active.astype(jnp.float32)
    plate, foundation = plate_owner[:, 0], found_owner[:, 0]
    owner, other = jnp.where(side == 0, plate, foundation), jnp.where(side == 0, foundation, plate)
    slot, other_slot = (jnp.where(side == i, slot_pairs[:, 0], slot_pairs[:, 1]) for i in range(2))
    index = jnp.arange(npatch, dtype=jnp.int32)
    earlier = (owner[None, :] == owner[:, None]) & (index[None, :] < index[:, None])
    rank = jnp.sum(earlier.astype(jnp.int32), axis=1)
    base, none = owner ^ me, 4 * nz
    place_a = jnp.where(rank < cut, base * cut + rank, none * cut) * nh
    place_b = jnp.where(rank < cut, none * (room - cut), base * (room - cut) + rank - cut) * nh

    def found(away):
        x_bit, y_bit, z_part = away & 1, (away >> 1) & 1, away >> 2
        found_a = ((y_bit * 2 + x_bit) * nz + z_part) * half + other_slot * nh
        found_b = ((x_bit * 2 + y_bit) * nz + z_part) * (half + 1) + (other_slot - nslot // 2) * nh
        return jnp.where(other_slot < nslot // 2, found_a, nsub * half + found_b)

    facts = jnp.stack([slot * nh, found(owner ^ other)], axis=1).astype(jnp.float32)
    facts = jnp.concatenate([facts, keep[:, None]], axis=1)
    facts = jnp.concatenate([compliance, jnp.pad(facts, ((0, 0), (0, LANES - 3)))], axis=1)
    row = (owner ^ me) * room + rank
    placed = (row[None, :] == jnp.arange(nrow, dtype=jnp.int32)[:, None]).astype(jnp.float32)
    facts = jnp.dot(placed, facts, precision=lax.Precision.HIGHEST).reshape(nsub, room, gap + LANES)
    lined = facts[:, :, :gap].reshape(nsub, room * nh, LANES)
    lined = jnp.pad(lined, ((0, 0), (0, lines * SUBLANES - room * nh), (0, 0)))
    named = jnp.pad(facts[:, :, gap:], ((0, 0), (0, deep * SUBLANES - room), (0, 0)))
    table = jnp.concatenate([lined, named], axis=1).reshape(nsub, lines + deep, SUBLANES, LANES)
    start = (keep[None, :, None] * rhs).reshape(ncase, npatch, nh, LANES)
    start = jnp.transpose(start, (1, 2, 0, 3))
    picked = found(me ^ other).astype(jnp.int32)
    place_a, place_b, picked = lax.optimization_barrier((place_a, place_b, picked))

    a_z = call(
        functools.partial(pack_kernel, nh, nz, True),
        (f32(4 * first, ncase, LANES),) * nz,
        [SMEM, VMEM],
        place_a,
        start,
        scratch=[pltpu.VMEM(((nsub + 1) * cut * nh, ncase, LANES), jnp.float32)],
    )
    b_near = call(
        functools.partial(pack_kernel, nh, nz, False),
        (f32(nz * second, ncase, LANES),) * 4,
        [SMEM, VMEM, VMEM],
        place_b,
        start,
        table,
        scratch=[pltpu.VMEM(((nsub + 1) * (room - cut) * nh, ncase, LANES), jnp.float32)],
    )
    a_z = [a_z[0]] + [swap(a_z[z], 4 * z) for z in range(1, nz)]
    b_near = [b_near[0]] + [swap(b_near[m], m) for m in range(1, 4)]
    block = call(
        block_kernel,
        jax.ShapeDtypeStruct(block.shape, block.dtype),
        [HBM],
        pltpu.with_memory_space_constraint(block, pltpu.HBM),
        scratch=[pltpu.SemaphoreType.DMA((nslot,))],
        cost=pl.CostEstimate(flops=0, bytes_accessed=4 * block.size, transcendentals=0),
    )
    a_z, b_near, block = lax.optimization_barrier((a_z, b_near, block))
    b_far = [
        swap(jnp.concatenate([part[z * second : (z + 1) * second] for part in b_near]), 4 * z)
        for z in range(1, nz)
    ]
    a_far = [
        swap(jnp.concatenate([part[m * first : (m + 1) * first] for part in a_z]), m) for m in range(1, 4)
    ]
    field = f32(nrow, nh, ncase, LANES)
    answer = f32(per, ncase, LANES)
    load = pltpu.VMEM((nslot * nh, ncase, LANES), jnp.float32)
    spread = pltpu.VMEM((nsub * per, ncase, LANES), jnp.float32)
    near, far, on, home_r, comp, own = pl.pallas_call(
        functools.partial(start_kernel, nh, cut, room, lines, extra, nz),
        out_shape=(jax.ShapeDtypeStruct((nrow,), jnp.int32),) * 2
        + (f32(nrow), field, f32(nsub * lines, ncase, LANES), answer),
        in_specs=[VMEM] * (2 * nz + 7),
        out_specs=(SMEM,) * 3 + (VMEM,) * 3,
        scratch_shapes=[
            load,
            pltpu.SMEM((nsub, deep, SUBLANES, LANES), jnp.float32),
            pltpu.SemaphoreType.DMA((nsub,)),
        ],
        compiler_params=PARAMS,
    )(block, *a_z, *a_far, *b_near, *b_far)
    def update(step, lists, known, part):
        return call(
            functools.partial(list_kernel, step == 0),
            (f32(npatch, nh, ncase, LANES),) * 4,
            [SMEM] + [VMEM] * (4 + len(lists)),
            keep,
            known,
            compliance,
            part,
            sibling(part),
            *lists,
            cost=pl.CostEstimate(flops=16 * rhs.size, bytes_accessed=44 * rhs.size, transcendentals=0),
        )

    known = jnp.zeros((ncase, LANES), jnp.float32)
    state = [home_r]
    lists = [start]
    for step in range(ITERS - 1):
        last = step == ITERS - 2
        spread_out = sibling(own)
        if step > 0:
            spread_out, part = lax.optimization_barrier((spread_out, part))
            lists = update(step - 1, lists, known, part)
        spread_out = jnp.concatenate([spread_out[: per - 1], own[per - 1 :] + spread_out[per - 1 :]])
        parts = [spread_out] + [swap(spread_out, 4 * z) for z in range(1, nz)]
        a = jnp.concatenate([part[:half] for part in parts])
        b = jnp.concatenate([part[half:] for part in parts])
        far_a, far_b = swap(a, 1), swap(b, 2)
        a, b = jnp.concatenate([a, far_a]), jnp.concatenate([b, far_b])
        far_a, far_b = swap(a, 2), swap(b, 1)
        if step > 0:
            far_a, far_b, lists = lax.optimization_barrier((far_a, far_b, lists))
        *state, own, part, known = call(
            functools.partial(home_kernel, step == 0, last, nh, room, lines),
            (field,) * (0 if last else 2) + (f32(nbody * nsub, ncase, LANES) if last else answer, f32(npatch, nh, ncase, LANES), f32(ncase, LANES)),
            [SMEM] * 4 + [VMEM] * (8 + len(state)),
            near,
            far,
            on,
            picked,
            comp,
            own,
            a,
            far_a,
            b,
            far_b,
            known,
            block,
            *state,
            scratch=[load, spread],
        )
    sums = lax.all_to_all(own, ("body", "sub"), split_axis=0, concat_axis=0, tiled=True)
    return call(
        end_kernel,
        f32(ncase, npatch, gap),
        [SMEM] + [VMEM] * 9,
        keep,
        sums,
        known,
        compliance,
        part,
        sibling(part),
        *lists,
        scratch=[pltpu.VMEM((nh, npatch, ncase, LANES), jnp.float32)],
    )


def solution(mesh):
    in_specs = (
        P(None, "sub", None),
        P("sub", None),
        P("sub", None),
        P("sub", None),
        P("sub", None),
        P("sub"),
        P("body", "sub", None, None),
    )
    out_specs = P(None, "sub", None)
    return jax.shard_map(
        on_device, mesh=mesh, in_specs=in_specs, out_specs=out_specs, check_vma=False
    )
```

```python
import functools

import jax
import jax.numpy as jnp
from jax import lax
from jax.experimental import pallas as pl
from jax.experimental.pallas import tpu as pltpu
from jax.sharding import PartitionSpec as P

ITERS = 4
LANES = 128
SUBLANES = 8
VMEM = pl.BlockSpec(memory_space=pltpu.VMEM)
SMEM = pl.BlockSpec(memory_space=pltpu.SMEM)
HBM = pl.BlockSpec(memory_space=pltpu.HBM)
PARAMS = pltpu.CompilerParams(vmem_limit_bytes=16 * 1024 * 1024)


def f32(*shape):
    return jax.ShapeDtypeStruct(shape, jnp.float32)


def call(kernel, out_shape, specs, *operands, scratch=(), cost=None):
    several = isinstance(out_shape, (tuple, list))
    return pl.pallas_call(
        kernel,
        out_shape=tuple(out_shape) if several else out_shape,
        in_specs=specs,
        out_specs=(VMEM,) * len(out_shape) if several else VMEM,
        scratch_shapes=list(scratch),
        compiler_params=PARAMS,
        cost_estimate=cost,
    )(*operands)


def per_case(value):
    return jnp.sum(value, axis=1, keepdims=True)


def respond(block, load, gamma, energy, answer, last=False):
    ntile, ncase, width = load.shape
    value = jnp.concatenate([load[i] for i in range(ntile)], axis=1)
    high = value.astype(jnp.bfloat16)
    low = (value - high.astype(jnp.float32)).astype(jnp.bfloat16)
    total = jnp.dot(jnp.concatenate([high, low], axis=0), block[...], preferred_element_type=jnp.float32)
    total = total[:ncase] + total[ncase:]
    work = 0.5 * energy
    for i in range(ntile):
        tile = total[:, i * width : (i + 1) * width]
        if not last:
            answer[i] = tile
        work = work + load[i] * tile
    lane = lax.broadcasted_iota(jnp.int32, work.shape, 1)
    sums = jnp.where(lane == 0, per_case(0.5 * gamma), 0.0)
    sums = jnp.where(lane == 1, per_case(work), sums)
    if last:
        answer[...] = jnp.broadcast_to(sums[None], answer.shape)
    else:
        answer[ntile] = sums


def pack_kernel(nh, nz, by_z, place, field, *refs):
    if not by_z:
        table, *refs = refs
    *outs, whole = refs
    tiles = whole.shape[0] // (4 * nz + 1)
    whole[...] = jnp.zeros_like(whole)

    def body(p, carry):
        whole[pl.ds(place[p], nh)] = field[p]
        return carry

    lax.fori_loop(0, field.shape[0], body, 0, unroll=4)
    for i, out in enumerate(outs):
        size = out.shape[0] // (4 * nz // len(outs))
        for k in range(out.shape[0] // size):
            owner = i * 4 + k if by_z else k * 4 + i
            out[k * size : k * size + tiles] = whole[owner * tiles : (owner + 1) * tiles]
            if not by_z:
                out[k * size + tiles : (k + 1) * size] = table[owner]


def block_kernel(block, held, sems):
    pieces = sems.shape[0]
    size = block.shape[0] // pieces
    copies = []
    for j in range(pieces):
        rows = pl.ds(j * size, size)
        copies.append(pltpu.make_async_copy(block.at[rows], held.at[rows], sems.at[j]))
        copies[-1].start()
    for copy in copies:
        copy.wait()


def start_kernel(nh, cut, room, lines, extra, nz, block, *refs):
    a_z, refs = refs[:nz], refs[nz:]
    a_far, refs = refs[:3], refs[3:]
    b_near, refs = refs[:4], refs[4:]
    b_far, refs = refs[: nz - 1], refs[nz - 1 :]
    near, far, on, r_out, comp, answer, load, facts, sems = refs
    first, second = cut * nh, (room - cut) * nh
    blocks = []
    for z in range(nz):
        for m in range(4):
            one = (a_z[z], 0) if m == 0 else (a_far[m - 1], z * first)
            two = (b_near[m], 0) if z == 0 else (b_far[z - 1], m * (second + extra))
            blocks.append((*one, *two))
    copies = []
    for i, (_, _, two, at_two) in enumerate(blocks):
        rows = pl.ds(at_two + second + lines, extra - lines)
        copies.append(pltpu.make_async_copy(two.at[rows], facts.at[i], sems.at[i]))
        copies[-1].start()
    load[...] = jnp.zeros_like(load)
    gamma = energy = jnp.zeros(r_out.shape[2:], jnp.float32)
    for i, (one, at_one, two, at_two) in enumerate(blocks):
        at_comp = at_two + second
        comp[i * lines : (i + 1) * lines] = two[at_comp : at_comp + lines]
        copies[i].wait()
        for j in range(room):
            row = i * room + j
            slot = facts[i, j // SUBLANES, j % SUBLANES, 0].astype(jnp.int32)
            near[row] = slot
            far[row] = facts[i, j // SUBLANES, j % SUBLANES, 1].astype(jnp.int32)
            on[row] = facts[i, j // SUBLANES, j % SUBLANES, 2]
            if j < cut:
                r = one[at_one + j * nh : at_one + (j + 1) * nh]
            else:
                r = two[at_two + (j - cut) * nh : at_two + (j - cut + 1) * nh]
            r_out[row] = r
            load[pl.ds(slot, nh)] += r
            for h in range(nh):
                line, sub = divmod(j * nh + h, SUBLANES)
                square = r[h] * r[h]
                gamma = gamma + square
                energy = energy + two[at_comp + line, sub : sub + 1, :] * square
    respond(block, load, gamma, energy, answer)


def tree(values):
    while len(values) > 1:
        values = [a + b for a, b in zip(values[::2], values[1::2])]
    return values[0]


def steps(first, sums, known):
    gamma, delta = sums[:, 0:1], sums[:, 1:2]
    if first:
        return gamma, gamma / delta, jnp.zeros_like(gamma)
    beta = gamma / known[:, 0:1]
    return gamma, gamma / (delta - beta * gamma / known[:, 1:2]), beta


def home_kernel(first, last, nh, room, lines, place, away, keep, picked, comp, own, near_a, far_a, near_b, far_b, known, block, *refs):
    r_in, *refs = refs
    if not first:
        s_in, *refs = refs
    if not last:
        r, s, *refs = refs
    answer, part, known_out, load, resp = refs
    load[...] = jnp.zeros_like(load)
    nrow, _, ncase, width = r_in.shape
    at = 0
    for piece in (near_a, far_a, near_b, far_b):
        resp[at : at + piece.shape[0]] = piece[...]
        at += piece.shape[0]
    each = own.shape[0] // 2 + 1
    sums = tree([piece[i + each - 1] for piece in (near_b, far_b) for i in range(0, piece.shape[0], each)])
    gamma, alpha, beta = steps(first, sums, known[...])
    lane = lax.broadcasted_iota(jnp.int32, (ncase, width), 1)
    known_out[...] = jnp.where(lane == 0, gamma, jnp.where(lane == 1, alpha, beta))
    alpha = jnp.broadcast_to(alpha, (ncase, width))
    beta = jnp.broadcast_to(beta, (ncase, width))
    zero = jnp.zeros((ncase, width), jnp.float32)

    def pick(p, carry):
        part[p] = resp[pl.ds(picked[p], nh)]
        return carry

    lax.fori_loop(0, part.shape[0], pick, 0, unroll=8)

    def pair(i, sums):
        gamma, energy = sums
        for j in range(room):
            row = i * room + j
            near, far, on = place[row], away[row], keep[row]
            for h in range(nh):
                line, sub = divmod(j * nh + h, SUBLANES)
                c = comp[i * lines + line, sub : sub + 1, :]
                residual = r_in[row, h]
                image = on * (own[near + h] + resp[far + h] + c * residual)
                if not first:
                    image = image + beta * s_in[row, h]
                residual = residual - alpha * image
                if not last:
                    r[row, h], s[row, h] = residual, image
                load[near + h] += residual
                square = residual * residual
                gamma = gamma + square
                energy = energy + c * square
        return gamma, energy

    gamma, energy = lax.fori_loop(0, nrow // room, pair, (zero, zero))
    respond(block, load, gamma, energy, answer, last=last)


def list_kernel(first, keep, known, comp, mine, theirs, *refs):
    if first:
        r_in, r, d, x, s = refs
    else:
        r_in, d_in, x_in, s_in, r, d, x, s = refs
    npatch, nh, ncase, width = r.shape
    alpha = jnp.broadcast_to(known[:, 1:2], (ncase, width))
    beta = jnp.broadcast_to(known[:, 2:3], (ncase, width))

    def body(p, carry):
        on, row = keep[p], comp[pl.ds(p, 1), :]
        for h in range(nh):
            residual = r_in[p, h]
            c = row[:, h * width : (h + 1) * width]
            image = on * (mine[p, h] + theirs[p, h] + c * residual)
            if first:
                direction, moved = residual, alpha * residual
            else:
                direction = residual + beta * d_in[p, h]
                image = image + beta * s_in[p, h]
                moved = x_in[p, h] + alpha * direction
            r[p, h], d[p, h], x[p, h], s[p, h] = residual - alpha * image, direction, moved, image
        return carry

    lax.fori_loop(0, npatch, body, 0, unroll=4)


def end_kernel(keep, sums, known, comp, mine, theirs, r_in, d_in, x_in, s_in, out, moved):
    npatch, nh, ncase, width = r_in.shape
    total = sums[0]
    for i in range(1, sums.shape[0]):
        total = total + sums[i]
    _, alpha, beta = steps(False, total, known[...])
    one, two = jnp.broadcast_to(alpha, (ncase, width)), jnp.broadcast_to(beta, (ncase, width))
    alpha = jnp.broadcast_to(known[:, 1:2], (ncase, width))
    beta = jnp.broadcast_to(known[:, 2:3], (ncase, width))

    def body(p, carry):
        on, row = keep[p], comp[pl.ds(p, 1), :]
        for h in range(nh):
            residual = r_in[p, h]
            c = row[:, h * width : (h + 1) * width]
            image = on * (mine[p, h] + theirs[p, h] + c * residual) + beta * s_in[p, h]
            direction = residual + beta * d_in[p, h]
            residual = residual - alpha * image
            moved[h, p] = x_in[p, h] + alpha * direction + one * (residual + two * direction)
        return carry

    lax.fori_loop(0, npatch, body, 0, unroll=4)
    for h in range(nh):
        out[:, :, h * width : (h + 1) * width] = jnp.swapaxes(moved[h], 0, 1)


def on_device(rhs, compliance, plate_owner, found_owner, slot_pairs, active, inverse):
    nsub = lax.axis_size("sub")
    nbody = lax.axis_size("body")
    side = lax.axis_index("body")
    me = lax.axis_index("sub")
    ncase, npatch, gap = rhs.shape
    block = inverse[0, 0]
    nslot = block.shape[0] // gap
    nh = gap // LANES
    per = nslot * nh + 1
    room = max(2, 2 * npatch // nsub)
    nrow = nsub * room
    lines = -(-room * nh // SUBLANES)
    deep = -(-room // SUBLANES)
    extra = lines + deep
    cut = room // 2
    first = cut * nh
    second = (room - cut) * nh + extra
    nz = nsub // 4
    half = nslot // 2 * nh

    def swap(value, far):
        return lax.ppermute(value, "sub", [(i, i ^ far) for i in range(nsub)])

    def sibling(value):
        return lax.ppermute(value, "body", [(i, nbody - 1 - i) for i in range(nbody)])

    small = jnp.stack([plate_owner[:, 0], found_owner[:, 0], slot_pairs[:, 0], slot_pairs[:, 1], active])
    plate, foundation, plate_slot, found_slot, active = lax.optimization_barrier(small)
    keep = active.astype(jnp.float32)
    owner, other = jnp.where(side == 0, plate, foundation), jnp.where(side == 0, foundation, plate)
    slot, other_slot = jnp.where(side == 0, plate_slot, found_slot), jnp.where(side == 0, found_slot, plate_slot)
    index = jnp.arange(npatch, dtype=jnp.int32)
    earlier = (owner[None, :] == owner[:, None]) & (index[None, :] < index[:, None])
    rank = jnp.sum(earlier.astype(jnp.int32), axis=1)
    base, none = owner ^ me, 4 * nz
    place_a = jnp.where(rank < cut, base * cut + rank, none * cut) * nh
    place_b = jnp.where(rank < cut, none * (room - cut), base * (room - cut) + rank - cut) * nh

    def found(away):
        x_bit, y_bit, z_part = away & 1, (away >> 1) & 1, away >> 2
        found_a = ((y_bit * 2 + x_bit) * nz + z_part) * half + other_slot * nh
        found_b = ((x_bit * 2 + y_bit) * nz + z_part) * (half + 1) + (other_slot - nslot // 2) * nh
        return jnp.where(other_slot < nslot // 2, found_a, nsub * half + found_b)

    facts = jnp.stack([slot * nh, found(owner ^ other)], axis=1).astype(jnp.float32)
    facts = jnp.concatenate([facts, keep[:, None]], axis=1)
    facts = jnp.concatenate([compliance, jnp.pad(facts, ((0, 0), (0, LANES - 3)))], axis=1)
    row = (owner ^ me) * room + rank
    placed = (row[None, :] == jnp.arange(nrow, dtype=jnp.int32)[:, None]).astype(jnp.float32)
    facts = jnp.dot(placed, facts, precision=lax.Precision.HIGHEST).reshape(nsub, room, gap + LANES)
    lined = facts[:, :, :gap].reshape(nsub, room * nh, LANES)
    lined = jnp.pad(lined, ((0, 0), (0, lines * SUBLANES - room * nh), (0, 0)))
    named = jnp.pad(facts[:, :, gap:], ((0, 0), (0, deep * SUBLANES - room), (0, 0)))
    table = jnp.concatenate([lined, named], axis=1).reshape(nsub, lines + deep, SUBLANES, LANES)
    start = (keep[None, :, None] * rhs).reshape(ncase, npatch, nh, LANES)
    start = jnp.transpose(start, (1, 2, 0, 3))
    picked = found(me ^ other).astype(jnp.int32)
    place_a, place_b, picked = lax.optimization_barrier((place_a, place_b, picked))

    a_z = call(
        functools.partial(pack_kernel, nh, nz, True),
        (f32(4 * first, ncase, LANES),) * nz,
        [SMEM, VMEM],
        place_a,
        start,
        scratch=[pltpu.VMEM(((nsub + 1) * cut * nh, ncase, LANES), jnp.float32)],
    )
    b_near = call(
        functools.partial(pack_kernel, nh, nz, False),
        (f32(nz * second, ncase, LANES),) * 4,
        [SMEM, VMEM, VMEM],
        place_b,
        start,
        table,
        scratch=[pltpu.VMEM(((nsub + 1) * (room - cut) * nh, ncase, LANES), jnp.float32)],
    )
    a_z = [a_z[0]] + [swap(a_z[z], 4 * z) for z in range(1, nz)]
    b_near = [b_near[0]] + [swap(b_near[m], m) for m in range(1, 4)]
    block = call(
        block_kernel,
        jax.ShapeDtypeStruct(block.shape, block.dtype),
        [HBM],
        pltpu.with_memory_space_constraint(block, pltpu.HBM),
        scratch=[pltpu.SemaphoreType.DMA((nslot,))],
        cost=pl.CostEstimate(flops=0, bytes_accessed=4 * block.size, transcendentals=0),
    )
    a_z, b_near, block = lax.optimization_barrier((a_z, b_near, block))
    b_far = [
        swap(jnp.concatenate([part[z * second : (z + 1) * second] for part in b_near]), 4 * z)
        for z in range(1, nz)
    ]
    a_far = [
        swap(jnp.concatenate([part[m * first : (m + 1) * first] for part in a_z]), m) for m in range(1, 4)
    ]
    field = f32(nrow, nh, ncase, LANES)
    answer = f32(per, ncase, LANES)
    load = pltpu.VMEM((nslot * nh, ncase, LANES), jnp.float32)
    spread = pltpu.VMEM((nsub * per, ncase, LANES), jnp.float32)
    near, far, on, home_r, comp, own = pl.pallas_call(
        functools.partial(start_kernel, nh, cut, room, lines, extra, nz),
        out_shape=(jax.ShapeDtypeStruct((nrow,), jnp.int32),) * 2
        + (f32(nrow), field, f32(nsub * lines, ncase, LANES), answer),
        in_specs=[VMEM] * (2 * nz + 7),
        out_specs=(SMEM,) * 3 + (VMEM,) * 3,
        scratch_shapes=[
            load,
            pltpu.SMEM((nsub, deep, SUBLANES, LANES), jnp.float32),
            pltpu.SemaphoreType.DMA((nsub,)),
        ],
        compiler_params=PARAMS,
    )(block, *a_z, *a_far, *b_near, *b_far)
    def update(step, lists, known, part):
        return call(
            functools.partial(list_kernel, step == 0),
            (f32(npatch, nh, ncase, LANES),) * 4,
            [SMEM] + [VMEM] * (4 + len(lists)),
            keep,
            known,
            compliance,
            part,
            sibling(part),
            *lists,
            cost=pl.CostEstimate(flops=16 * rhs.size, bytes_accessed=44 * rhs.size, transcendentals=0),
        )

    known = jnp.zeros((ncase, LANES), jnp.float32)
    state = [home_r]
    lists = [start]
    for step in range(ITERS - 1):
        last = step == ITERS - 2
        spread_out = sibling(own)
        if step > 0:
            spread_out, part = lax.optimization_barrier((spread_out, part))
            lists = update(step - 1, lists, known, part)
        spread_out = jnp.concatenate([spread_out[: per - 1], own[per - 1 :] + spread_out[per - 1 :]])
        parts = [spread_out] + [swap(spread_out, 4 * z) for z in range(1, nz)]
        a = jnp.concatenate([part[:half] for part in parts])
        b = jnp.concatenate([part[half:] for part in parts])
        far_a, far_b = swap(a, 1), swap(b, 2)
        a, b = jnp.concatenate([a, far_a]), jnp.concatenate([b, far_b])
        far_a, far_b = swap(a, 2), swap(b, 1)
        if step > 0:
            far_a, far_b, lists = lax.optimization_barrier((far_a, far_b, lists))
        *state, own, part, known = call(
            functools.partial(home_kernel, step == 0, last, nh, room, lines),
            (field,) * (0 if last else 2) + (f32(nbody * nsub, ncase, LANES) if last else answer, f32(npatch, nh, ncase, LANES), f32(ncase, LANES)),
            [SMEM] * 4 + [VMEM] * (8 + len(state)),
            near,
            far,
            on,
            picked,
            comp,
            own,
            a,
            far_a,
            b,
            far_b,
            known,
            block,
            *state,
            scratch=[load, spread],
        )
    sums = lax.all_to_all(own, ("body", "sub"), split_axis=0, concat_axis=0, tiled=True)
    return call(
        end_kernel,
        f32(ncase, npatch, gap),
        [SMEM] + [VMEM] * 9,
        keep,
        sums,
        known,
        compliance,
        part,
        sibling(part),
        *lists,
        scratch=[pltpu.VMEM((nh, npatch, ncase, LANES), jnp.float32)],
    )


def solution(mesh):
    in_specs = (
        P(None, "sub", None),
        P("sub", None),
        P("sub", None),
        P("sub", None),
        P("sub", None),
        P("sub"),
        P("body", "sub", None, None),
    )
    out_specs = P(None, "sub", None)
    return jax.shard_map(
        on_device, mesh=mesh, in_specs=in_specs, out_specs=out_specs, check_vma=False
    )
```

```python
import functools

import jax
import jax.numpy as jnp
from jax import lax
from jax.experimental import pallas as pl
from jax.experimental.pallas import tpu as pltpu
from jax.sharding import PartitionSpec as P

ITERS = 4
LANES = 128
SUBLANES = 8
VMEM = pl.BlockSpec(memory_space=pltpu.VMEM)
SMEM = pl.BlockSpec(memory_space=pltpu.SMEM)
HBM = pl.BlockSpec(memory_space=pltpu.HBM)
PARAMS = pltpu.CompilerParams(vmem_limit_bytes=16 * 1024 * 1024)


def f32(*shape):
    return jax.ShapeDtypeStruct(shape, jnp.float32)


def call(kernel, out_shape, specs, *operands, scratch=(), cost=None):
    several = isinstance(out_shape, (tuple, list))
    return pl.pallas_call(
        kernel,
        out_shape=tuple(out_shape) if several else out_shape,
        in_specs=specs,
        out_specs=(VMEM,) * len(out_shape) if several else VMEM,
        scratch_shapes=list(scratch),
        compiler_params=PARAMS,
        cost_estimate=cost,
    )(*operands)


def per_case(value):
    return jnp.sum(value, axis=1, keepdims=True)


def respond(block, load, gamma, energy, answer, last=False):
    ntile, ncase, width = load.shape
    value = jnp.concatenate([load[i] for i in range(ntile)], axis=1)
    high = value.astype(jnp.bfloat16)
    low = (value - high.astype(jnp.float32)).astype(jnp.bfloat16)
    total = jnp.dot(jnp.concatenate([high, low], axis=0), block[...], preferred_element_type=jnp.float32)
    total = total[:ncase] + total[ncase:]
    work = 0.5 * energy
    for i in range(ntile):
        tile = total[:, i * width : (i + 1) * width]
        if not last:
            answer[i] = tile
        work = work + load[i] * tile
    lane = lax.broadcasted_iota(jnp.int32, work.shape, 1)
    sums = jnp.where(lane == 0, per_case(0.5 * gamma), 0.0)
    sums = jnp.where(lane == 1, per_case(work), sums)
    if last:
        answer[...] = jnp.broadcast_to(sums[None], answer.shape)
    else:
        answer[ntile] = sums


def pack_kernel(nh, nz, by_z, place, field, *refs):
    if not by_z:
        table, *refs = refs
    *outs, whole = refs
    tiles = whole.shape[0] // (4 * nz + 1)
    whole[...] = jnp.zeros_like(whole)

    def body(p, carry):
        whole[pl.ds(place[p], nh)] = field[p]
        return carry

    lax.fori_loop(0, field.shape[0], body, 0, unroll=4)
    for i, out in enumerate(outs):
        size = out.shape[0] // (4 * nz // len(outs))
        for k in range(out.shape[0] // size):
            owner = i * 4 + k if by_z else k * 4 + i
            out[k * size : k * size + tiles] = whole[owner * tiles : (owner + 1) * tiles]
            if not by_z:
                out[k * size + tiles : (k + 1) * size] = table[owner]


def block_kernel(block, held, sems):
    pieces = sems.shape[0]
    size = block.shape[0] // pieces
    copies = []
    for j in range(pieces):
        rows = pl.ds(j * size, size)
        copies.append(pltpu.make_async_copy(block.at[rows], held.at[rows], sems.at[j]))
        copies[-1].start()
    for copy in copies:
        copy.wait()


def start_kernel(nh, cut, room, lines, extra, nz, block, *refs):
    a_z, refs = refs[:nz], refs[nz:]
    a_far, refs = refs[:3], refs[3:]
    b_near, refs = refs[:4], refs[4:]
    b_far, refs = refs[: nz - 1], refs[nz - 1 :]
    near, far, on, r_out, comp, answer, load, facts, sems = refs
    first, second = cut * nh, (room - cut) * nh
    blocks = []
    for z in range(nz):
        for m in range(4):
            one = (a_z[z], 0) if m == 0 else (a_far[m - 1], z * first)
            two = (b_near[m], 0) if z == 0 else (b_far[z - 1], m * (second + extra))
            blocks.append((*one, *two))
    copies = []
    for i, (_, _, two, at_two) in enumerate(blocks):
        rows = pl.ds(at_two + second + lines, extra - lines)
        copies.append(pltpu.make_async_copy(two.at[rows], facts.at[i], sems.at[i]))
        copies[-1].start()
    load[...] = jnp.zeros_like(load)
    gamma = energy = jnp.zeros(r_out.shape[2:], jnp.float32)
    for i, (one, at_one, two, at_two) in enumerate(blocks):
        at_comp = at_two + second
        comp[i * lines : (i + 1) * lines] = two[at_comp : at_comp + lines]
        copies[i].wait()
        for j in range(room):
            row = i * room + j
            slot = facts[i, j // SUBLANES, j % SUBLANES, 0].astype(jnp.int32)
            near[row] = slot
            far[row] = facts[i, j // SUBLANES, j % SUBLANES, 1].astype(jnp.int32)
            on[row] = facts[i, j // SUBLANES, j % SUBLANES, 2]
            if j < cut:
                r = one[at_one + j * nh : at_one + (j + 1) * nh]
            else:
                r = two[at_two + (j - cut) * nh : at_two + (j - cut + 1) * nh]
            r_out[row] = r
            load[pl.ds(slot, nh)] += r
            for h in range(nh):
                line, sub = divmod(j * nh + h, SUBLANES)
                square = r[h] * r[h]
                gamma = gamma + square
                energy = energy + two[at_comp + line, sub : sub + 1, :] * square
    respond(block, load, gamma, energy, answer)


def tree(values):
    while len(values) > 1:
        values = [a + b for a, b in zip(values[::2], values[1::2])]
    return values[0]


def steps(first, sums, known):
    gamma, delta = sums[:, 0:1], sums[:, 1:2]
    if first:
        return gamma, gamma / delta, jnp.zeros_like(gamma)
    beta = gamma / known[:, 0:1]
    return gamma, gamma / (delta - beta * gamma / known[:, 1:2]), beta


def home_kernel(first, last, nh, room, lines, place, away, keep, picked, comp, own, near_a, far_a, near_b, far_b, known, block, *refs):
    r_in, *refs = refs
    if not first:
        s_in, *refs = refs
    if not last:
        r, s, *refs = refs
    answer, part, known_out, load, resp = refs
    load[...] = jnp.zeros_like(load)
    nrow, _, ncase, width = r_in.shape
    at = 0
    for piece in (near_a, far_a, near_b, far_b):
        resp[at : at + piece.shape[0]] = piece[...]
        at += piece.shape[0]
    each = own.shape[0] // 2 + 1
    sums = tree([piece[i + each - 1] for piece in (near_b, far_b) for i in range(0, piece.shape[0], each)])
    gamma, alpha, beta = steps(first, sums, known[...])
    lane = lax.broadcasted_iota(jnp.int32, (ncase, width), 1)
    known_out[...] = jnp.where(lane == 0, gamma, jnp.where(lane == 1, alpha, beta))
    alpha = jnp.broadcast_to(alpha, (ncase, width))
    beta = jnp.broadcast_to(beta, (ncase, width))
    zero = jnp.zeros((ncase, width), jnp.float32)

    def pick(p, carry):
        part[p] = resp[pl.ds(picked[p], nh)]
        return carry

    lax.fori_loop(0, part.shape[0], pick, 0, unroll=8)

    def pair(i, sums):
        gamma, energy = sums
        for j in range(room):
            row = i * room + j
            near, far, on = place[row], away[row], keep[row]
            for h in range(nh):
                line, sub = divmod(j * nh + h, SUBLANES)
                c = comp[i * lines + line, sub : sub + 1, :]
                residual = r_in[row, h]
                image = on * (own[near + h] + resp[far + h] + c * residual)
                if not first:
                    image = image + beta * s_in[row, h]
                residual = residual - alpha * image
                if not last:
                    r[row, h], s[row, h] = residual, image
                load[near + h] += residual
                square = residual * residual
                gamma = gamma + square
                energy = energy + c * square
        return gamma, energy

    gamma, energy = lax.fori_loop(0, nrow // room, pair, (zero, zero))
    respond(block, load, gamma, energy, answer, last=last)


def list_kernel(first, keep, known, comp, mine, theirs, *refs):
    if first:
        r_in, r, d, x, s = refs
    else:
        r_in, d_in, x_in, s_in, r, d, x, s = refs
    npatch, nh, ncase, width = r.shape
    alpha = jnp.broadcast_to(known[:, 1:2], (ncase, width))
    beta = jnp.broadcast_to(known[:, 2:3], (ncase, width))

    def body(p, carry):
        on, row = keep[p], comp[pl.ds(p, 1), :]
        for h in range(nh):
            residual = r_in[p, h]
            c = row[:, h * width : (h + 1) * width]
            image = on * (mine[p, h] + theirs[p, h] + c * residual)
            if first:
                direction, moved = residual, alpha * residual
            else:
                direction = residual + beta * d_in[p, h]
                image = image + beta * s_in[p, h]
                moved = x_in[p, h] + alpha * direction
            r[p, h], d[p, h], x[p, h], s[p, h] = residual - alpha * image, direction, moved, image
        return carry

    lax.fori_loop(0, npatch, body, 0, unroll=4)


def end_kernel(keep, sums, known, comp, mine, theirs, r_in, d_in, x_in, s_in, out, moved):
    npatch, nh, ncase, width = r_in.shape
    total = sums[0]
    for i in range(1, sums.shape[0]):
        total = total + sums[i]
    _, alpha, beta = steps(False, total, known[...])
    one, two = jnp.broadcast_to(alpha, (ncase, width)), jnp.broadcast_to(beta, (ncase, width))
    alpha = jnp.broadcast_to(known[:, 1:2], (ncase, width))
    beta = jnp.broadcast_to(known[:, 2:3], (ncase, width))

    def body(p, carry):
        on, row = keep[p], comp[pl.ds(p, 1), :]
        for h in range(nh):
            residual = r_in[p, h]
            c = row[:, h * width : (h + 1) * width]
            image = on * (mine[p, h] + theirs[p, h] + c * residual) + beta * s_in[p, h]
            direction = residual + beta * d_in[p, h]
            residual = residual - alpha * image
            moved[h, p] = x_in[p, h] + alpha * direction + one * (residual + two * direction)
        return carry

    lax.fori_loop(0, npatch, body, 0, unroll=4)
    for h in range(nh):
        out[:, :, h * width : (h + 1) * width] = jnp.swapaxes(moved[h], 0, 1)


def on_device(rhs, compliance, plate_owner, found_owner, slot_pairs, active, inverse):
    nsub = lax.axis_size("sub")
    nbody = lax.axis_size("body")
    side = lax.axis_index("body")
    me = lax.axis_index("sub")
    ncase, npatch, gap = rhs.shape
    block = inverse[0, 0]
    nslot = block.shape[0] // gap
    nh = gap // LANES
    per = nslot * nh + 1
    room = max(2, 2 * npatch // nsub)
    nrow = nsub * room
    lines = -(-room * nh // SUBLANES)
    deep = -(-room // SUBLANES)
    extra = lines + deep
    cut = room // 2
    first = cut * nh
    second = (room - cut) * nh + extra
    nz = nsub // 4
    half = nslot // 2 * nh

    def swap(value, far):
        return lax.ppermute(value, "sub", [(i, i ^ far) for i in range(nsub)])

    def sibling(value):
        return lax.ppermute(value, "body", [(i, nbody - 1 - i) for i in range(nbody)])

    small = jnp.stack([plate_owner[:, 0], found_owner[:, 0], slot_pairs[:, 0], slot_pairs[:, 1], active])
    plate, foundation, plate_slot, found_slot, active = lax.optimization_barrier(small)
    keep = active.astype(jnp.float32)
    owner, other = jnp.where(side == 0, plate, foundation), jnp.where(side == 0, foundation, plate)
    slot, other_slot = jnp.where(side == 0, plate_slot, found_slot), jnp.where(side == 0, found_slot, plate_slot)
    index = jnp.arange(npatch, dtype=jnp.int32)
    earlier = (owner[None, :] == owner[:, None]) & (index[None, :] < index[:, None])
    rank = jnp.sum(earlier.astype(jnp.int32), axis=1)
    base, none = owner ^ me, 4 * nz
    place_a = jnp.where(rank < cut, base * cut + rank, none * cut) * nh
    place_b = jnp.where(rank < cut, none * (room - cut), base * (room - cut) + rank - cut) * nh

    def found(away):
        x_bit, y_bit, z_part = away & 1, (away >> 1) & 1, away >> 2
        found_a = ((y_bit * 2 + x_bit) * nz + z_part) * half + other_slot * nh
        found_b = ((x_bit * 2 + y_bit) * nz + z_part) * (half + 1) + (other_slot - nslot // 2) * nh
        return jnp.where(other_slot < nslot // 2, found_a, nsub * half + found_b)

    facts = jnp.stack([slot * nh, found(owner ^ other)], axis=1).astype(jnp.float32)
    facts = jnp.concatenate([facts, keep[:, None]], axis=1)
    facts = jnp.concatenate([compliance, jnp.pad(facts, ((0, 0), (0, LANES - 3)))], axis=1)
    row = (owner ^ me) * room + rank
    placed = (row[None, :] == jnp.arange(nrow, dtype=jnp.int32)[:, None]).astype(jnp.float32)
    facts = jnp.dot(placed, facts, precision=lax.Precision.HIGHEST).reshape(nsub, room, gap + LANES)
    lined = facts[:, :, :gap].reshape(nsub, room * nh, LANES)
    lined = jnp.pad(lined, ((0, 0), (0, lines * SUBLANES - room * nh), (0, 0)))
    named = jnp.pad(facts[:, :, gap:], ((0, 0), (0, deep * SUBLANES - room), (0, 0)))
    table = jnp.concatenate([lined, named], axis=1).reshape(nsub, lines + deep, SUBLANES, LANES)
    start = (keep[None, :, None] * rhs).reshape(ncase, npatch, nh, LANES)
    start = jnp.transpose(start, (1, 2, 0, 3))
    picked = found(me ^ other).astype(jnp.int32)
    place_a, place_b, picked = lax.optimization_barrier((place_a, place_b, picked))

    a_z = call(
        functools.partial(pack_kernel, nh, nz, True),
        (f32(4 * first, ncase, LANES),) * nz,
        [SMEM, VMEM],
        place_a,
        start,
        scratch=[pltpu.VMEM(((nsub + 1) * cut * nh, ncase, LANES), jnp.float32)],
    )
    b_near = call(
        functools.partial(pack_kernel, nh, nz, False),
        (f32(nz * second, ncase, LANES),) * 4,
        [SMEM, VMEM, VMEM],
        place_b,
        start,
        table,
        scratch=[pltpu.VMEM(((nsub + 1) * (room - cut) * nh, ncase, LANES), jnp.float32)],
    )
    a_z = [a_z[0]] + [swap(a_z[z], 4 * z) for z in range(1, nz)]
    b_near = [b_near[0]] + [swap(b_near[m], m) for m in range(1, 4)]
    block = call(
        block_kernel,
        jax.ShapeDtypeStruct(block.shape, block.dtype),
        [HBM],
        pltpu.with_memory_space_constraint(block, pltpu.HBM),
        scratch=[pltpu.SemaphoreType.DMA((nslot,))],
        cost=pl.CostEstimate(flops=0, bytes_accessed=4 * block.size, transcendentals=0),
    )
    a_z, b_near, block = lax.optimization_barrier((a_z[::-1], b_near, block))
    a_z = a_z[::-1]
    b_far = [
        swap(jnp.concatenate([part[z * second : (z + 1) * second] for part in b_near]), 4 * z)
        for z in range(1, nz)
    ]
    a_far = [
        swap(jnp.concatenate([part[m * first : (m + 1) * first] for part in a_z]), m) for m in range(1, 4)
    ]
    field = f32(nrow, nh, ncase, LANES)
    answer = f32(per, ncase, LANES)
    load = pltpu.VMEM((nslot * nh, ncase, LANES), jnp.float32)
    spread = pltpu.VMEM((nsub * per, ncase, LANES), jnp.float32)
    near, far, on, home_r, comp, own = pl.pallas_call(
        functools.partial(start_kernel, nh, cut, room, lines, extra, nz),
        out_shape=(jax.ShapeDtypeStruct((nrow,), jnp.int32),) * 2
        + (f32(nrow), field, f32(nsub * lines, ncase, LANES), answer),
        in_specs=[VMEM] * (2 * nz + 7),
        out_specs=(SMEM,) * 3 + (VMEM,) * 3,
        scratch_shapes=[
            load,
            pltpu.SMEM((nsub, deep, SUBLANES, LANES), jnp.float32),
            pltpu.SemaphoreType.DMA((nsub,)),
        ],
        compiler_params=PARAMS,
    )(block, *a_z, *a_far, *b_near, *b_far)
    def update(step, lists, known, part):
        return call(
            functools.partial(list_kernel, step == 0),
            (f32(npatch, nh, ncase, LANES),) * 4,
            [SMEM] + [VMEM] * (4 + len(lists)),
            keep,
            known,
            compliance,
            part,
            sibling(part),
            *lists,
            cost=pl.CostEstimate(flops=16 * rhs.size, bytes_accessed=44 * rhs.size, transcendentals=0),
        )

    known = jnp.zeros((ncase, LANES), jnp.float32)
    state = [home_r]
    lists = [start]
    for step in range(ITERS - 1):
        last = step == ITERS - 2
        spread_out = sibling(own)
        if step > 0:
            spread_out, part = lax.optimization_barrier((spread_out, part))
            lists = update(step - 1, lists, known, part)
        spread_out = jnp.concatenate([spread_out[: per - 1], own[per - 1 :] + spread_out[per - 1 :]])
        parts = [spread_out] + [swap(spread_out, 4 * z) for z in range(1, nz)]
        parts = lax.optimization_barrier(parts[::-1])[::-1]
        a = jnp.concatenate([part[:half] for part in parts])
        b = jnp.concatenate([part[half:] for part in parts])
        far_a, far_b = swap(a, 1), swap(b, 2)
        a, b = jnp.concatenate([a, far_a]), jnp.concatenate([b, far_b])
        far_a, far_b = swap(a, 2), swap(b, 1)
        if step > 0:
            far_a, far_b, lists = lax.optimization_barrier((far_a, far_b, lists))
        *state, own, part, known = call(
            functools.partial(home_kernel, step == 0, last, nh, room, lines),
            (field,) * (0 if last else 2) + (f32(nbody * nsub, ncase, LANES) if last else answer, f32(npatch, nh, ncase, LANES), f32(ncase, LANES)),
            [SMEM] * 4 + [VMEM] * (8 + len(state)),
            near,
            far,
            on,
            picked,
            comp,
            own,
            a,
            far_a,
            b,
            far_b,
            known,
            block,
            *state,
            scratch=[load, spread],
        )
    sums = lax.all_to_all(own, ("body", "sub"), split_axis=0, concat_axis=0, tiled=True)
    return call(
        end_kernel,
        f32(ncase, npatch, gap),
        [SMEM] + [VMEM] * 9,
        keep,
        sums,
        known,
        compliance,
        part,
        sibling(part),
        *lists,
        scratch=[pltpu.VMEM((nh, npatch, ncase, LANES), jnp.float32)],
    )


def solution(mesh):
    in_specs = (
        P(None, "sub", None),
        P("sub", None),
        P("sub", None),
        P("sub", None),
        P("sub", None),
        P("sub"),
        P("body", "sub", None, None),
    )
    out_specs = P(None, "sub", None)
    return jax.shard_map(
        on_device, mesh=mesh, in_specs=in_specs, out_specs=out_specs, check_vma=False
    )
```

```python
import functools

import jax
import jax.numpy as jnp
from jax import lax
from jax.experimental import pallas as pl
from jax.experimental.pallas import tpu as pltpu
from jax.sharding import PartitionSpec as P

ITERS = 4
LANES = 128
SUBLANES = 8
VMEM = pl.BlockSpec(memory_space=pltpu.VMEM)
SMEM = pl.BlockSpec(memory_space=pltpu.SMEM)
HBM = pl.BlockSpec(memory_space=pltpu.HBM)
PARAMS = pltpu.CompilerParams(vmem_limit_bytes=16 * 1024 * 1024)


def f32(*shape):
    return jax.ShapeDtypeStruct(shape, jnp.float32)


def call(kernel, out_shape, specs, *operands, scratch=(), cost=None):
    several = isinstance(out_shape, (tuple, list))
    return pl.pallas_call(
        kernel,
        out_shape=tuple(out_shape) if several else out_shape,
        in_specs=specs,
        out_specs=(VMEM,) * len(out_shape) if several else VMEM,
        scratch_shapes=list(scratch),
        compiler_params=PARAMS,
        cost_estimate=cost,
    )(*operands)


def per_case(value):
    return jnp.sum(value, axis=1, keepdims=True)


def respond(block, load, gamma, energy, answer, last=False):
    ntile, ncase, width = load.shape
    value = jnp.concatenate([load[i] for i in range(ntile)], axis=1)
    high = value.astype(jnp.bfloat16)
    low = (value - high.astype(jnp.float32)).astype(jnp.bfloat16)
    total = jnp.dot(jnp.concatenate([high, low], axis=0), block[...], preferred_element_type=jnp.float32)
    total = total[:ncase] + total[ncase:]
    work = 0.5 * energy
    for i in range(ntile):
        tile = total[:, i * width : (i + 1) * width]
        if not last:
            answer[i] = tile
        work = work + load[i] * tile
    lane = lax.broadcasted_iota(jnp.int32, work.shape, 1)
    sums = jnp.where(lane == 0, per_case(0.5 * gamma), 0.0)
    sums = jnp.where(lane == 1, per_case(work), sums)
    if last:
        answer[...] = jnp.broadcast_to(sums[None], answer.shape)
    else:
        answer[ntile] = sums


def pack_kernel(nh, nz, by_z, place, field, *refs):
    if not by_z:
        table, *refs = refs
    *outs, whole = refs
    tiles = whole.shape[0] // (4 * nz + 1)
    whole[...] = jnp.zeros_like(whole)

    def body(p, carry):
        whole[pl.ds(place[p], nh)] = field[p]
        return carry

    lax.fori_loop(0, field.shape[0], body, 0, unroll=4)
    for i, out in enumerate(outs):
        size = out.shape[0] // (4 * nz // len(outs))
        for k in range(out.shape[0] // size):
            owner = i * 4 + k if by_z else k * 4 + i
            out[k * size : k * size + tiles] = whole[owner * tiles : (owner + 1) * tiles]
            if not by_z:
                out[k * size + tiles : (k + 1) * size] = table[owner]


def block_kernel(block, held, sems):
    pieces = sems.shape[0]
    size = block.shape[0] // pieces
    copies = []
    for j in range(pieces):
        rows = pl.ds(j * size, size)
        copies.append(pltpu.make_async_copy(block.at[rows], held.at[rows], sems.at[j]))
        copies[-1].start()
    for copy in copies:
        copy.wait()


def start_kernel(nh, cut, room, lines, extra, nz, block, *refs):
    a_z, refs = refs[:nz], refs[nz:]
    a_far, refs = refs[:3], refs[3:]
    b_near, refs = refs[:4], refs[4:]
    b_far, refs = refs[: nz - 1], refs[nz - 1 :]
    near, far, on, r_out, comp, answer, load, facts, sems = refs
    first, second = cut * nh, (room - cut) * nh
    blocks = []
    for z in range(nz):
        for m in range(4):
            one = (a_z[z], 0) if m == 0 else (a_far[m - 1], z * first)
            two = (b_near[m], 0) if z == 0 else (b_far[z - 1], m * (second + extra))
            blocks.append((*one, *two))
    copies = []
    for i, (_, _, two, at_two) in enumerate(blocks):
        rows = pl.ds(at_two + second + lines, extra - lines)
        copies.append(pltpu.make_async_copy(two.at[rows], facts.at[i], sems.at[i]))
        copies[-1].start()
    load[...] = jnp.zeros_like(load)
    gamma = energy = jnp.zeros(r_out.shape[2:], jnp.float32)
    for i, (one, at_one, two, at_two) in enumerate(blocks):
        at_comp = at_two + second
        comp[i * lines : (i + 1) * lines] = two[at_comp : at_comp + lines]
        copies[i].wait()
        for j in range(room):
            row = i * room + j
            slot = facts[i, j // SUBLANES, j % SUBLANES, 0].astype(jnp.int32)
            near[row] = slot
            far[row] = facts[i, j // SUBLANES, j % SUBLANES, 1].astype(jnp.int32)
            on[row] = facts[i, j // SUBLANES, j % SUBLANES, 2]
            if j < cut:
                r = one[at_one + j * nh : at_one + (j + 1) * nh]
            else:
                r = two[at_two + (j - cut) * nh : at_two + (j - cut + 1) * nh]
            r_out[row] = r
            load[pl.ds(slot, nh)] += r
            for h in range(nh):
                line, sub = divmod(j * nh + h, SUBLANES)
                square = r[h] * r[h]
                gamma = gamma + square
                energy = energy + two[at_comp + line, sub : sub + 1, :] * square
    respond(block, load, gamma, energy, answer)


def tree(values):
    while len(values) > 1:
        values = [a + b for a, b in zip(values[::2], values[1::2])]
    return values[0]


def steps(first, sums, known):
    gamma, delta = sums[:, 0:1], sums[:, 1:2]
    if first:
        return gamma, gamma / delta, jnp.zeros_like(gamma)
    beta = gamma / known[:, 0:1]
    return gamma, gamma / (delta - beta * gamma / known[:, 1:2]), beta


def home_kernel(first, last, nh, room, lines, place, away, keep, picked, comp, own, near_a, far_a, near_b, far_b, known, block, *refs):
    r_in, *refs = refs
    if not first:
        s_in, *refs = refs
    if not last:
        r, s, *refs = refs
    answer, part, known_out, load, resp = refs
    load[...] = jnp.zeros_like(load)
    nrow, _, ncase, width = r_in.shape
    at = 0
    for piece in (near_a, far_a, near_b, far_b):
        resp[at : at + piece.shape[0]] = piece[...]
        at += piece.shape[0]
    size = near_b.shape[0] // 2
    sums = tree([piece[i + size - 1] for piece in (near_b, far_b) for i in (0, size)])
    gamma, alpha, beta = steps(first, sums, known[...])
    lane = lax.broadcasted_iota(jnp.int32, (ncase, width), 1)
    known_out[...] = jnp.where(lane == 0, gamma, jnp.where(lane == 1, alpha, beta))
    alpha = jnp.broadcast_to(alpha, (ncase, width))
    beta = jnp.broadcast_to(beta, (ncase, width))
    zero = jnp.zeros((ncase, width), jnp.float32)

    def pick(p, carry):
        part[p] = resp[pl.ds(picked[p], nh)]
        return carry

    lax.fori_loop(0, part.shape[0], pick, 0, unroll=8)

    def pair(i, sums):
        gamma, energy = sums
        for j in range(room):
            row = i * room + j
            near, far, on = place[row], away[row], keep[row]
            for h in range(nh):
                line, sub = divmod(j * nh + h, SUBLANES)
                c = comp[i * lines + line, sub : sub + 1, :]
                residual = r_in[row, h]
                image = on * (own[near + h] + resp[far + h] + c * residual)
                if not first:
                    image = image + beta * s_in[row, h]
                residual = residual - alpha * image
                if not last:
                    r[row, h], s[row, h] = residual, image
                load[near + h] += residual
                square = residual * residual
                gamma = gamma + square
                energy = energy + c * square
        return gamma, energy

    gamma, energy = lax.fori_loop(0, nrow // room, pair, (zero, zero))
    respond(block, load, gamma, energy, answer, last=last)


def list_kernel(first, keep, known, comp, mine, theirs, *refs):
    if first:
        r_in, r, d, x, s = refs
    else:
        r_in, d_in, x_in, s_in, r, d, x, s = refs
    npatch, nh, ncase, width = r.shape
    alpha = jnp.broadcast_to(known[:, 1:2], (ncase, width))
    beta = jnp.broadcast_to(known[:, 2:3], (ncase, width))

    def body(p, carry):
        on, row = keep[p], comp[pl.ds(p, 1), :]
        for h in range(nh):
            residual = r_in[p, h]
            c = row[:, h * width : (h + 1) * width]
            image = on * (mine[p, h] + theirs[p, h] + c * residual)
            if first:
                direction, moved = residual, alpha * residual
            else:
                direction = residual + beta * d_in[p, h]
                image = image + beta * s_in[p, h]
                moved = x_in[p, h] + alpha * direction
            r[p, h], d[p, h], x[p, h], s[p, h] = residual - alpha * image, direction, moved, image
        return carry

    lax.fori_loop(0, npatch, body, 0, unroll=4)


def end_kernel(keep, sums, known, comp, mine, theirs, r_in, d_in, x_in, s_in, out, moved):
    npatch, nh, ncase, width = r_in.shape
    total = sums[0]
    for i in range(1, sums.shape[0]):
        total = total + sums[i]
    _, alpha, beta = steps(False, total, known[...])
    one, two = jnp.broadcast_to(alpha, (ncase, width)), jnp.broadcast_to(beta, (ncase, width))
    alpha = jnp.broadcast_to(known[:, 1:2], (ncase, width))
    beta = jnp.broadcast_to(known[:, 2:3], (ncase, width))

    def body(p, carry):
        on, row = keep[p], comp[pl.ds(p, 1), :]
        for h in range(nh):
            residual = r_in[p, h]
            c = row[:, h * width : (h + 1) * width]
            image = on * (mine[p, h] + theirs[p, h] + c * residual) + beta * s_in[p, h]
            direction = residual + beta * d_in[p, h]
            residual = residual - alpha * image
            moved[h, p] = x_in[p, h] + alpha * direction + one * (residual + two * direction)
        return carry

    lax.fori_loop(0, npatch, body, 0, unroll=4)
    for h in range(nh):
        out[:, :, h * width : (h + 1) * width] = jnp.swapaxes(moved[h], 0, 1)


def on_device(rhs, compliance, plate_owner, found_owner, slot_pairs, active, inverse):
    nsub = lax.axis_size("sub")
    nbody = lax.axis_size("body")
    side = lax.axis_index("body")
    me = lax.axis_index("sub")
    ncase, npatch, gap = rhs.shape
    block = inverse[0, 0]
    nslot = block.shape[0] // gap
    nh = gap // LANES
    per = nslot * nh + 1
    room = max(2, 2 * npatch // nsub)
    nrow = nsub * room
    lines = -(-room * nh // SUBLANES)
    deep = -(-room // SUBLANES)
    extra = lines + deep
    cut = room // 2
    first = cut * nh
    second = (room - cut) * nh + extra
    nz = nsub // 4
    half = nslot // 2 * nh

    def swap(value, far):
        return lax.ppermute(value, "sub", [(i, i ^ far) for i in range(nsub)])

    def sibling(value):
        return lax.ppermute(value, "body", [(i, nbody - 1 - i) for i in range(nbody)])

    small = jnp.stack([plate_owner[:, 0], found_owner[:, 0], slot_pairs[:, 0], slot_pairs[:, 1], active])
    plate, foundation, plate_slot, found_slot, active = lax.optimization_barrier(small)
    keep = active.astype(jnp.float32)
    owner, other = jnp.where(side == 0, plate, foundation), jnp.where(side == 0, foundation, plate)
    slot, other_slot = jnp.where(side == 0, plate_slot, found_slot), jnp.where(side == 0, found_slot, plate_slot)
    index = jnp.arange(npatch, dtype=jnp.int32)
    earlier = (owner[None, :] == owner[:, None]) & (index[None, :] < index[:, None])
    rank = jnp.sum(earlier.astype(jnp.int32), axis=1)
    base, none = owner ^ me, 4 * nz
    place_a = jnp.where(rank < cut, base * cut + rank, none * cut) * nh
    place_b = jnp.where(rank < cut, none * (room - cut), base * (room - cut) + rank - cut) * nh

    def found(away):
        x_bit, y_bit, z_part = away & 1, (away >> 1) & 1, away >> 2
        found_a = ((y_bit * 2 + x_bit) * nz + z_part) * half + other_slot * nh
        found_b = (x_bit * 2 + y_bit) * (nz * half + 1) + z_part * half + (other_slot - nslot // 2) * nh
        return jnp.where(other_slot < nslot // 2, found_a, nsub * half + found_b)

    facts = jnp.stack([slot * nh, found(owner ^ other)], axis=1).astype(jnp.float32)
    facts = jnp.concatenate([facts, keep[:, None]], axis=1)
    facts = jnp.concatenate([compliance, jnp.pad(facts, ((0, 0), (0, LANES - 3)))], axis=1)
    row = (owner ^ me) * room + rank
    placed = (row[None, :] == jnp.arange(nrow, dtype=jnp.int32)[:, None]).astype(jnp.float32)
    facts = jnp.dot(placed, facts, precision=lax.Precision.HIGHEST).reshape(nsub, room, gap + LANES)
    lined = facts[:, :, :gap].reshape(nsub, room * nh, LANES)
    lined = jnp.pad(lined, ((0, 0), (0, lines * SUBLANES - room * nh), (0, 0)))
    named = jnp.pad(facts[:, :, gap:], ((0, 0), (0, deep * SUBLANES - room), (0, 0)))
    table = jnp.concatenate([lined, named], axis=1).reshape(nsub, lines + deep, SUBLANES, LANES)
    start = (keep[None, :, None] * rhs).reshape(ncase, npatch, nh, LANES)
    start = jnp.transpose(start, (1, 2, 0, 3))
    picked = found(me ^ other).astype(jnp.int32)
    place_a, place_b, picked = lax.optimization_barrier((place_a, place_b, picked))

    a_z = call(
        functools.partial(pack_kernel, nh, nz, True),
        (f32(4 * first, ncase, LANES),) * nz,
        [SMEM, VMEM],
        place_a,
        start,
        scratch=[pltpu.VMEM(((nsub + 1) * cut * nh, ncase, LANES), jnp.float32)],
    )
    b_near = call(
        functools.partial(pack_kernel, nh, nz, False),
        (f32(nz * second, ncase, LANES),) * 4,
        [SMEM, VMEM, VMEM],
        place_b,
        start,
        table,
        scratch=[pltpu.VMEM(((nsub + 1) * (room - cut) * nh, ncase, LANES), jnp.float32)],
    )
    a_z = [a_z[0]] + [swap(a_z[z], 4 * z) for z in range(1, nz)]
    b_near = [b_near[0]] + [swap(b_near[m], m) for m in range(1, 4)]
    block = call(
        block_kernel,
        jax.ShapeDtypeStruct(block.shape, block.dtype),
        [HBM],
        pltpu.with_memory_space_constraint(block, pltpu.HBM),
        scratch=[pltpu.SemaphoreType.DMA((nslot,))],
        cost=pl.CostEstimate(flops=0, bytes_accessed=4 * block.size, transcendentals=0),
    )
    a_z, b_near, block = lax.optimization_barrier((a_z[::-1], b_near, block))
    a_z = a_z[::-1]
    b_far = [
        swap(jnp.concatenate([part[z * second : (z + 1) * second] for part in b_near]), 4 * z)
        for z in range(1, nz)
    ]
    signal = sibling(a_z[1][:1])
    a_far = [
        swap(jnp.concatenate([part[m * first : (m + 1) * first] for part in a_z] + [signal]), m)
        for m in range(1, 4)
    ]
    a_far, b_far = lax.optimization_barrier((a_far, b_far[::-1]))
    b_far = b_far[::-1]
    field = f32(nrow, nh, ncase, LANES)
    answer = f32(per, ncase, LANES)
    load = pltpu.VMEM((nslot * nh, ncase, LANES), jnp.float32)
    spread = pltpu.VMEM((nsub * 2 * half + 4, ncase, LANES), jnp.float32)
    near, far, on, home_r, comp, own = pl.pallas_call(
        functools.partial(start_kernel, nh, cut, room, lines, extra, nz),
        out_shape=(jax.ShapeDtypeStruct((nrow,), jnp.int32),) * 2
        + (f32(nrow), field, f32(nsub * lines, ncase, LANES), answer),
        in_specs=[VMEM] * (2 * nz + 7),
        out_specs=(SMEM,) * 3 + (VMEM,) * 3,
        scratch_shapes=[
            load,
            pltpu.SMEM((nsub, deep, SUBLANES, LANES), jnp.float32),
            pltpu.SemaphoreType.DMA((nsub,)),
        ],
        compiler_params=PARAMS,
    )(block, *a_z, *a_far, *b_near, *b_far)
    def update(step, lists, known, part):
        return call(
            functools.partial(list_kernel, step == 0),
            (f32(npatch, nh, ncase, LANES),) * 4,
            [SMEM] + [VMEM] * (4 + len(lists)),
            keep,
            known,
            compliance,
            part,
            sibling(part),
            *lists,
            cost=pl.CostEstimate(flops=16 * rhs.size, bytes_accessed=44 * rhs.size, transcendentals=0),
        )

    known = jnp.zeros((ncase, LANES), jnp.float32)
    state = [home_r]
    lists = [start]
    for step in range(ITERS - 1):
        last = step == ITERS - 2
        spread_out = sibling(own)
        if step > 0:
            spread_out, part = lax.optimization_barrier((spread_out, part))
            lists = update(step - 1, lists, known, part)
        spread_out = jnp.concatenate([spread_out[: per - 1], own[per - 1 :] + spread_out[per - 1 :]])
        parts = [spread_out] + [swap(spread_out, 4 * z) for z in range(1, nz)]
        parts = lax.optimization_barrier(parts)
        a = jnp.concatenate([part[:half] for part in parts])
        sums = tree([part[per - 1 :] for part in parts])
        b = jnp.concatenate([part[half : per - 1] for part in parts] + [sums])
        far_a, far_b = swap(a, 1), swap(b, 2)
        a, b = jnp.concatenate([a, far_a]), jnp.concatenate([b, far_b])
        far_a, far_b = swap(a, 2), swap(b, 1)
        if step > 0:
            far_a, far_b, lists = lax.optimization_barrier((far_a, far_b, lists))
        *state, own, part, known = call(
            functools.partial(home_kernel, step == 0, last, nh, room, lines),
            (field,) * (0 if last else 2) + (f32(nbody * nsub, ncase, LANES) if last else answer, f32(npatch, nh, ncase, LANES), f32(ncase, LANES)),
            [SMEM] * 4 + [VMEM] * (8 + len(state)),
            near,
            far,
            on,
            picked,
            comp,
            own,
            a,
            far_a,
            b,
            far_b,
            known,
            block,
            *state,
            scratch=[load, spread],
        )
    sums = lax.all_to_all(own, ("body", "sub"), split_axis=0, concat_axis=0, tiled=True)
    return call(
        end_kernel,
        f32(ncase, npatch, gap),
        [SMEM] + [VMEM] * 9,
        keep,
        sums,
        known,
        compliance,
        part,
        sibling(part),
        *lists,
        scratch=[pltpu.VMEM((nh, npatch, ncase, LANES), jnp.float32)],
    )


def solution(mesh):
    in_specs = (
        P(None, "sub", None),
        P("sub", None),
        P("sub", None),
        P("sub", None),
        P("sub", None),
        P("sub"),
        P("body", "sub", None, None),
    )
    out_specs = P(None, "sub", None)
    return jax.shard_map(
        on_device, mesh=mesh, in_specs=in_specs, out_specs=out_specs, check_vma=False
    )
```

```python
import functools

import jax
import jax.numpy as jnp
from jax import lax
from jax.experimental import pallas as pl
from jax.experimental.pallas import tpu as pltpu
from jax.sharding import PartitionSpec as P

ITERS = 4
LANES = 128
SUBLANES = 8
VMEM = pl.BlockSpec(memory_space=pltpu.VMEM)
SMEM = pl.BlockSpec(memory_space=pltpu.SMEM)
HBM = pl.BlockSpec(memory_space=pltpu.HBM)
PARAMS = pltpu.CompilerParams(vmem_limit_bytes=16 * 1024 * 1024)


def f32(*shape):
    return jax.ShapeDtypeStruct(shape, jnp.float32)


def call(kernel, out_shape, specs, *operands, scratch=(), cost=None):
    several = isinstance(out_shape, (tuple, list))
    return pl.pallas_call(
        kernel,
        out_shape=tuple(out_shape) if several else out_shape,
        in_specs=specs,
        out_specs=(VMEM,) * len(out_shape) if several else VMEM,
        scratch_shapes=list(scratch),
        compiler_params=PARAMS,
        cost_estimate=cost,
    )(*operands)


def per_case(value):
    return jnp.sum(value, axis=1, keepdims=True)


def respond(block, loads, gamma, energy, answer, last=False):
    load = loads[0]
    load[...] = functools.reduce(jnp.add, [part[...] for part in loads])
    ntile, ncase, width = load.shape
    value = jnp.concatenate([load[i] for i in range(ntile)], axis=1)
    high = value.astype(jnp.bfloat16)
    low = (value - high.astype(jnp.float32)).astype(jnp.bfloat16)
    total = jnp.dot(jnp.concatenate([high, low], axis=0), block[...], preferred_element_type=jnp.float32)
    total = total[:ncase] + total[ncase:]
    work = 0.5 * energy
    for i in range(ntile):
        tile = total[:, i * width : (i + 1) * width]
        if not last:
            answer[i] = tile
        work = work + load[i] * tile
    lane = lax.broadcasted_iota(jnp.int32, work.shape, 1)
    sums = jnp.where(lane == 0, per_case(0.5 * gamma), 0.0)
    sums = jnp.where(lane == 1, per_case(work), sums)
    if last:
        answer[...] = jnp.broadcast_to(sums[None], answer.shape)
    else:
        answer[ntile] = sums


def pack_kernel(nh, nz, by_z, place, field, *refs):
    if not by_z:
        table, *refs = refs
    *outs, whole = refs
    tiles = whole.shape[0] // (4 * nz + 1)
    whole[...] = jnp.zeros_like(whole)

    def body(p, carry):
        whole[pl.ds(place[p], nh)] = field[p]
        return carry

    lax.fori_loop(0, field.shape[0], body, 0, unroll=4)
    for i, out in enumerate(outs):
        size = out.shape[0] // (4 * nz // len(outs))
        for k in range(out.shape[0] // size):
            owner = i * 4 + k if by_z else k * 4 + i
            out[k * size : k * size + tiles] = whole[owner * tiles : (owner + 1) * tiles]
            if not by_z:
                out[k * size + tiles : (k + 1) * size] = table[owner]


def block_kernel(block, held, sems):
    pieces = sems.shape[0]
    size = block.shape[0] // pieces
    copies = []
    for j in range(pieces):
        rows = pl.ds(j * size, size)
        copies.append(pltpu.make_async_copy(block.at[rows], held.at[rows], sems.at[j]))
        copies[-1].start()
    for copy in copies:
        copy.wait()


def start_kernel(nh, cut, room, lines, extra, nz, block, *refs):
    a_z, refs = refs[:nz], refs[nz:]
    a_far, refs = refs[:3], refs[3:]
    b_near, refs = refs[:4], refs[4:]
    b_far, refs = refs[: nz - 1], refs[nz - 1 :]
    near, far, on, r_out, comp, answer, *loads, facts, sems = refs
    first, second = cut * nh, (room - cut) * nh
    blocks = []
    for z in range(nz):
        for m in range(4):
            one = (a_z[z], 0) if m == 0 else (a_far[m - 1], z * first)
            two = (b_near[m], 0) if z == 0 else (b_far[z - 1], m * (second + extra))
            blocks.append((*one, *two))
    copies = []
    for i, (_, _, two, at_two) in enumerate(blocks):
        rows = pl.ds(at_two + second + lines, extra - lines)
        copies.append(pltpu.make_async_copy(two.at[rows], facts.at[i], sems.at[i]))
        copies[-1].start()
    for load in loads:
        load[...] = jnp.zeros_like(load)
    gamma = energy = jnp.zeros(r_out.shape[2:], jnp.float32)
    for i, (one, at_one, two, at_two) in enumerate(blocks):
        at_comp = at_two + second
        comp[i * lines : (i + 1) * lines] = two[at_comp : at_comp + lines]
        copies[i].wait()
        for j in range(room):
            row = i * room + j
            slot = facts[i, j // SUBLANES, j % SUBLANES, 0].astype(jnp.int32)
            near[row] = slot
            far[row] = facts[i, j // SUBLANES, j % SUBLANES, 1].astype(jnp.int32)
            on[row] = facts[i, j // SUBLANES, j % SUBLANES, 2]
            if j < cut:
                r = one[at_one + j * nh : at_one + (j + 1) * nh]
            else:
                r = two[at_two + (j - cut) * nh : at_two + (j - cut + 1) * nh]
            r_out[row] = r
            loads[j % len(loads)][pl.ds(slot, nh)] += r
            for h in range(nh):
                line, sub = divmod(j * nh + h, SUBLANES)
                square = r[h] * r[h]
                gamma = gamma + square
                energy = energy + two[at_comp + line, sub : sub + 1, :] * square
    respond(block, loads, gamma, energy, answer)


def tree(values):
    while len(values) > 1:
        values = [a + b for a, b in zip(values[::2], values[1::2])]
    return values[0]


def steps(first, sums, known):
    gamma, delta = sums[:, 0:1], sums[:, 1:2]
    if first:
        return gamma, gamma / delta, jnp.zeros_like(gamma)
    beta = gamma / known[:, 0:1]
    return gamma, gamma / (delta - beta * gamma / known[:, 1:2]), beta


def home_kernel(first, last, nh, room, lines, place, away, keep, picked, comp, own, near_a, far_a, near_b, far_b, known, block, *refs):
    r_in, *refs = refs
    if not first:
        s_in, *refs = refs
    if not last:
        r, s, *refs = refs
    answer, part, known_out, *loads, resp = refs
    for load in loads:
        load[...] = jnp.zeros_like(load)
    nrow, _, ncase, width = r_in.shape
    at = 0
    for piece in (near_a, far_a, near_b, far_b):
        resp[at : at + piece.shape[0]] = piece[...]
        at += piece.shape[0]
    each = own.shape[0] // 2 + 1
    sums = tree([piece[i + each - 1] for piece in (near_b, far_b) for i in range(0, piece.shape[0], each)])
    gamma, alpha, beta = steps(first, sums, known[...])
    lane = lax.broadcasted_iota(jnp.int32, (ncase, width), 1)
    known_out[...] = jnp.where(lane == 0, gamma, jnp.where(lane == 1, alpha, beta))
    alpha = jnp.broadcast_to(alpha, (ncase, width))
    beta = jnp.broadcast_to(beta, (ncase, width))
    zero = jnp.zeros((ncase, width), jnp.float32)

    def pick(p, carry):
        part[p] = resp[pl.ds(picked[p], nh)]
        return carry

    lax.fori_loop(0, part.shape[0], pick, 0, unroll=8)

    def pair(i, sums):
        gamma, energy = sums
        for j in range(room):
            row = i * room + j
            near, far, on = place[row], away[row], keep[row]
            for h in range(nh):
                line, sub = divmod(j * nh + h, SUBLANES)
                c = comp[i * lines + line, sub : sub + 1, :]
                residual = r_in[row, h]
                image = on * (own[near + h] + resp[far + h] + c * residual)
                if not first:
                    image = image + beta * s_in[row, h]
                residual = residual - alpha * image
                if not last:
                    r[row, h], s[row, h] = residual, image
                loads[j % len(loads)][near + h] += residual
                square = residual * residual
                gamma = gamma + square
                energy = energy + c * square
        return gamma, energy

    gamma, energy = lax.fori_loop(0, nrow // room, pair, (zero, zero))
    respond(block, loads, gamma, energy, answer, last=last)


def list_kernel(first, keep, known, comp, mine, theirs, *refs):
    if first:
        r_in, r, d, x, s = refs
    else:
        r_in, d_in, x_in, s_in, r, d, x, s = refs
    npatch, nh, ncase, width = r.shape
    alpha = jnp.broadcast_to(known[:, 1:2], (ncase, width))
    beta = jnp.broadcast_to(known[:, 2:3], (ncase, width))

    def body(p, carry):
        on, row = keep[p], comp[pl.ds(p, 1), :]
        for h in range(nh):
            residual = r_in[p, h]
            c = row[:, h * width : (h + 1) * width]
            image = on * (mine[p, h] + theirs[p, h] + c * residual)
            if first:
                direction, moved = residual, alpha * residual
            else:
                direction = residual + beta * d_in[p, h]
                image = image + beta * s_in[p, h]
                moved = x_in[p, h] + alpha * direction
            r[p, h], d[p, h], x[p, h], s[p, h] = residual - alpha * image, direction, moved, image
        return carry

    lax.fori_loop(0, npatch, body, 0, unroll=4)


def end_kernel(keep, sums, known, comp, mine, theirs, r_in, d_in, x_in, s_in, out, moved):
    npatch, nh, ncase, width = r_in.shape
    total = sums[0]
    for i in range(1, sums.shape[0]):
        total = total + sums[i]
    _, alpha, beta = steps(False, total, known[...])
    one, two = jnp.broadcast_to(alpha, (ncase, width)), jnp.broadcast_to(beta, (ncase, width))
    alpha = jnp.broadcast_to(known[:, 1:2], (ncase, width))
    beta = jnp.broadcast_to(known[:, 2:3], (ncase, width))

    def body(p, carry):
        on, row = keep[p], comp[pl.ds(p, 1), :]
        for h in range(nh):
            residual = r_in[p, h]
            c = row[:, h * width : (h + 1) * width]
            image = on * (mine[p, h] + theirs[p, h] + c * residual) + beta * s_in[p, h]
            direction = residual + beta * d_in[p, h]
            residual = residual - alpha * image
            moved[h, p] = x_in[p, h] + alpha * direction + one * (residual + two * direction)
        return carry

    lax.fori_loop(0, npatch, body, 0, unroll=4)
    for h in range(nh):
        out[:, :, h * width : (h + 1) * width] = jnp.swapaxes(moved[h], 0, 1)


def on_device(rhs, compliance, plate_owner, found_owner, slot_pairs, active, inverse):
    nsub = lax.axis_size("sub")
    nbody = lax.axis_size("body")
    side = lax.axis_index("body")
    me = lax.axis_index("sub")
    ncase, npatch, gap = rhs.shape
    block = inverse[0, 0]
    nslot = block.shape[0] // gap
    nh = gap // LANES
    per = nslot * nh + 1
    room = max(2, 2 * npatch // nsub)
    nrow = nsub * room
    lines = -(-room * nh // SUBLANES)
    deep = -(-room // SUBLANES)
    extra = lines + deep
    cut = room // 2
    first = cut * nh
    second = (room - cut) * nh + extra
    nz = nsub // 4
    half = nslot // 2 * nh

    def swap(value, far):
        return lax.ppermute(value, "sub", [(i, i ^ far) for i in range(nsub)])

    def sibling(value):
        return lax.ppermute(value, "body", [(i, nbody - 1 - i) for i in range(nbody)])

    small = jnp.stack([plate_owner[:, 0], found_owner[:, 0], slot_pairs[:, 0], slot_pairs[:, 1], active])
    plate, foundation, plate_slot, found_slot, active = lax.optimization_barrier(small)
    keep = active.astype(jnp.float32)
    owner, other = jnp.where(side == 0, plate, foundation), jnp.where(side == 0, foundation, plate)
    slot, other_slot = jnp.where(side == 0, plate_slot, found_slot), jnp.where(side == 0, found_slot, plate_slot)
    index = jnp.arange(npatch, dtype=jnp.int32)
    earlier = (owner[None, :] == owner[:, None]) & (index[None, :] < index[:, None])
    rank = jnp.sum(earlier.astype(jnp.int32), axis=1)
    base, none = owner ^ me, 4 * nz
    place_a = jnp.where(rank < cut, base * cut + rank, none * cut) * nh
    place_b = jnp.where(rank < cut, none * (room - cut), base * (room - cut) + rank - cut) * nh

    def found(away):
        x_bit, y_bit, z_part = away & 1, (away >> 1) & 1, away >> 2
        found_a = ((y_bit * 2 + x_bit) * nz + z_part) * half + other_slot * nh
        found_b = ((x_bit * 2 + y_bit) * nz + z_part) * (half + 1) + (other_slot - nslot // 2) * nh
        return jnp.where(other_slot < nslot // 2, found_a, nsub * half + found_b)

    facts = jnp.stack([slot * nh, found(owner ^ other)], axis=1).astype(jnp.float32)
    facts = jnp.concatenate([facts, keep[:, None]], axis=1)
    facts = jnp.concatenate([compliance, jnp.pad(facts, ((0, 0), (0, LANES - 3)))], axis=1)
    row = (owner ^ me) * room + rank
    placed = (row[None, :] == jnp.arange(nrow, dtype=jnp.int32)[:, None]).astype(jnp.float32)
    facts = jnp.dot(placed, facts, precision=lax.Precision.HIGHEST).reshape(nsub, room, gap + LANES)
    lined = facts[:, :, :gap].reshape(nsub, room * nh, LANES)
    lined = jnp.pad(lined, ((0, 0), (0, lines * SUBLANES - room * nh), (0, 0)))
    named = jnp.pad(facts[:, :, gap:], ((0, 0), (0, deep * SUBLANES - room), (0, 0)))
    table = jnp.concatenate([lined, named], axis=1).reshape(nsub, lines + deep, SUBLANES, LANES)
    start = (keep[None, :, None] * rhs).reshape(ncase, npatch, nh, LANES)
    start = jnp.transpose(start, (1, 2, 0, 3))
    picked = found(me ^ other).astype(jnp.int32)
    place_a, place_b, picked = lax.optimization_barrier((place_a, place_b, picked))

    a_z = call(
        functools.partial(pack_kernel, nh, nz, True),
        (f32(4 * first, ncase, LANES),) * nz,
        [SMEM, VMEM],
        place_a,
        start,
        scratch=[pltpu.VMEM(((nsub + 1) * cut * nh, ncase, LANES), jnp.float32)],
    )
    b_near = call(
        functools.partial(pack_kernel, nh, nz, False),
        (f32(nz * second, ncase, LANES),) * 4,
        [SMEM, VMEM, VMEM],
        place_b,
        start,
        table,
        scratch=[pltpu.VMEM(((nsub + 1) * (room - cut) * nh, ncase, LANES), jnp.float32)],
    )
    a_z = [a_z[0]] + [swap(a_z[z], 4 * z) for z in range(1, nz)]
    b_near = [b_near[0]] + [swap(b_near[m], m) for m in range(1, 4)]
    block = call(
        block_kernel,
        jax.ShapeDtypeStruct(block.shape, block.dtype),
        [HBM],
        pltpu.with_memory_space_constraint(block, pltpu.HBM),
        scratch=[pltpu.SemaphoreType.DMA((nslot,))],
        cost=pl.CostEstimate(flops=0, bytes_accessed=4 * block.size, transcendentals=0),
    )
    a_z, b_near, block = lax.optimization_barrier((a_z[::-1], b_near, block))
    a_z = a_z[::-1]
    b_far = [
        swap(jnp.concatenate([part[z * second : (z + 1) * second] for part in b_near]), 4 * z)
        for z in range(1, nz)
    ]
    a_far = [
        swap(jnp.concatenate([part[m * first : (m + 1) * first] for part in a_z]), m) for m in range(1, 4)
    ]
    field = f32(nrow, nh, ncase, LANES)
    answer = f32(per, ncase, LANES)
    loads = [pltpu.VMEM((nslot * nh, ncase, LANES), jnp.float32)] * 4
    spread = pltpu.VMEM((nsub * per, ncase, LANES), jnp.float32)
    near, far, on, home_r, comp, own = pl.pallas_call(
        functools.partial(start_kernel, nh, cut, room, lines, extra, nz),
        out_shape=(jax.ShapeDtypeStruct((nrow,), jnp.int32),) * 2
        + (f32(nrow), field, f32(nsub * lines, ncase, LANES), answer),
        in_specs=[VMEM] * (2 * nz + 7),
        out_specs=(SMEM,) * 3 + (VMEM,) * 3,
        scratch_shapes=[
            *loads,
            pltpu.SMEM((nsub, deep, SUBLANES, LANES), jnp.float32),
            pltpu.SemaphoreType.DMA((nsub,)),
        ],
        compiler_params=PARAMS,
    )(block, *a_z, *a_far, *b_near, *b_far)
    def update(step, lists, known, part):
        return call(
            functools.partial(list_kernel, step == 0),
            (f32(npatch, nh, ncase, LANES),) * 4,
            [SMEM] + [VMEM] * (4 + len(lists)),
            keep,
            known,
            compliance,
            part,
            sibling(part),
            *lists,
            cost=pl.CostEstimate(flops=16 * rhs.size, bytes_accessed=44 * rhs.size, transcendentals=0),
        )

    known = jnp.zeros((ncase, LANES), jnp.float32)
    state = [home_r]
    lists = [start]
    for step in range(ITERS - 1):
        last = step == ITERS - 2
        spread_out = sibling(own)
        if step > 0:
            spread_out, part = lax.optimization_barrier((spread_out, part))
            lists = update(step - 1, lists, known, part)
        spread_out = jnp.concatenate([spread_out[: per - 1], own[per - 1 :] + spread_out[per - 1 :]])
        parts = [spread_out] + [swap(spread_out, 4 * z) for z in range(1, nz)]
        parts = lax.optimization_barrier(parts[::-1])[::-1]
        a = jnp.concatenate([part[:half] for part in parts])
        b = jnp.concatenate([part[half:] for part in parts])
        far_a, far_b = swap(a, 1), swap(b, 2)
        a, b = jnp.concatenate([a, far_a]), jnp.concatenate([b, far_b])
        far_a, far_b = swap(a, 2), swap(b, 1)
        if step > 0:
            far_a, far_b, lists = lax.optimization_barrier((far_a, far_b, lists))
        *state, own, part, known = call(
            functools.partial(home_kernel, step == 0, last, nh, room, lines),
            (field,) * (0 if last else 2) + (f32(nbody * nsub, ncase, LANES) if last else answer, f32(npatch, nh, ncase, LANES), f32(ncase, LANES)),
            [SMEM] * 4 + [VMEM] * (8 + len(state)),
            near,
            far,
            on,
            picked,
            comp,
            own,
            a,
            far_a,
            b,
            far_b,
            known,
            block,
            *state,
            scratch=[*loads, spread],
        )
    sums = lax.all_to_all(own, ("body", "sub"), split_axis=0, concat_axis=0, tiled=True)
    return call(
        end_kernel,
        f32(ncase, npatch, gap),
        [SMEM] + [VMEM] * 9,
        keep,
        sums,
        known,
        compliance,
        part,
        sibling(part),
        *lists,
        scratch=[pltpu.VMEM((nh, npatch, ncase, LANES), jnp.float32)],
    )


def solution(mesh):
    in_specs = (
        P(None, "sub", None),
        P("sub", None),
        P("sub", None),
        P("sub", None),
        P("sub", None),
        P("sub"),
        P("body", "sub", None, None),
    )
    out_specs = P(None, "sub", None)
    return jax.shard_map(
        on_device, mesh=mesh, in_specs=in_specs, out_specs=out_specs, check_vma=False
    )
```

```python
import functools

import jax
import jax.numpy as jnp
from jax import lax
from jax.experimental import pallas as pl
from jax.experimental.pallas import tpu as pltpu
from jax.sharding import PartitionSpec as P

ITERS = 4
LANES = 128
SUBLANES = 8
VMEM = pl.BlockSpec(memory_space=pltpu.VMEM)
SMEM = pl.BlockSpec(memory_space=pltpu.SMEM)
HBM = pl.BlockSpec(memory_space=pltpu.HBM)
PARAMS = pltpu.CompilerParams(vmem_limit_bytes=16 * 1024 * 1024)


def f32(*shape):
    return jax.ShapeDtypeStruct(shape, jnp.float32)


def call(kernel, out_shape, specs, *operands, scratch=(), cost=None):
    several = isinstance(out_shape, (tuple, list))
    return pl.pallas_call(
        kernel,
        out_shape=tuple(out_shape) if several else out_shape,
        in_specs=specs,
        out_specs=(VMEM,) * len(out_shape) if several else VMEM,
        scratch_shapes=list(scratch),
        compiler_params=PARAMS,
        cost_estimate=cost,
    )(*operands)


def per_case(value):
    return jnp.sum(value, axis=1, keepdims=True)


def respond(block, loads, gamma, energy, answer, last=False):
    load = loads[0]
    load[...] = functools.reduce(jnp.add, [part[...] for part in loads])
    ntile, ncase, width = load.shape
    value = jnp.concatenate([load[i] for i in range(ntile)], axis=1)
    high = value.astype(jnp.bfloat16)
    low = (value - high.astype(jnp.float32)).astype(jnp.bfloat16)
    total = jnp.dot(jnp.concatenate([high, low], axis=0), block[...], preferred_element_type=jnp.float32)
    total = total[:ncase] + total[ncase:]
    work = 0.5 * energy
    for i in range(ntile):
        tile = total[:, i * width : (i + 1) * width]
        if not last:
            answer[i] = tile
        work = work + load[i] * tile
    lane = lax.broadcasted_iota(jnp.int32, work.shape, 1)
    sums = jnp.where(lane == 0, per_case(0.5 * gamma), 0.0)
    sums = jnp.where(lane == 1, per_case(work), sums)
    if last:
        answer[...] = jnp.broadcast_to(sums[None], answer.shape)
    else:
        answer[ntile] = sums


def pack_kernel(nh, nz, by_z, place, field, *refs):
    if not by_z:
        table, *refs = refs
    *outs, whole = refs
    tiles = whole.shape[0] // (4 * nz + 1)
    whole[...] = jnp.zeros_like(whole)

    def body(p, carry):
        whole[pl.ds(place[p], nh)] = field[p]
        return carry

    lax.fori_loop(0, field.shape[0], body, 0, unroll=4)
    for i, out in enumerate(outs):
        size = out.shape[0] // (4 * nz // len(outs))
        for k in range(out.shape[0] // size):
            owner = i * 4 + k if by_z else k * 4 + i
            out[k * size : k * size + tiles] = whole[owner * tiles : (owner + 1) * tiles]
            if not by_z:
                out[k * size + tiles : (k + 1) * size] = table[owner]


def block_kernel(block, held, sems):
    pieces = sems.shape[0]
    size = block.shape[0] // pieces
    copies = []
    for j in range(pieces):
        rows = pl.ds(j * size, size)
        copies.append(pltpu.make_async_copy(block.at[rows], held.at[rows], sems.at[j]))
        copies[-1].start()
    for copy in copies:
        copy.wait()


def start_kernel(nh, cut, room, lines, extra, nz, block, *refs):
    a_z, refs = refs[:nz], refs[nz:]
    a_far, refs = refs[:3], refs[3:]
    b_near, refs = refs[:4], refs[4:]
    b_far, refs = refs[: nz - 1], refs[nz - 1 :]
    near, far, on, r_out, comp, answer, *loads, facts, sems = refs
    first, second = cut * nh, (room - cut) * nh
    blocks = []
    for z in range(nz):
        for m in range(4):
            one = (a_z[z], 0) if m == 0 else (a_far[m - 1], z * first)
            two = (b_near[m], 0) if z == 0 else (b_far[z - 1], m * (second + extra))
            blocks.append((*one, *two))
    copies = []
    for i, (_, _, two, at_two) in enumerate(blocks):
        rows = pl.ds(at_two + second + lines, extra - lines)
        copies.append(pltpu.make_async_copy(two.at[rows], facts.at[i], sems.at[i]))
        copies[-1].start()
    for load in loads:
        load[...] = jnp.zeros_like(load)
    gamma = energy = jnp.zeros(r_out.shape[2:], jnp.float32)
    for i, (one, at_one, two, at_two) in enumerate(blocks):
        at_comp = at_two + second
        comp[i * lines : (i + 1) * lines] = two[at_comp : at_comp + lines]
        copies[i].wait()
        for j in range(room):
            row = i * room + j
            slot = facts[i, j // SUBLANES, j % SUBLANES, 0].astype(jnp.int32)
            near[row] = slot
            far[row] = facts[i, j // SUBLANES, j % SUBLANES, 1].astype(jnp.int32)
            on[row] = facts[i, j // SUBLANES, j % SUBLANES, 2]
            if j < cut:
                r = one[at_one + j * nh : at_one + (j + 1) * nh]
            else:
                r = two[at_two + (j - cut) * nh : at_two + (j - cut + 1) * nh]
            r_out[row] = r
            loads[j % len(loads)][pl.ds(slot, nh)] += r
            for h in range(nh):
                line, sub = divmod(j * nh + h, SUBLANES)
                square = r[h] * r[h]
                gamma = gamma + square
                energy = energy + two[at_comp + line, sub : sub + 1, :] * square
    respond(block, loads, gamma, energy, answer)


def tree(values):
    while len(values) > 1:
        values = [a + b for a, b in zip(values[::2], values[1::2])]
    return values[0]


def steps(first, sums, known):
    gamma, delta = sums[:, 0:1], sums[:, 1:2]
    if first:
        return gamma, gamma / delta, jnp.zeros_like(gamma)
    beta = gamma / known[:, 0:1]
    return gamma, gamma / (delta - beta * gamma / known[:, 1:2]), beta


def home_kernel(first, last, nh, room, lines, place, away, keep, picked, comp, own, near_a, far_a, near_b, far_b, known, block, *refs):
    r_in, *refs = refs
    if not first:
        s_in, *refs = refs
    if not last:
        r, s, *refs = refs
    answer, part, known_out, *loads, resp = refs
    for load in loads:
        load[...] = jnp.zeros_like(load)
    nrow, _, ncase, width = r_in.shape
    at = 0
    for piece in (near_a, far_a, near_b, far_b):
        resp[at : at + piece.shape[0]] = piece[...]
        at += piece.shape[0]
    each = own.shape[0] // 2 + 1
    sums = tree([piece[i + each - 1] for piece in (near_b, far_b) for i in range(0, piece.shape[0], each)])
    gamma, alpha, beta = steps(first, sums, known[...])
    lane = lax.broadcasted_iota(jnp.int32, (ncase, width), 1)
    known_out[...] = jnp.where(lane == 0, gamma, jnp.where(lane == 1, alpha, beta))
    alpha = jnp.broadcast_to(alpha, (ncase, width))
    beta = jnp.broadcast_to(beta, (ncase, width))
    zero = jnp.zeros((ncase, width), jnp.float32)

    def pick(p, carry):
        part[p] = resp[pl.ds(picked[p], nh)]
        return carry

    lax.fori_loop(0, part.shape[0], pick, 0, unroll=8)

    def pair(i, sums):
        gamma, energy = sums
        for j in range(room):
            row = i * room + j
            near, far, on = place[row], away[row], keep[row]
            for h in range(nh):
                line, sub = divmod(j * nh + h, SUBLANES)
                c = comp[i * lines + line, sub : sub + 1, :]
                residual = r_in[row, h]
                image = on * (own[near + h] + resp[far + h] + c * residual)
                if not first:
                    image = image + beta * s_in[row, h]
                residual = residual - alpha * image
                if not last:
                    r[row, h], s[row, h] = residual, image
                loads[j % len(loads)][near + h] += residual
                square = residual * residual
                gamma = gamma + square
                energy = energy + c * square
        return gamma, energy

    gamma, energy = lax.fori_loop(0, nrow // room, pair, (zero, zero), unroll=2)
    respond(block, loads, gamma, energy, answer, last=last)


def list_kernel(first, keep, known, comp, mine, theirs, *refs):
    if first:
        r_in, r, d, x, s = refs
    else:
        r_in, d_in, x_in, s_in, r, d, x, s = refs
    npatch, nh, ncase, width = r.shape
    alpha = jnp.broadcast_to(known[:, 1:2], (ncase, width))
    beta = jnp.broadcast_to(known[:, 2:3], (ncase, width))

    def body(p, carry):
        on, row = keep[p], comp[pl.ds(p, 1), :]
        for h in range(nh):
            residual = r_in[p, h]
            c = row[:, h * width : (h + 1) * width]
            image = on * (mine[p, h] + theirs[p, h] + c * residual)
            if first:
                direction, moved = residual, alpha * residual
            else:
                direction = residual + beta * d_in[p, h]
                image = image + beta * s_in[p, h]
                moved = x_in[p, h] + alpha * direction
            r[p, h], d[p, h], x[p, h], s[p, h] = residual - alpha * image, direction, moved, image
        return carry

    lax.fori_loop(0, npatch, body, 0, unroll=4)


def end_kernel(keep, sums, known, comp, mine, theirs, r_in, d_in, x_in, s_in, out, moved):
    npatch, nh, ncase, width = r_in.shape
    total = sums[0]
    for i in range(1, sums.shape[0]):
        total = total + sums[i]
    _, alpha, beta = steps(False, total, known[...])
    one, two = jnp.broadcast_to(alpha, (ncase, width)), jnp.broadcast_to(beta, (ncase, width))
    alpha = jnp.broadcast_to(known[:, 1:2], (ncase, width))
    beta = jnp.broadcast_to(known[:, 2:3], (ncase, width))

    def body(p, carry):
        on, row = keep[p], comp[pl.ds(p, 1), :]
        for h in range(nh):
            residual = r_in[p, h]
            c = row[:, h * width : (h + 1) * width]
            image = on * (mine[p, h] + theirs[p, h] + c * residual) + beta * s_in[p, h]
            direction = residual + beta * d_in[p, h]
            residual = residual - alpha * image
            moved[h, p] = x_in[p, h] + alpha * direction + one * (residual + two * direction)
        return carry

    lax.fori_loop(0, npatch, body, 0, unroll=4)
    for h in range(nh):
        out[:, :, h * width : (h + 1) * width] = jnp.swapaxes(moved[h], 0, 1)


def on_device(rhs, compliance, plate_owner, found_owner, slot_pairs, active, inverse):
    nsub = lax.axis_size("sub")
    nbody = lax.axis_size("body")
    side = lax.axis_index("body")
    me = lax.axis_index("sub")
    ncase, npatch, gap = rhs.shape
    block = inverse[0, 0]
    nslot = block.shape[0] // gap
    nh = gap // LANES
    per = nslot * nh + 1
    room = max(2, 2 * npatch // nsub)
    nrow = nsub * room
    lines = -(-room * nh // SUBLANES)
    deep = -(-room // SUBLANES)
    extra = lines + deep
    cut = room // 2
    first = cut * nh
    second = (room - cut) * nh + extra
    nz = nsub // 4
    half = nslot // 2 * nh

    def swap(value, far):
        return lax.ppermute(value, "sub", [(i, i ^ far) for i in range(nsub)])

    def sibling(value):
        return lax.ppermute(value, "body", [(i, nbody - 1 - i) for i in range(nbody)])

    small = jnp.stack([plate_owner[:, 0], found_owner[:, 0], slot_pairs[:, 0], slot_pairs[:, 1], active])
    plate, foundation, plate_slot, found_slot, active = lax.optimization_barrier(small)
    keep = active.astype(jnp.float32)
    owner, other = jnp.where(side == 0, plate, foundation), jnp.where(side == 0, foundation, plate)
    slot, other_slot = jnp.where(side == 0, plate_slot, found_slot), jnp.where(side == 0, found_slot, plate_slot)
    index = jnp.arange(npatch, dtype=jnp.int32)
    earlier = (owner[None, :] == owner[:, None]) & (index[None, :] < index[:, None])
    rank = jnp.sum(earlier.astype(jnp.int32), axis=1)
    base, none = owner ^ me, 4 * nz
    place_a = jnp.where(rank < cut, base * cut + rank, none * cut) * nh
    place_b = jnp.where(rank < cut, none * (room - cut), base * (room - cut) + rank - cut) * nh

    def found(away):
        x_bit, y_bit, z_part = away & 1, (away >> 1) & 1, away >> 2
        found_a = ((y_bit * 2 + x_bit) * nz + z_part) * half + other_slot * nh
        found_b = ((x_bit * 2 + y_bit) * nz + z_part) * (half + 1) + (other_slot - nslot // 2) * nh
        return jnp.where(other_slot < nslot // 2, found_a, nsub * half + found_b)

    facts = jnp.stack([slot * nh, found(owner ^ other)], axis=1).astype(jnp.float32)
    facts = jnp.concatenate([facts, keep[:, None]], axis=1)
    facts = jnp.concatenate([compliance, jnp.pad(facts, ((0, 0), (0, LANES - 3)))], axis=1)
    row = (owner ^ me) * room + rank
    placed = (row[None, :] == jnp.arange(nrow, dtype=jnp.int32)[:, None]).astype(jnp.float32)
    facts = jnp.dot(placed, facts, precision=lax.Precision.HIGHEST).reshape(nsub, room, gap + LANES)
    lined = facts[:, :, :gap].reshape(nsub, room * nh, LANES)
    lined = jnp.pad(lined, ((0, 0), (0, lines * SUBLANES - room * nh), (0, 0)))
    named = jnp.pad(facts[:, :, gap:], ((0, 0), (0, deep * SUBLANES - room), (0, 0)))
    table = jnp.concatenate([lined, named], axis=1).reshape(nsub, lines + deep, SUBLANES, LANES)
    start = (keep[None, :, None] * rhs).reshape(ncase, npatch, nh, LANES)
    start = jnp.transpose(start, (1, 2, 0, 3))
    picked = found(me ^ other).astype(jnp.int32)
    place_a, place_b, picked = lax.optimization_barrier((place_a, place_b, picked))

    a_z = call(
        functools.partial(pack_kernel, nh, nz, True),
        (f32(4 * first, ncase, LANES),) * nz,
        [SMEM, VMEM],
        place_a,
        start,
        scratch=[pltpu.VMEM(((nsub + 1) * cut * nh, ncase, LANES), jnp.float32)],
    )
    b_near = call(
        functools.partial(pack_kernel, nh, nz, False),
        (f32(nz * second, ncase, LANES),) * 4,
        [SMEM, VMEM, VMEM],
        place_b,
        start,
        table,
        scratch=[pltpu.VMEM(((nsub + 1) * (room - cut) * nh, ncase, LANES), jnp.float32)],
    )
    a_z = [a_z[0]] + [swap(a_z[z], 4 * z) for z in range(1, nz)]
    b_near = [b_near[0]] + [swap(b_near[m], m) for m in range(1, 4)]
    block = call(
        block_kernel,
        jax.ShapeDtypeStruct(block.shape, block.dtype),
        [HBM],
        pltpu.with_memory_space_constraint(block, pltpu.HBM),
        scratch=[pltpu.SemaphoreType.DMA((nslot,))],
        cost=pl.CostEstimate(flops=0, bytes_accessed=4 * block.size, transcendentals=0),
    )
    a_z, b_near, block = lax.optimization_barrier((a_z[::-1], b_near, block))
    a_z = a_z[::-1]
    b_far = [
        swap(jnp.concatenate([part[z * second : (z + 1) * second] for part in b_near]), 4 * z)
        for z in range(1, nz)
    ]
    a_far = [
        swap(jnp.concatenate([part[m * first : (m + 1) * first] for part in a_z]), m) for m in range(1, 4)
    ]
    field = f32(nrow, nh, ncase, LANES)
    answer = f32(per, ncase, LANES)
    loads = [pltpu.VMEM((nslot * nh, ncase, LANES), jnp.float32)] * 8
    spread = pltpu.VMEM((nsub * per, ncase, LANES), jnp.float32)
    near, far, on, home_r, comp, own = pl.pallas_call(
        functools.partial(start_kernel, nh, cut, room, lines, extra, nz),
        out_shape=(jax.ShapeDtypeStruct((nrow,), jnp.int32),) * 2
        + (f32(nrow), field, f32(nsub * lines, ncase, LANES), answer),
        in_specs=[VMEM] * (2 * nz + 7),
        out_specs=(SMEM,) * 3 + (VMEM,) * 3,
        scratch_shapes=[
            *loads,
            pltpu.SMEM((nsub, deep, SUBLANES, LANES), jnp.float32),
            pltpu.SemaphoreType.DMA((nsub,)),
        ],
        compiler_params=PARAMS,
    )(block, *a_z, *a_far, *b_near, *b_far)
    def update(step, lists, known, part):
        return call(
            functools.partial(list_kernel, step == 0),
            (f32(npatch, nh, ncase, LANES),) * 4,
            [SMEM] + [VMEM] * (4 + len(lists)),
            keep,
            known,
            compliance,
            part,
            sibling(part),
            *lists,
            cost=pl.CostEstimate(flops=16 * rhs.size, bytes_accessed=44 * rhs.size, transcendentals=0),
        )

    known = jnp.zeros((ncase, LANES), jnp.float32)
    state = [home_r]
    lists = [start]
    for step in range(ITERS - 1):
        last = step == ITERS - 2
        spread_out = sibling(own)
        if step > 0:
            spread_out, part = lax.optimization_barrier((spread_out, part))
            lists = update(step - 1, lists, known, part)
        spread_out = jnp.concatenate([spread_out[: per - 1], own[per - 1 :] + spread_out[per - 1 :]])
        parts = [spread_out] + [swap(spread_out, 4 * z) for z in range(1, nz)]
        parts = lax.optimization_barrier(parts[::-1])[::-1]
        a = jnp.concatenate([part[:half] for part in parts])
        b = jnp.concatenate([part[half:] for part in parts])
        far_a, far_b = swap(a, 1), swap(b, 2)
        a, b = jnp.concatenate([a, far_a]), jnp.concatenate([b, far_b])
        far_a, far_b = swap(a, 2), swap(b, 1)
        if step > 0:
            far_a, far_b, lists = lax.optimization_barrier((far_a, far_b, lists))
        *state, own, part, known = call(
            functools.partial(home_kernel, step == 0, last, nh, room, lines),
            (field,) * (0 if last else 2) + (f32(nbody * nsub, ncase, LANES) if last else answer, f32(npatch, nh, ncase, LANES), f32(ncase, LANES)),
            [SMEM] * 4 + [VMEM] * (8 + len(state)),
            near,
            far,
            on,
            picked,
            comp,
            own,
            a,
            far_a,
            b,
            far_b,
            known,
            block,
            *state,
            scratch=[*loads, spread],
        )
    sums = lax.all_to_all(own, ("body", "sub"), split_axis=0, concat_axis=0, tiled=True)
    return call(
        end_kernel,
        f32(ncase, npatch, gap),
        [SMEM] + [VMEM] * 9,
        keep,
        sums,
        known,
        compliance,
        part,
        sibling(part),
        *lists,
        scratch=[pltpu.VMEM((nh, npatch, ncase, LANES), jnp.float32)],
    )


def solution(mesh):
    in_specs = (
        P(None, "sub", None),
        P("sub", None),
        P("sub", None),
        P("sub", None),
        P("sub", None),
        P("sub"),
        P("body", "sub", None, None),
    )
    out_specs = P(None, "sub", None)
    return jax.shard_map(
        on_device, mesh=mesh, in_specs=in_specs, out_specs=out_specs, check_vma=False
    )
```
